32 devices in a mesh: rows: 16 (over z, y, core), feat: 2 (over x).
Axes of the slice: x: 2, y: 2, z: 4, core: 2. Of those that a mesh axis runs over, the one named last changes fastest.
Arguments:
- logits: float32 [49152, 32], P('rows'), may hold values from -6 to 6
- labels: int32 [49152], P('rows'), may hold values from 0 to 31
- node_ids: int32 [49152], P('rows'), may hold values from 0 to 7
- bin_codes: int32 [49152, 256], P('rows', 'feat'), may hold values from 0 to 63
- split_feature: int32 [8], replicated, may hold values from 0 to 255
- split_bin: int32 [8], replicated, may hold values from 1 to 63
- split_missing: int32 [8], replicated, may hold values from 0 to 1
Outputs:
- new_logits: float32 [49152, 32], P('rows')
- gain_table: float32 [16, 128, 128], P('rows', 'feat')
- leaves: float32 [8, 2, 32], replicated
The draws below stay inside these ranges and needn't reach their ends.
Inputs may be any that keep to these rules, and one draw needn't show every extreme that they name: `split_missing`: 1 sends the missing code 64 - 1 to the left child, 0 to the right child.
All inputs are finite; a program needn't handle non-finite values.
Results may differ from the reference program's by a relative error of at most 0.0014.
Values sent between devices are 32-bit elements; how exact they have to be, the bound alone decides.
No kernel may reach another device: no remote copies, remote signals or barrier semaphores. Data moves between devices by JAX's collectives and lax.ppermute only.
A program may use at most 64 MiB of HBM per device.

```python
import math
import jax
import jax.numpy as jnp
import numpy as np
from jax import lax

K = 32
FEAT = 256
BINS = 64
NODES = 8
TOTAL_ROWS = 49152
N_ROWS = 16
N_FEAT = 2


def place_ends(array, key, smallest, largest):
    dims = array.shape
    place = [jax.random.randint(jax.random.fold_in(key, axis), (), 0, dims[axis]) for axis in range(len(dims))]
    array = array.at[tuple(place)].set(smallest)
    longest = dims.index(max(dims))
    place[longest] = (place[longest] + 1) % dims[longest]
    return array.at[tuple(place)].set(largest)


def levels(key, extent, cuts, low, high):
    def one(dim, parts):
        draws = jax.random.uniform(jax.random.fold_in(jax.random.fold_in(key, 6), dim), (parts,), jnp.float32, low / len(cuts), high / len(cuts))
        return jnp.repeat(jnp.exp(draws), extent[dim] // parts).reshape((-1,) + (1,) * (len(extent) - dim - 1))

    level = one(*cuts[0])
    for cut in cuts[1:]:
        level = level * one(*cut)
    return level


def rank_bounds(amount, slope):
    loads = [(1 << 20) // math.isqrt(rank ** slope) + 1 for rank in range(1, amount + 1)]
    scale = 1 + sum(loads) // (1 << 30)
    return np.cumsum(np.array([max(1, weight // scale) for weight in loads]))


def ranked_ids(stream_key, shape, number_of, slope):
    table = rank_bounds(number_of, slope)
    lot = jax.random.randint(jax.random.fold_in(stream_key, 1), shape, 0, int(table[number_of - 1]))
    standing = jnp.searchsorted(jnp.asarray(table, jnp.int32), lot, side="right")
    return jax.random.permutation(jax.random.fold_in(stream_key, 2), number_of)[standing].astype(jnp.int32)


def gaussian(stream_key, shape, width, most, split=(), kind=jnp.bfloat16):
    entries = jax.random.normal(stream_key, shape, jnp.float32) * width
    if len(split) > 0:
        entries = levels(stream_key, shape, split, -0.22, 0.18) * entries
    return jnp.clip(entries, min=-most, max=most).astype(kind)


def setup_inputs(seed: int = 0) -> dict:
    key_of = jax.random.split(jax.random.key(seed), 8)
    return {
        "logits": gaussian(key_of[0], (TOTAL_ROWS, K), 1.5, 6.0, ((0, 16),), jnp.float32),
        "labels": place_ends(ranked_ids(key_of[1], (TOTAL_ROWS,), K, 2), jax.random.fold_in(key_of[1], 3), 0, K - 1).astype(jnp.int32),
        "node_ids": place_ends(ranked_ids(key_of[2], (TOTAL_ROWS,), NODES, 1), jax.random.fold_in(key_of[2], 3), 0, NODES - 1).astype(jnp.int32),
        "bin_codes": place_ends(ranked_ids(key_of[3], (TOTAL_ROWS, FEAT), BINS, 2), jax.random.fold_in(key_of[3], 3), 0, BINS - 1).astype(jnp.int32),
        "split_feature": place_ends(jax.random.randint(key_of[4], (NODES,), 0, FEAT), jax.random.fold_in(key_of[4], 1), 0, FEAT - 1).astype(jnp.int32),
        "split_bin": place_ends(jax.random.randint(key_of[5], (NODES,), 1, BINS), jax.random.fold_in(key_of[5], 1), 1, BINS - 1).astype(jnp.int32),
        "split_missing": place_ends(jax.random.randint(key_of[6], (NODES,), 0, 2), jax.random.fold_in(key_of[6], 1), 0, 1).astype(jnp.int32),
    }


reg_lambda = 1.0
step_size = 0.3


def gradients(logits, labels):
    expo_vals = jnp.exp(logits)
    soft_prob = expo_vals / jnp.sum(expo_vals, axis=1, keepdims=True)
    target = (labels[:, None] == jnp.arange(K, dtype=jnp.int32)[None, :]).astype(jnp.float32)
    grad_rows = (soft_prob - target).astype(jnp.bfloat16)
    hess_rows = (soft_prob * (1.0 - soft_prob)).astype(jnp.bfloat16)
    return jnp.concatenate([grad_rows, hess_rows], axis=1)


def split_score(sums):
    grad_part = sums[..., :K]
    hess_part = sums[..., K:]
    return jnp.sum(grad_part * grad_part / (hess_part + reg_lambda), axis=-1)


def reference(logits, labels, node_ids, bin_codes, split_feature, split_bin, split_missing):
    grad_hess = gradients(logits, labels).astype(jnp.float32)

    def feature_hist(codes):
        return jax.ops.segment_sum(grad_hess, node_ids * BINS + codes, num_segments=NODES * BINS)

    hist = lax.map(feature_hist, bin_codes.T)
    hist = hist.reshape(FEAT, NODES, BINS, 2 * K).transpose(1, 0, 2, 3)
    cumul = jnp.cumsum(hist[:, :, :BINS - 1, :], axis=2)
    left_base = jnp.concatenate([jnp.zeros_like(hist[:, :, :1, :]), cumul], axis=2)
    node_total = jnp.sum(hist, axis=2, keepdims=True)
    missing_sum = hist[:, :, BINS - 1:, :]
    left_miss = left_base + missing_sum
    parent_score = split_score(node_total)
    gain_left = split_score(left_miss) + split_score(node_total - left_miss) - parent_score
    gain_right = split_score(left_base) + split_score(node_total - left_base) - parent_score
    gain = jnp.concatenate([gain_left, gain_right], axis=-1) / (2.0 * K)
    per_node = N_ROWS // NODES
    pairs_dev = FEAT // N_FEAT // per_node
    gain = gain.reshape(NODES, N_FEAT, per_node, pairs_dev, 2 * BINS).transpose(0, 2, 1, 3, 4)
    gain_table = gain.reshape(N_ROWS, N_FEAT * pairs_dev, 2 * BINS)

    chosen = hist[jnp.arange(NODES, dtype=jnp.int32), split_feature]
    bin_iota = jnp.arange(BINS, dtype=jnp.int32)
    bin_mask = ((bin_iota[None, :] < split_bin[:, None]) & (bin_iota[None, :] < BINS - 1)).astype(jnp.float32)
    left_sum = jnp.sum(chosen * bin_mask[:, :, None], axis=1) + chosen[:, BINS - 1, :] * split_missing[:, None].astype(jnp.float32)
    node_sum = jnp.sum(chosen, axis=1)
    side_sums = jnp.stack([left_sum, node_sum - left_sum], axis=1)
    leaves = -side_sums[..., :K] / (side_sums[..., K:] + reg_lambda)

    row_feature = split_feature[node_ids]
    row_code = jnp.take_along_axis(bin_codes, row_feature[:, None], axis=1)[:, 0]
    goes_left = (row_code < split_bin[node_ids]) | ((row_code == BINS - 1) & (split_missing[node_ids] == 1))
    row_side = jnp.where(goes_left, 0, 1).astype(jnp.int32)
    new_logits = logits + step_size * leaves[node_ids, row_side]
    return (new_logits, gain_table, leaves)
```

```python
import functools

import jax
import jax.numpy as jnp
from jax import lax
from jax.experimental import pallas as pl
from jax.experimental.pallas import tpu as pltpu
from jax.sharding import PartitionSpec as P

BINS = 64


reg_lambda = 1.0
step_size = 0.3


def split_score(sums, classes):
    grad_part = sums[..., :classes]
    hess_part = sums[..., classes:]
    return jnp.sum(grad_part * grad_part / (hess_part + reg_lambda), axis=-1)


def three_parts(x):
    first = x.astype(jnp.bfloat16)
    rest = x - first.astype(jnp.float32)
    second = rest.astype(jnp.bfloat16)
    third = (rest - second.astype(jnp.float32)).astype(jnp.bfloat16)
    return first, second, third


def threshold_masks():
    row = lax.broadcasted_iota(jnp.int32, (2 * BINS, 4 * BINS), 0)
    col = lax.broadcasted_iota(jnp.int32, (2 * BINS, 4 * BINS), 1)
    bin_of = row % BINS
    threshold = col % BINS
    first_dir = (col // BINS) % 2 == 0
    below = (bin_of < threshold) & (bin_of < BINS - 1)
    missing = (bin_of == BINS - 1) & first_dir
    same = row // BINS == col // (2 * BINS)
    return jnp.where((below | missing) & same, 1.0, 0.0).astype(jnp.bfloat16)


def add_rows(codes_ref, prob_ref, hist_ref, classes, node_count):
    prob = prob_ref[0, :classes, :]
    label = prob_ref[0, classes : classes + 1, :]
    node = prob_ref[0, classes + 1 : classes + 2, :]
    rows = prob.shape[1]
    class_iota = lax.broadcasted_iota(jnp.int32, (classes, rows), 0).astype(jnp.float32)
    target = jnp.where(class_iota == label, 1.0, 0.0)
    grad_hess = jnp.concatenate([prob - target, prob * (1.0 - prob)], axis=0)
    masked = jnp.concatenate(
        [jnp.where(node == float(n), grad_hess, 0.0).astype(jnp.bfloat16) for n in range(node_count)],
        axis=0,
    )
    bin_iota = lax.broadcasted_iota(jnp.int32, (BINS, rows), 0)
    hot = jnp.concatenate(
        [
            jnp.where(codes_ref[0, f : f + 1, :] == bin_iota, 1.0, 0.0).astype(jnp.bfloat16)
            for f in range(codes_ref.shape[1])
        ],
        axis=0,
    )
    hist_ref[...] += lax.dot_general(
        masked, hot, (((1,), (1,)), ((), ())), preferred_element_type=jnp.float32
    )


def hist_kernel(classes, node_count, codes_ref, prob_ref, hist_ref):
    @pl.when(pl.program_id(0) == 0)
    def _():
        hist_ref[...] = jnp.zeros_like(hist_ref)

    add_rows(codes_ref, prob_ref, hist_ref, classes, node_count)


def gain_kernel(classes, node_count, codes_ref, prob_ref, gain_ref, hist_ref):
    @pl.when(pl.program_id(0) == 0)
    def _():
        hist_ref[...] = jnp.zeros_like(hist_ref)

    add_rows(codes_ref, prob_ref, hist_ref, classes, node_count)

    @pl.when(pl.program_id(0) == pl.num_programs(0) - 1)
    def _():
        masks = threshold_masks()
        ones = jnp.where(
            lax.broadcasted_iota(jnp.int32, (2 * BINS, 4 * BINS), 0) < BINS, 1.0, 0.0
        ).astype(jnp.bfloat16)

        def times(parts, right):
            return sum(jnp.dot(part, right, preferred_element_type=jnp.float32) for part in parts)

        total = times(three_parts(hist_ref[:, : 2 * BINS]), ones)
        for pair in range(gain_ref.shape[1] // 2):
            span = slice(pair * 2 * BINS, (pair + 1) * 2 * BINS)
            left = times(three_parts(hist_ref[:, span]), masks)
            right = total - left
            for n in range(node_count):
                grads = slice(n * 2 * classes, n * 2 * classes + classes)
                hesss = slice(n * 2 * classes + classes, (n + 1) * 2 * classes)
                score = (
                    left[grads] * left[grads] / (left[hesss] + reg_lambda)
                    + right[grads] * right[grads] / (right[hesss] + reg_lambda)
                )
                parent = total[grads] * total[grads] / (total[hesss] + reg_lambda)
                gain = (
                    jnp.sum(score, axis=0, keepdims=True) - jnp.sum(parent, axis=0, keepdims=True)
                ) / (2.0 * classes)
                gain_ref[n, 2 * pair : 2 * pair + 1, :] = gain[:, : 2 * BINS]
                gain_ref[n, 2 * pair + 1 : 2 * pair + 2, :] = gain[:, 2 * BINS :]


def local(logits, labels, node_ids, bin_codes, split_feature, split_bin, split_missing):
    rows_dev, classes = logits.shape
    feats_dev = bin_codes.shape[1]
    node_count = split_feature.shape[0]
    n_rows = lax.axis_size("rows")
    per_node = n_rows // node_count
    pairs_dev = feats_dev // per_node
    width = 2 * classes
    feats_own = max(8, feats_dev // n_rows)
    group = feats_dev // feats_own
    group_count = n_rows // group
    row_index = lax.axis_index("rows")
    feat_index = lax.axis_index("feat")

    expo_vals = jnp.exp(logits.T)
    soft_prob = expo_vals / jnp.sum(expo_vals, axis=0, keepdims=True)
    row_info = jnp.concatenate(
        [
            soft_prob,
            labels[None, :].astype(jnp.float32),
            node_ids[None, :].astype(jnp.float32),
        ],
        axis=0,
    )
    if group_count == 1:
        order = (per_node, node_count, feats_own, rows_dev)
        codes_out = bin_codes.T.reshape(order).transpose(1, 0, 2, 3).reshape(group, feats_own, rows_dev)
        members = None
    else:
        codes_out = bin_codes.T.reshape(group, feats_own, rows_dev)
        members = [[g * group + r for r in range(group)] for g in range(group_count)]
    codes_in = lax.all_to_all(codes_out, "rows", 0, 0, tiled=True, axis_index_groups=members)
    info_in = lax.all_gather(row_info, "rows", axis=0, axis_index_groups=members)

    node_iota = jnp.arange(node_count, dtype=jnp.int32)
    node_match = node_ids[:, None] == node_iota[None, :]
    row_feature = jnp.sum(jnp.where(node_match, split_feature[None, :], 0), axis=1)
    row_bin = jnp.sum(jnp.where(node_match, split_bin[None, :], 0), axis=1)
    row_missing = jnp.sum(jnp.where(node_match, split_missing[None, :], 0), axis=1)
    local_col = row_feature - feat_index * feats_dev
    is_owned = (local_col >= 0) & (local_col < feats_dev)
    col_iota = jnp.arange(feats_dev, dtype=jnp.int32)
    row_code = jnp.sum(jnp.where(col_iota[None, :] == local_col[:, None], bin_codes, 0), axis=1)
    goes_left = (row_code < row_bin) | (row_code == BINS - 1) & (row_missing == 1)
    right_flag = jnp.where(is_owned & jnp.logical_not(goes_left), 1.0, 0.0).astype(jnp.float32)
    side_count = lax.psum(right_flag, "feat")
    row_side = (side_count > 0.5).astype(jnp.int32)
    slot_iota = jnp.arange(2 * node_count, dtype=jnp.int32)
    own_slot = node_ids * 2 + jnp.logical_not(goes_left).astype(jnp.int32)
    own_hot = ((own_slot[None, :] == slot_iota[:, None]) & is_owned[None, :]).astype(jnp.bfloat16)
    target = (labels[None, :] == jnp.arange(classes, dtype=jnp.int32)[:, None]).astype(jnp.float32)
    grad_hess = jnp.concatenate(
        [
            (soft_prob - target).astype(jnp.bfloat16),
            (soft_prob * (1.0 - soft_prob)).astype(jnp.bfloat16),
        ],
        axis=0,
    )
    own_sums = lax.dot_general(
        own_hot, grad_hess, (((1,), (1,)), ((), ())), preferred_element_type=jnp.float32
    )
    side_sums = lax.psum(own_sums, ("rows", "feat")).reshape(node_count, 2, width)
    leaves = -side_sums[..., :classes] / (side_sums[..., classes:] + reg_lambda)
    slot_hot = (node_ids * 2 + row_side)[:, None] == slot_iota[None, :]
    update = jnp.dot(
        slot_hot.astype(jnp.float32),
        leaves.reshape(2 * node_count, classes),
        precision=lax.Precision.HIGHEST,
    )
    new_logits = logits + step_size * update

    info_rows = row_info.shape[0]
    in_specs = [
        pl.BlockSpec((1, feats_own, rows_dev), lambda s: (s, 0, 0)),
        pl.BlockSpec((1, info_rows, rows_dev), lambda s: (s, 0, 0)),
    ]
    hist_shape = (node_count * width, feats_own * BINS)
    cost = pl.CostEstimate(
        flops=2 * hist_shape[0] * hist_shape[1] * group * rows_dev,
        bytes_accessed=4 * group * rows_dev * (feats_own + info_rows),
        transcendentals=0,
    )
    params = pltpu.CompilerParams(vmem_limit_bytes=48 * 1024 * 1024)
    if group_count == 1:
        gains = pl.pallas_call(
            functools.partial(gain_kernel, classes, node_count),
            grid=(group,),
            in_specs=in_specs,
            out_specs=pl.BlockSpec((node_count, feats_own, 2 * BINS), lambda s: (0, 0, 0)),
            out_shape=jax.ShapeDtypeStruct((node_count, feats_own, 2 * BINS), jnp.float32),
            scratch_shapes=[pltpu.VMEM(hist_shape, jnp.float32)],
            compiler_params=params,
            cost_estimate=cost,
        )(codes_in, info_in)
        halves = [[h + n * per_node for n in range(node_count)] for h in range(per_node)]
        gain_rows = lax.all_to_all(gains, "rows", 0, 0, tiled=True, axis_index_groups=halves)
        return (new_logits, gain_rows.reshape(1, pairs_dev, 2 * BINS), leaves)

    hist = pl.pallas_call(
        functools.partial(hist_kernel, classes, node_count),
        grid=(group,),
        in_specs=in_specs,
        out_specs=pl.BlockSpec(hist_shape, lambda s: (0, 0)),
        out_shape=jax.ShapeDtypeStruct(hist_shape, jnp.float32),
        compiler_params=params,
        cost_estimate=cost,
    )(codes_in, info_in)
    cuts = feats_own // pairs_dev
    hist = hist.reshape(node_count, width, cuts, pairs_dev, BINS).transpose(0, 2, 3, 4, 1)
    peers = [[g * group + r for g in range(group_count)] for r in range(group)]
    owned = lax.psum_scatter(
        hist.reshape(group_count, pairs_dev, BINS, width),
        "rows",
        scatter_dimension=0,
        axis_index_groups=peers,
    )
    bin_iota = jnp.arange(BINS, dtype=jnp.int32)
    lower_mask = (
        (bin_iota[:, None] < bin_iota[None, :]) & (bin_iota[:, None] < BINS - 1)
    ).astype(jnp.float32)
    left_base = jnp.einsum("pbc,bt->ptc", owned, lower_mask, precision=lax.Precision.HIGHEST)
    node_total = jnp.sum(owned, axis=1, keepdims=True)
    left_miss = left_base + owned[:, BINS - 1 :, :]
    parent_score = split_score(node_total, classes)
    gain_left = (
        split_score(left_miss, classes)
        + split_score(node_total - left_miss, classes)
        - parent_score
    )
    gain_right = (
        split_score(left_base, classes)
        + split_score(node_total - left_base, classes)
        - parent_score
    )
    gain = jnp.concatenate([gain_left, gain_right], axis=1) / (2.0 * classes)
    moves = [
        (n * per_node + cut * group + r, n * per_node + r * cuts + cut)
        for n in range(node_count)
        for cut in range(cuts)
        for r in range(group)
    ]
    gain_rows = lax.ppermute(gain, "rows", moves)
    return (new_logits, gain_rows[None], leaves)


def solution(mesh):
    return jax.shard_map(
        local,
        mesh=mesh,
        in_specs=(P("rows", None), P("rows"), P("rows"), P("rows", "feat"), P(), P(), P()),
        out_specs=(P("rows", None), P("rows", "feat", None), P()),
        check_vma=False,
    )
```

```python
import functools

import jax
import jax.numpy as jnp
from jax import lax
from jax.experimental import pallas as pl
from jax.experimental.pallas import tpu as pltpu
from jax.sharding import PartitionSpec as P

BINS = 64
LANES = 128


reg_lambda = 1.0
step_size = 0.3


def split_score(sums, classes):
    grad_part = sums[..., :classes]
    hess_part = sums[..., classes:]
    return jnp.sum(grad_part * grad_part / (hess_part + reg_lambda), axis=-1)


def three_parts(x):
    first = x.astype(jnp.bfloat16)
    rest = x - first.astype(jnp.float32)
    second = rest.astype(jnp.bfloat16)
    third = (rest - second.astype(jnp.float32)).astype(jnp.bfloat16)
    return first, second, third


def threshold_masks():
    row = lax.broadcasted_iota(jnp.int32, (2 * BINS, 4 * BINS), 0)
    col = lax.broadcasted_iota(jnp.int32, (2 * BINS, 4 * BINS), 1)
    bin_of = row % BINS
    threshold = col % BINS
    first_dir = (col // BINS) % 2 == 0
    below = (bin_of < threshold) & (bin_of < BINS - 1)
    missing = (bin_of == BINS - 1) & first_dir
    same = row // BINS == col // (2 * BINS)
    return jnp.where((below | missing) & same, 1.0, 0.0).astype(jnp.bfloat16)


def info_kernel(logits_ref, labels_ref, nodes_ref, info_ref):
    rows, classes = logits_ref.shape
    expo_vals = jnp.exp(logits_ref[...].T)
    info_ref[:, :rows] = expo_vals / jnp.sum(expo_vals, axis=0, keepdims=True)
    chunks = rows // LANES
    info_ref[:, rows:] = jnp.zeros((classes, 2 * LANES), jnp.float32)
    info_ref[:chunks, rows : rows + LANES] = labels_ref[...].astype(jnp.float32)
    info_ref[:chunks, rows + LANES :] = nodes_ref[...].astype(jnp.float32)


def read_info(info, rows):
    chunks = rows // LANES
    prob = info[:, :rows]
    labels = info[:, rows : rows + LANES]
    nodes = info[:, rows + LANES : rows + 2 * LANES]
    label = jnp.concatenate([labels[i : i + 1] for i in range(chunks)], axis=1)
    node = jnp.concatenate([nodes[i : i + 1] for i in range(chunks)], axis=1)
    return prob, label, node


def codes_kernel(group, own, starts_ref, codes_ref, *refs):
    outs, turned = refs[:-1], refs[-1]
    turned[...] = codes_ref[...].T
    for m in range(group):
        start = pl.multiple_of(starts_ref[m], own)
        outs[m][...] = turned[pl.ds(start, own), :]


def side_kernel(node_count, split_ref, info_ref, codes_ref, flag_ref, sums_ref, turned):
    rows, feats = codes_ref.shape
    prob, label, node = read_info(info_ref[...], rows)
    turned[...] = codes_ref[...].T
    side = jnp.zeros((1, rows), jnp.float32)
    for n in range(node_count):
        col = split_ref[0, n]
        held = (col >= 0) & (col < feats)
        code = turned[pl.ds(jnp.clip(col, 0, feats - 1), 1), :]
        threshold = jnp.where(held, split_ref[1, n], -1)
        last = jnp.where(held & (split_ref[2, n] == 1), BINS - 1, -1)
        left = (code < threshold) | (code == last)
        value = jnp.where(left, 1.0, jnp.where(held, 2.0, 0.0))
        side = jnp.where(node == float(n), value, side)
    flag_ref[...] = jnp.where(side == 2.0, 1.0, 0.0)
    grad_hess = gradients(prob, label)
    hot = jnp.concatenate(
        [
            jnp.where((node == float(slot // 2)) & (side == float(slot % 2 + 1)), 1.0, 0.0)
            for slot in range(2 * node_count)
        ],
        axis=0,
    ).astype(jnp.bfloat16)
    sums_ref[...] = lax.dot_general(
        hot,
        grad_hess.astype(jnp.bfloat16),
        (((1,), (1,)), ((), ())),
        preferred_element_type=jnp.float32,
    )


def gradients(prob, label):
    class_iota = lax.broadcasted_iota(jnp.int32, prob.shape, 0).astype(jnp.float32)
    target = jnp.where(class_iota == label, 1.0, 0.0)
    return jnp.concatenate([prob - target, prob * (1.0 - prob)], axis=0)


def add_rows(codes, info, hist_ref, node_count):
    feats, rows = codes.shape
    prob, label, node = read_info(info, rows)
    grad_hess = gradients(prob, label)
    masked = jnp.concatenate(
        [jnp.where(node == float(n), grad_hess, 0.0).astype(jnp.bfloat16) for n in range(node_count)],
        axis=0,
    )
    bin_iota = lax.broadcasted_iota(jnp.int32, (BINS, rows), 0)
    hot = jnp.concatenate(
        [
            jnp.where(codes[f : f + 1, :] == bin_iota, 1.0, 0.0).astype(jnp.bfloat16)
            for f in range(feats)
        ],
        axis=0,
    )
    hist_ref[...] += lax.dot_general(
        masked, hot, (((1,), (1,)), ((), ())), preferred_element_type=jnp.float32
    )


def write_gains(hist_ref, gain_ref, classes, node_count):
    masks = threshold_masks()
    ones = jnp.where(
        lax.broadcasted_iota(jnp.int32, (2 * BINS, 4 * BINS), 0) < BINS, 1.0, 0.0
    ).astype(jnp.bfloat16)

    def times(parts, right):
        return sum(jnp.dot(part, right, preferred_element_type=jnp.float32) for part in parts)

    total = times(three_parts(hist_ref[:, : 2 * BINS]), ones)
    for pair in range(gain_ref.shape[1] // 2):
        span = slice(pair * 2 * BINS, (pair + 1) * 2 * BINS)
        left = times(three_parts(hist_ref[:, span]), masks)
        right = total - left
        for n in range(node_count):
            grads = slice(n * 2 * classes, n * 2 * classes + classes)
            hesss = slice(n * 2 * classes + classes, (n + 1) * 2 * classes)
            score = (
                left[grads] * left[grads] / (left[hesss] + reg_lambda)
                + right[grads] * right[grads] / (right[hesss] + reg_lambda)
            )
            parent = total[grads] * total[grads] / (total[hesss] + reg_lambda)
            gain = (
                jnp.sum(score, axis=0, keepdims=True) - jnp.sum(parent, axis=0, keepdims=True)
            ) / (2.0 * classes)
            gain_ref[n, 2 * pair : 2 * pair + 1, :] = gain[:, : 2 * BINS]
            gain_ref[n, 2 * pair + 1 : 2 * pair + 2, :] = gain[:, 2 * BINS :]


def hist_kernel(classes, node_count, sources, first, gains, *refs):
    codes_refs, info_refs = refs[:sources], refs[sources : 2 * sources]
    rest = refs[2 * sources :]
    hist_in = None
    if not first:
        hist_in, rest = rest[0], rest[1:]
    out_ref, codes_buf, info_buf, code_sems, info_sems = rest[:5]
    hist_ref = rest[5] if gains else out_ref
    for s in range(sources):
        pltpu.make_async_copy(codes_refs[s], codes_buf.at[s], code_sems.at[s]).start()
        pltpu.make_async_copy(info_refs[s], info_buf.at[s], info_sems.at[s]).start()
    hist_ref[...] = jnp.zeros_like(hist_ref) if first else hist_in[...]

    @pl.loop(0, sources)
    def _(s):
        pltpu.make_async_copy(codes_buf.at[s], codes_buf.at[s], code_sems.at[s]).wait()
        pltpu.make_async_copy(info_buf.at[s], info_buf.at[s], info_sems.at[s]).wait()
        add_rows(codes_buf[s], info_buf[s], hist_ref, node_count)

    if gains:
        write_gains(hist_ref, out_ref, classes, node_count)


def add_sources(classes, node_count, codes, infos, hist, gains):
    sources = len(codes)
    own, rows = codes[0].shape
    info_shape = infos[0].shape
    hist_shape = (2 * classes * node_count, own * BINS)
    anywhere = pl.BlockSpec(memory_space=pl.ANY)
    whole = pl.BlockSpec(memory_space=pltpu.VMEM)
    out_shape = (node_count, own, 2 * BINS) if gains else hist_shape
    scratch = [
        pltpu.VMEM((sources, own, rows), jnp.int32),
        pltpu.VMEM((sources,) + info_shape, jnp.float32),
        pltpu.SemaphoreType.DMA((sources,)),
        pltpu.SemaphoreType.DMA((sources,)),
    ]
    if gains:
        scratch.append(pltpu.VMEM(hist_shape, jnp.float32))
    held = [] if hist is None else [hist]
    return pl.pallas_call(
        functools.partial(hist_kernel, classes, node_count, sources, hist is None, gains),
        in_specs=[anywhere] * (2 * sources) + [whole] * len(held),
        out_specs=whole,
        out_shape=jax.ShapeDtypeStruct(out_shape, jnp.float32),
        scratch_shapes=scratch,
        compiler_params=pltpu.CompilerParams(vmem_limit_bytes=48 * 1024 * 1024),
        cost_estimate=pl.CostEstimate(
            flops=2 * hist_shape[0] * hist_shape[1] * sources * rows,
            bytes_accessed=4 * sources * rows * (own + classes) + 8 * hist_shape[0] * hist_shape[1],
            transcendentals=0,
        ),
    )(*codes, *infos, *held)


def swap(x, axis, bit):
    size = lax.axis_size(axis)
    return lax.ppermute(x, axis, [(i, i ^ bit) for i in range(size)])


def sum_over(x, axis):
    bit = 1
    while bit < lax.axis_size(axis):
        x = x + swap(x, axis, bit)
        bit *= 2
    return x


def local(logits, labels, node_ids, bin_codes, split_feature, split_bin, split_missing):
    rows_dev, classes = logits.shape
    feats_dev = bin_codes.shape[1]
    node_count = split_feature.shape[0]
    n_rows = lax.axis_size("rows")
    per_node = n_rows // node_count
    pairs_dev = feats_dev // per_node
    width = 2 * classes
    feats_own = max(8, feats_dev // n_rows)
    group = feats_dev // feats_own
    group_count = n_rows // group
    row_index = lax.axis_index("rows")
    feat_index = lax.axis_index("feat")
    whole = pl.BlockSpec(memory_space=pltpu.VMEM)
    scalars = pl.BlockSpec(memory_space=pltpu.SMEM)
    params = pltpu.CompilerParams(vmem_limit_bytes=48 * 1024 * 1024)

    info = pl.pallas_call(
        info_kernel,
        in_specs=[whole] * 3,
        out_specs=whole,
        out_shape=jax.ShapeDtypeStruct((classes, rows_dev + 2 * LANES), jnp.float32),
        compiler_params=params,
    )(logits, labels.reshape(-1, LANES), node_ids.reshape(-1, LANES))

    taker = row_index ^ jnp.arange(group, dtype=jnp.int32)
    if group_count == 1:
        starts = (taker % per_node) * pairs_dev + (taker // per_node) * feats_own
    else:
        starts = (taker % group) * feats_own
    codes_out = pl.pallas_call(
        functools.partial(codes_kernel, group, feats_own),
        in_specs=[scalars, whole],
        out_specs=[whole] * group,
        out_shape=[jax.ShapeDtypeStruct((feats_own, rows_dev), jnp.int32)] * group,
        scratch_shapes=[pltpu.VMEM((feats_dev, rows_dev), jnp.int32)],
        compiler_params=params,
    )(starts, bin_codes)

    infos = [info] + [None] * (group - 1)
    for m in sorted(range(1, group), key=lambda m: -(m & -m)):
        low = m & -m
        infos[m] = swap(infos[m ^ low], "rows", low)
    codes_in = [codes_out[0]] + [swap(codes_out[m], "rows", m) for m in range(1, group)]

    splits = jnp.stack([split_feature - feat_index * feats_dev, split_bin, split_missing])
    right_flag, own_sums = pl.pallas_call(
        functools.partial(side_kernel, node_count),
        in_specs=[scalars, whole, whole],
        out_specs=[whole, whole],
        out_shape=[
            jax.ShapeDtypeStruct((1, rows_dev), jnp.float32),
            jax.ShapeDtypeStruct((2 * node_count, width), jnp.float32),
        ],
        scratch_shapes=[pltpu.VMEM((feats_dev, rows_dev), jnp.int32)],
        compiler_params=params,
    )(splits, info, bin_codes)
    side_count = sum_over(right_flag, "feat")[0]
    side_sums = sum_over(sum_over(own_sums, "rows"), "feat").reshape(node_count, 2, width)
    leaves = -side_sums[..., :classes] / (side_sums[..., classes:] + reg_lambda)
    row_side = (side_count > 0.5).astype(jnp.int32)
    slot_iota = jnp.arange(2 * node_count, dtype=jnp.int32)
    slot_hot = (node_ids * 2 + row_side)[:, None] == slot_iota[None, :]
    update = jnp.dot(
        slot_hot.astype(jnp.float32),
        leaves.reshape(2 * node_count, classes),
        precision=lax.Precision.HIGHEST,
    )
    new_logits = logits + step_size * update

    batch = 4
    hist = None
    for low in range(0, group, batch):
        span = slice(low, low + batch)
        gains = group_count == 1 and low + batch >= group
        hist = add_sources(classes, node_count, codes_in[span], infos[span], hist, gains)
    if group_count == 1:
        halves = [[h + n * per_node for n in range(node_count)] for h in range(per_node)]
        gain_rows = lax.all_to_all(hist, "rows", 0, 0, tiled=True, axis_index_groups=halves)
        return (new_logits, gain_rows.reshape(1, pairs_dev, 2 * BINS), leaves)

    cuts = feats_own // pairs_dev
    hist = hist.reshape(node_count, width, cuts, pairs_dev, BINS).transpose(0, 2, 3, 4, 1)
    peers = [[g * group + r for g in range(group_count)] for r in range(group)]
    owned = lax.psum_scatter(
        hist.reshape(group_count, pairs_dev, BINS, width),
        "rows",
        scatter_dimension=0,
        axis_index_groups=peers,
    )
    bin_iota = jnp.arange(BINS, dtype=jnp.int32)
    lower_mask = (
        (bin_iota[:, None] < bin_iota[None, :]) & (bin_iota[:, None] < BINS - 1)
    ).astype(jnp.float32)
    left_base = jnp.einsum("pbc,bt->ptc", owned, lower_mask, precision=lax.Precision.HIGHEST)
    node_total = jnp.sum(owned, axis=1, keepdims=True)
    left_miss = left_base + owned[:, BINS - 1 :, :]
    parent_score = split_score(node_total, classes)
    gain_left = (
        split_score(left_miss, classes)
        + split_score(node_total - left_miss, classes)
        - parent_score
    )
    gain_right = (
        split_score(left_base, classes)
        + split_score(node_total - left_base, classes)
        - parent_score
    )
    gain = jnp.concatenate([gain_left, gain_right], axis=1) / (2.0 * classes)
    moves = [
        (n * per_node + cut * group + r, n * per_node + r * cuts + cut)
        for n in range(node_count)
        for cut in range(cuts)
        for r in range(group)
    ]
    gain_rows = lax.ppermute(gain, "rows", moves)
    return (new_logits, gain_rows[None], leaves)


def solution(mesh):
    return jax.shard_map(
        local,
        mesh=mesh,
        in_specs=(P("rows", None), P("rows"), P("rows"), P("rows", "feat"), P(), P(), P()),
        out_specs=(P("rows", None), P("rows", "feat", None), P()),
        check_vma=False,
    )
```

```python
import functools

import jax
import jax.numpy as jnp
from jax import lax
from jax.experimental import pallas as pl
from jax.experimental.pallas import tpu as pltpu
from jax.sharding import PartitionSpec as P

BINS = 64
LANES = 128
BATCHES = ((2, 4, 6, 8), (10, 12), (14,))
SMALL_COST = pl.CostEstimate(flops=1000000, bytes_accessed=1000000, transcendentals=0)


reg_lambda = 1.0
step_size = 0.3


def split_score(sums, classes):
    grad_part = sums[..., :classes]
    hess_part = sums[..., classes:]
    return jnp.sum(grad_part * grad_part / (hess_part + reg_lambda), axis=-1)


def three_parts(x):
    first = x.astype(jnp.bfloat16)
    rest = x - first.astype(jnp.float32)
    second = rest.astype(jnp.bfloat16)
    third = (rest - second.astype(jnp.float32)).astype(jnp.bfloat16)
    return first, second, third


def threshold_masks():
    row = lax.broadcasted_iota(jnp.int32, (2 * BINS, 4 * BINS), 0)
    col = lax.broadcasted_iota(jnp.int32, (2 * BINS, 4 * BINS), 1)
    bin_of = row % BINS
    threshold = col % BINS
    first_dir = (col // BINS) % 2 == 0
    below = (bin_of < threshold) & (bin_of < BINS - 1)
    missing = (bin_of == BINS - 1) & first_dir
    same = row // BINS == col // (2 * BINS)
    return jnp.where((below | missing) & same, 1.0, 0.0).astype(jnp.bfloat16)


def info_kernel(logits_ref, labels_ref, nodes_ref, info_ref):
    classes, rows = logits_ref.shape
    expo_vals = jnp.exp(logits_ref[...])
    info_ref[:, :rows] = expo_vals / jnp.sum(expo_vals, axis=0, keepdims=True)
    chunks = rows // LANES
    info_ref[:, rows:] = jnp.zeros((classes, 2 * LANES), jnp.float32)
    info_ref[:chunks, rows : rows + LANES] = labels_ref[...].astype(jnp.float32)
    info_ref[:chunks, rows + LANES :] = nodes_ref[...].astype(jnp.float32)


def read_info(info, rows):
    chunks = rows // LANES
    prob = info[:, :rows]
    labels = info[:, rows : rows + LANES]
    nodes = info[:, rows + LANES : rows + 2 * LANES]
    label = jnp.concatenate([labels[i : i + 1] for i in range(chunks)], axis=1)
    node = jnp.concatenate([nodes[i : i + 1] for i in range(chunks)], axis=1)
    return prob, label, node


def codes_kernel(own, starts_ref, split_ref, codes_ref, sent_ref, kept_ref, picked_ref, turned):
    turned[...] = codes_ref[...].T
    for half, out_ref in ((1, sent_ref), (0, kept_ref)):
        for m in range(out_ref.shape[0]):
            start = pl.multiple_of(starts_ref[half, m], own)
            out_ref[m] = turned[pl.ds(start, own), :]
    for n in range(picked_ref.shape[0]):
        col = jnp.clip(split_ref[0, n], 0, turned.shape[0] - 1)
        picked_ref[n : n + 1, :] = turned[pl.ds(col, 1), :]


def side_kernel(feats, split_ref, info_ref, picked_ref, flag_ref, sums_ref):
    node_count, rows = picked_ref.shape
    prob, label, node = read_info(info_ref[...], rows)
    side = jnp.zeros((1, rows), jnp.float32)
    for n in range(node_count):
        col = split_ref[0, n]
        held = (col >= 0) & (col < feats)
        code = picked_ref[n : n + 1, :]
        threshold = jnp.where(held, split_ref[1, n], -1)
        last = jnp.where(held & (split_ref[2, n] == 1), BINS - 1, -1)
        left = (code < threshold) | (code == last)
        value = jnp.where(left, 1.0, jnp.where(held, 2.0, 0.0))
        side = jnp.where(node == float(n), value, side)
    flag_ref[...] = jnp.where(side == 2.0, 1.0, 0.0)
    grad_hess = gradients(prob, label)
    hot = jnp.concatenate(
        [
            jnp.where((node == float(slot // 2)) & (side == float(slot % 2 + 1)), 1.0, 0.0)
            for slot in range(2 * node_count)
        ],
        axis=0,
    ).astype(jnp.bfloat16)
    sums_ref[...] = lax.dot_general(
        hot,
        grad_hess.astype(jnp.bfloat16),
        (((1,), (1,)), ((), ())),
        preferred_element_type=jnp.float32,
    )


def gradients(prob, label):
    class_iota = lax.broadcasted_iota(jnp.int32, prob.shape, 0).astype(jnp.float32)
    target = jnp.where(class_iota == label, 1.0, 0.0)
    return jnp.concatenate([prob - target, prob * (1.0 - prob)], axis=0)


def masked_gradients(info, rows, node_count):
    prob, label, node = read_info(info, rows)
    grad_hess = gradients(prob, label)
    return jnp.concatenate(
        [jnp.where(node == float(n), grad_hess, 0.0).astype(jnp.bfloat16) for n in range(node_count)],
        axis=0,
    )


def one_hot(codes):
    feats, rows = codes.shape
    bin_iota = lax.broadcasted_iota(jnp.int32, (BINS, rows), 0)
    return jnp.concatenate(
        [
            jnp.where(codes[f : f + 1, :] == bin_iota, 1.0, 0.0).astype(jnp.bfloat16)
            for f in range(feats)
        ],
        axis=0,
    )


def write_gains(hist_ref, gain_ref, classes, node_count):
    masks = threshold_masks()
    ones = jnp.where(
        lax.broadcasted_iota(jnp.int32, (2 * BINS, 4 * BINS), 0) < BINS, 1.0, 0.0
    ).astype(jnp.bfloat16)

    def times(parts, right):
        return sum(jnp.dot(part, right, preferred_element_type=jnp.float32) for part in parts)

    total = times(three_parts(hist_ref[:, : 2 * BINS]), ones)
    for pair in range(gain_ref.shape[1] // 2):
        span = slice(pair * 2 * BINS, (pair + 1) * 2 * BINS)
        left = times(three_parts(hist_ref[:, span]), masks)
        right = total - left
        for n in range(node_count):
            grads = slice(n * 2 * classes, n * 2 * classes + classes)
            hesss = slice(n * 2 * classes + classes, (n + 1) * 2 * classes)
            score = (
                left[grads] * left[grads] / (left[hesss] + reg_lambda)
                + right[grads] * right[grads] / (right[hesss] + reg_lambda)
            )
            parent = total[grads] * total[grads] / (total[hesss] + reg_lambda)
            gain = (
                jnp.sum(score, axis=0, keepdims=True) - jnp.sum(parent, axis=0, keepdims=True)
            ) / (2.0 * classes)
            gain_ref[n, 2 * pair : 2 * pair + 1, :] = gain[:, : 2 * BINS]
            gain_ref[n, 2 * pair + 1 : 2 * pair + 2, :] = gain[:, 2 * BINS :]


def hist_kernel(node_count, places, first, places_ref, codes_ref, *refs):
    info_refs = refs[: len(places)]
    out_ref = refs[-1]
    for s, place in enumerate(places):
        codes = codes_ref[places_ref[place]]
        masked = masked_gradients(info_refs[s][...], codes.shape[1], node_count)
        product = lax.dot_general(
            masked, one_hot(codes), (((1,), (1,)), ((), ())), preferred_element_type=jnp.float32
        )
        if s > 0:
            out_ref[...] += product
        elif first:
            out_ref[...] = product
        else:
            out_ref[...] = refs[len(places)][...] + product


def add_sources(classes, node_count, sources, places, codes, infos, hist):
    own = codes.shape[1]
    hist_shape = (2 * classes * node_count, own * BINS)
    whole = pl.BlockSpec(memory_space=pltpu.VMEM)
    held = [] if hist is None else [hist]
    return pl.pallas_call(
        functools.partial(hist_kernel, node_count, [m // 2 for m in sources], hist is None),
        in_specs=[pl.BlockSpec(memory_space=pltpu.SMEM)] + [whole] * (1 + len(sources) + len(held)),
        out_specs=whole,
        out_shape=jax.ShapeDtypeStruct(hist_shape, jnp.float32),
        compiler_params=pltpu.CompilerParams(vmem_limit_bytes=32 * 1024 * 1024),
        cost_estimate=SMALL_COST,
    )(places, codes, *[infos[m] for m in sources], *held)


def gain_kernel(classes, node_count, kept_ref, came_ref, gain_ref, hist_ref):
    hist_ref[...] = kept_ref[...] + came_ref[...]
    write_gains(hist_ref, gain_ref, classes, node_count)


def swap(x, axis, bit):
    size = lax.axis_size(axis)
    return lax.ppermute(x, axis, [(i, i ^ bit) for i in range(size)])


def local(logits, labels, node_ids, bin_codes, split_feature, split_bin, split_missing):
    rows_dev, classes = logits.shape
    feats_dev = bin_codes.shape[1]
    node_count = split_feature.shape[0]
    n_rows = lax.axis_size("rows")
    per_node = n_rows // node_count
    pairs_dev = feats_dev // per_node
    width = 2 * classes
    feats_own = max(8, feats_dev // n_rows)
    group = feats_dev // feats_own
    group_count = n_rows // group
    row_index = lax.axis_index("rows")
    feat_index = lax.axis_index("feat")
    whole = pl.BlockSpec(memory_space=pltpu.VMEM)
    scalars = pl.BlockSpec(memory_space=pltpu.SMEM)
    params = pltpu.CompilerParams(vmem_limit_bytes=16 * 1024 * 1024)

    logits_t = logits.T
    info = pl.pallas_call(
        info_kernel,
        in_specs=[whole] * 3,
        out_specs=whole,
        out_shape=jax.ShapeDtypeStruct((classes, rows_dev + 2 * LANES), jnp.float32),
        compiler_params=params,
        cost_estimate=SMALL_COST,
    )(logits_t, labels.reshape(-1, LANES), node_ids.reshape(-1, LANES))

    parity = row_index % 2
    sources = list(range(0, group, 2))
    chip_count = len(sources)
    chip = jnp.arange(chip_count, dtype=jnp.int32)
    half_of = jnp.stack([parity, 1 - parity])[:, None]
    if group_count == 1:
        starts = half_of * pairs_dev + (chip * 2 // per_node)[None, :] * feats_own
    else:
        starts = (chip[None, :] * 2 + half_of) * feats_own
    splits = jnp.stack([split_feature - feat_index * feats_dev, split_bin, split_missing])
    block_shape = jax.ShapeDtypeStruct((chip_count, feats_own, rows_dev), jnp.int32)
    codes_sent, codes_kept, picked = pl.pallas_call(
        functools.partial(codes_kernel, feats_own),
        in_specs=[scalars, scalars, whole],
        out_specs=[whole] * 3,
        out_shape=[
            block_shape,
            block_shape,
            jax.ShapeDtypeStruct((node_count, rows_dev), jnp.int32),
        ],
        scratch_shapes=[pltpu.VMEM((feats_dev, rows_dev), jnp.int32)],
        compiler_params=params,
        cost_estimate=SMALL_COST,
    )(starts, splits, bin_codes)
    members = [
        [g * group + 2 * r + k for r in range(chip_count)] for g in range(group_count) for k in range(2)
    ]
    places = (row_index % group // 2) ^ chip
    here = jnp.zeros((chip_count,), jnp.int32) + row_index % group // 2

    def exchange(blocks):
        return lax.all_to_all(blocks, "rows", 0, 0, tiled=True, axis_index_groups=members)

    add = functools.partial(add_sources, classes, node_count)
    infos = {0: info}
    came_sent = exchange(codes_sent)
    for m in sources[1:]:
        if m & (m - 1) == 0:
            infos[m] = swap(info, "rows", m)
    own_sent = add((0,), here, codes_sent, infos, None)
    own_kept = add((0,), here, codes_kept, infos, None)
    for m in sorted(sources[1:], key=lambda m: -(m & -m)):
        low = m & -m
        if m != low:
            infos[m] = swap(infos[m ^ low], "rows", low)

    right_flag, own_sums = pl.pallas_call(
        functools.partial(side_kernel, feats_dev),
        in_specs=[scalars, whole, whole],
        out_specs=[whole, whole],
        out_shape=[
            jax.ShapeDtypeStruct((1, rows_dev), jnp.float32),
            jax.ShapeDtypeStruct((2 * node_count, width), jnp.float32),
        ],
        compiler_params=params,
        cost_estimate=SMALL_COST,
    )(splits, info, picked)
    side_count = jnp.sum(lax.all_gather(right_flag, "feat"), axis=0)
    all_sums = lax.all_gather(own_sums, ("rows", "feat"))
    side_sums = jnp.sum(all_sums, axis=0).reshape(node_count, 2, width)
    leaves = -side_sums[..., :classes] / (side_sums[..., classes:] + reg_lambda)
    row_side = (side_count > 0.5).astype(jnp.int32)
    slot_iota = jnp.arange(2 * node_count, dtype=jnp.int32)
    slot_hot = (node_ids[None, :] * 2 + row_side) == slot_iota[:, None]
    update = jnp.dot(
        leaves.reshape(2 * node_count, classes).T,
        slot_hot.astype(jnp.float32),
        precision=lax.Precision.HIGHEST,
    )
    new_logits = (logits_t + step_size * update).T

    came_sent, codes_kept = lax.optimization_barrier((came_sent, codes_kept))
    came_kept = exchange(codes_kept)
    batches = BATCHES if chip_count == 8 else tuple((m,) for m in sources[1:])
    hist = own_sent
    for batch in batches:
        hist = add(batch, places, came_sent, infos, hist)
    came = swap(hist, "rows", 1)
    kept = add(tuple(sources[1:]), places, came_kept, infos, own_kept)
    if group_count == 1:
        gains = pl.pallas_call(
            functools.partial(gain_kernel, classes, node_count),
            in_specs=[whole] * 2,
            out_specs=whole,
            out_shape=jax.ShapeDtypeStruct((node_count, feats_own, 2 * BINS), jnp.float32),
            scratch_shapes=[pltpu.VMEM(kept.shape, jnp.float32)],
            compiler_params=params,
            cost_estimate=SMALL_COST,
        )(kept, came)
        halves = [[h + n * per_node for n in range(node_count)] for h in range(per_node)]
        gain_rows = lax.all_to_all(gains, "rows", 0, 0, tiled=True, axis_index_groups=halves)
        return (new_logits, gain_rows.reshape(1, pairs_dev, 2 * BINS), leaves)
    hist = kept + came

    cuts = feats_own // pairs_dev
    hist = hist.reshape(node_count, width, cuts, pairs_dev, BINS).transpose(0, 2, 3, 4, 1)
    peers = [[g * group + r for g in range(group_count)] for r in range(group)]
    owned = lax.psum_scatter(
        hist.reshape(group_count, pairs_dev, BINS, width),
        "rows",
        scatter_dimension=0,
        axis_index_groups=peers,
    )
    bin_iota = jnp.arange(BINS, dtype=jnp.int32)
    lower_mask = (
        (bin_iota[:, None] < bin_iota[None, :]) & (bin_iota[:, None] < BINS - 1)
    ).astype(jnp.float32)
    left_base = jnp.einsum("pbc,bt->ptc", owned, lower_mask, precision=lax.Precision.HIGHEST)
    node_total = jnp.sum(owned, axis=1, keepdims=True)
    left_miss = left_base + owned[:, BINS - 1 :, :]
    parent_score = split_score(node_total, classes)
    gain_left = (
        split_score(left_miss, classes)
        + split_score(node_total - left_miss, classes)
        - parent_score
    )
    gain_right = (
        split_score(left_base, classes)
        + split_score(node_total - left_base, classes)
        - parent_score
    )
    gain = jnp.concatenate([gain_left, gain_right], axis=1) / (2.0 * classes)
    moves = [
        (n * per_node + cut * group + r, n * per_node + r * cuts + cut)
        for n in range(node_count)
        for cut in range(cuts)
        for r in range(group)
    ]
    gain_rows = lax.ppermute(gain, "rows", moves)
    return (new_logits, gain_rows[None], leaves)


def solution(mesh):
    return jax.shard_map(
        local,
        mesh=mesh,
        in_specs=(P("rows", None), P("rows"), P("rows"), P("rows", "feat"), P(), P(), P()),
        out_specs=(P("rows", None), P("rows", "feat", None), P()),
        check_vma=False,
    )
```

```python
import functools

import jax
import jax.numpy as jnp
from jax import lax
from jax.experimental import pallas as pl
from jax.experimental.pallas import tpu as pltpu
from jax.sharding import PartitionSpec as P

BINS = 64
LANES = 128
SMALL_COST = pl.CostEstimate(flops=1000000, bytes_accessed=1000000, transcendentals=0)


reg_lambda = 1.0
step_size = 0.3


def split_score(sums, classes):
    grad_part = sums[..., :classes]
    hess_part = sums[..., classes:]
    return jnp.sum(grad_part * grad_part / (hess_part + reg_lambda), axis=-1)


def three_parts(x):
    first = x.astype(jnp.bfloat16)
    rest = x - first.astype(jnp.float32)
    second = rest.astype(jnp.bfloat16)
    third = (rest - second.astype(jnp.float32)).astype(jnp.bfloat16)
    return first, second, third


def threshold_masks():
    row = lax.broadcasted_iota(jnp.int32, (2 * BINS, 4 * BINS), 0)
    col = lax.broadcasted_iota(jnp.int32, (2 * BINS, 4 * BINS), 1)
    bin_of = row % BINS
    threshold = col % BINS
    first_dir = (col // BINS) % 2 == 0
    below = (bin_of < threshold) & (bin_of < BINS - 1)
    missing = (bin_of == BINS - 1) & first_dir
    same = row // BINS == col // (2 * BINS)
    return jnp.where((below | missing) & same, 1.0, 0.0).astype(jnp.bfloat16)


def read_info(info, rows):
    chunks = rows // LANES
    prob = info[:, :rows]
    labels = info[:, rows : rows + LANES]
    nodes = info[:, rows + LANES : rows + 2 * LANES]
    label = jnp.concatenate([labels[i : i + 1] for i in range(chunks)], axis=1)
    node = jnp.concatenate([nodes[i : i + 1] for i in range(chunks)], axis=1)
    return prob, label, node


def prep_kernel(
    own, blocks, starts_ref, split_ref, logits_ref, labels_ref, nodes_ref, codes_ref, *refs
):
    outs, flag_ref, turned = refs[: len(blocks)], refs[-2], refs[-1]
    classes, rows = logits_ref.shape
    chunks = rows // LANES
    turned[...] = codes_ref[...].T
    for (with_info, pieces), out_ref in zip(blocks, outs):
        base = classes if with_info else 0
        for i, (taker, quarter) in enumerate(pieces):
            start = pl.multiple_of(starts_ref[taker, quarter], own)
            low = base + i * own
            out_ref[low : low + own, :rows] = turned[pl.ds(start, own), :].astype(out_ref.dtype)
            if with_info:
                out_ref[low : low + own, rows:] = jnp.zeros((own, 2 * LANES), out_ref.dtype)
    expo_vals = jnp.exp(logits_ref[...])
    prob = expo_vals / jnp.sum(expo_vals, axis=0, keepdims=True)
    labels = labels_ref[...].astype(jnp.float32)
    nodes = nodes_ref[...].astype(jnp.float32)
    label = jnp.concatenate([labels[i : i + 1] for i in range(chunks)], axis=1)
    node = jnp.concatenate([nodes[i : i + 1] for i in range(chunks)], axis=1)

    feats = turned.shape[0]
    node_count = split_ref.shape[1]
    side = jnp.zeros((1, rows), jnp.float32)
    for n in range(node_count):
        col = split_ref[0, n]
        held = (col >= 0) & (col < feats)
        code = turned[pl.ds(jnp.clip(col, 0, feats - 1), 1), :]
        threshold = jnp.where(held, split_ref[1, n], -1)
        missing = jnp.where(held & (split_ref[2, n] == 1), BINS - 1, -1)
        left = (code < threshold) | (code == missing)
        value = jnp.where(left, 1.0, jnp.where(held, 2.0, 0.0))
        side = jnp.where(node == float(n), value, side)
    flag_ref[...] = jnp.where(side == 2.0, 1.0, 0.0)
    hot = jnp.concatenate(
        [
            jnp.where((node == float(slot // 2)) & (side == float(slot % 2 + 1)), 1.0, 0.0)
            for slot in range(2 * node_count)
        ],
        axis=0,
    ).astype(jnp.bfloat16)
    sums = lax.dot_general(
        hot,
        gradients(prob, label).astype(jnp.bfloat16),
        (((1,), (1,)), ((), ())),
        preferred_element_type=jnp.float32,
    )
    sums = jnp.concatenate([sums[:node_count], sums[node_count:]], axis=1)
    for (with_info, _), out_ref in zip(blocks, outs):
        if with_info:
            out_ref[:classes, :rows] = prob
            out_ref[:chunks, rows : rows + LANES] = labels
            out_ref[:chunks, rows + LANES :] = nodes
            if chunks < classes - node_count:
                out_ref[chunks : classes - node_count, rows : rows + LANES] = jnp.zeros(
                    (classes - node_count - chunks, LANES), jnp.float32
                )
            out_ref[classes - node_count : classes, rows : rows + LANES] = sums
            out_ref[chunks:classes, rows + LANES :] = jnp.zeros(
                (classes - chunks, LANES), jnp.float32
            )


def gradients(prob, label):
    class_iota = lax.broadcasted_iota(jnp.int32, prob.shape, 0).astype(jnp.float32)
    target = jnp.where(class_iota == label, 1.0, 0.0)
    return jnp.concatenate([prob - target, prob * (1.0 - prob)], axis=0)


def masked_gradients(info, rows, node_count):
    prob, label, node = read_info(info, rows)
    grad_hess = gradients(prob, label)
    return jnp.concatenate(
        [jnp.where(node == float(n), grad_hess, 0.0).astype(jnp.bfloat16) for n in range(node_count)],
        axis=0,
    )


def one_hot(codes):
    feats, rows = codes.shape
    bin_iota = lax.broadcasted_iota(jnp.int32, (BINS, rows), 0).astype(codes.dtype)
    return jnp.concatenate(
        [
            jnp.where(codes[f : f + 1, :] == bin_iota, 1.0, 0.0).astype(jnp.bfloat16)
            for f in range(feats)
        ],
        axis=0,
    )


def write_gains(hist_ref, gain_ref, classes, node_count):
    masks = threshold_masks()
    ones = jnp.where(
        lax.broadcasted_iota(jnp.int32, (2 * BINS, 4 * BINS), 0) < BINS, 1.0, 0.0
    ).astype(jnp.bfloat16)

    def times(parts, right):
        return sum(jnp.dot(part, right, preferred_element_type=jnp.float32) for part in parts)

    total = times(three_parts(hist_ref[:, : 2 * BINS]), ones)
    for pair in range(gain_ref.shape[1] // 2):
        span = slice(pair * 2 * BINS, (pair + 1) * 2 * BINS)
        left = times(three_parts(hist_ref[:, span]), masks)
        right = total - left
        for n in range(node_count):
            grads = slice(n * 2 * classes, n * 2 * classes + classes)
            hesss = slice(n * 2 * classes + classes, (n + 1) * 2 * classes)
            score = (
                left[grads] * left[grads] / (left[hesss] + reg_lambda)
                + right[grads] * right[grads] / (right[hesss] + reg_lambda)
            )
            parent = total[grads] * total[grads] / (total[hesss] + reg_lambda)
            gain = (
                jnp.sum(score, axis=0, keepdims=True) - jnp.sum(parent, axis=0, keepdims=True)
            ) / (2.0 * classes)
            gain_ref[n, 2 * pair : 2 * pair + 1, :] = gain[:, : 2 * BINS]
            gain_ref[n, 2 * pair + 1 : 2 * pair + 2, :] = gain[:, 2 * BINS :]


def add_kernel(classes, node_count, own, plan, place_ref, *refs):
    outs = len(plan[0][2])
    arrays = 1 + max(max(c, i) for c, i, _ in plan)
    out_refs = refs[-outs:]
    held_refs = refs[arrays:-outs]
    pairs = 2 * classes * node_count
    for s, (codes_at, info_at, firsts) in enumerate(plan):
        codes_ref, info_ref = refs[codes_at], refs[info_at]
        rows = info_ref.shape[1] - 2 * LANES
        if len(codes_ref.shape) == 3:
            codes_ref = codes_ref.at[place_ref[0, s]]
        info = info_ref[:classes, :]
        masked = masked_gradients(info, rows, node_count)
        sums = info[classes - node_count :, rows : rows + LANES]
        for i, first in enumerate(firsts):
            out_ref = out_refs[i]
            product = lax.dot_general(
                masked,
                one_hot(codes_ref[first : first + own, :rows]),
                (((1,), (1,)), ((), ())),
                preferred_element_type=jnp.float32,
            )
            if s == 0:
                if held_refs:
                    out_ref[...] = sum(ref[...] for ref in held_refs[i::outs])
                else:
                    out_ref[...] = jnp.zeros(out_ref.shape, out_ref.dtype)
            out_ref[:pairs, :] += product
            for line in range(out_ref.shape[1] // LANES):
                here = jnp.where(place_ref[0, s] == line, 1.0, 0.0)
                band = pl.ds(pl.multiple_of(pairs + place_ref[1, s] * node_count, node_count), node_count)
                out_ref[band, line * LANES : (line + 1) * LANES] += here * sums


def add_rows(classes, node_count, own, plan, places, arrays, *held):
    shape = (2 * classes * node_count + 4 * node_count, own * BINS)
    whole = pl.BlockSpec(memory_space=pltpu.VMEM)
    outs = len(plan[0][2])
    return pl.pallas_call(
        functools.partial(add_kernel, classes, node_count, own, plan),
        in_specs=[pl.BlockSpec(memory_space=pltpu.SMEM)]
        + [whole] * (len(arrays) + len(held) * outs),
        out_specs=[whole] * outs,
        out_shape=[jax.ShapeDtypeStruct(shape, jnp.float32)] * outs,
        compiler_params=pltpu.CompilerParams(vmem_limit_bytes=32 * 1024 * 1024),
        cost_estimate=SMALL_COST,
    )(places, *arrays, *[hist for hists in held for hist in hists])


def gain_kernel(classes, node_count, *refs):
    gain_ref, hist_ref = refs[-2:]
    hist_ref[...] = sum(ref[: hist_ref.shape[0], :] for ref in refs[:-2])
    write_gains(hist_ref, gain_ref, classes, node_count)


def swap(x, axis, bit):
    size = lax.axis_size(axis)
    return lax.ppermute(x, axis, [(i, i ^ bit) for i in range(size)])


def sum_over(x, axis):
    bit = 1
    while bit < lax.axis_size(axis):
        x = x + swap(x, axis, bit)
        bit *= 2
    return x


def prepare(blocks, starts, logits_t, labels, node_ids, bin_codes, splits):
    classes, rows_dev = logits_t.shape
    feats_dev = bin_codes.shape[1]
    own = 8
    whole = pl.BlockSpec(memory_space=pltpu.VMEM)
    scalars = pl.BlockSpec(memory_space=pltpu.SMEM)
    shapes = []
    for with_info, pieces in blocks:
        codes = len(pieces) * own
        if with_info:
            shape = (classes + codes, rows_dev + 2 * LANES)
            shapes.append(jax.ShapeDtypeStruct(shape, jnp.float32))
        else:
            shapes.append(jax.ShapeDtypeStruct((codes, rows_dev), jnp.int32))
    return pl.pallas_call(
        functools.partial(prep_kernel, own, blocks),
        in_specs=[scalars, scalars] + [whole] * 4,
        out_specs=[whole] * (len(blocks) + 1),
        out_shape=shapes + [jax.ShapeDtypeStruct((1, rows_dev), jnp.float32)],
        scratch_shapes=[pltpu.VMEM((feats_dev, rows_dev), jnp.int32)],
        compiler_params=pltpu.CompilerParams(vmem_limit_bytes=20 * 1024 * 1024),
        cost_estimate=SMALL_COST,
    )(
        starts,
        splits,
        logits_t,
        labels.reshape(-1, LANES),
        node_ids.reshape(-1, LANES),
        bin_codes,
    )


def child_sums(info, rows_dev, classes, node_count):
    return info[classes - node_count : classes, rows_dev : rows_dev + LANES]


def finish(logits_t, node_ids, side_count, sums, node_count):
    classes = logits_t.shape[0]
    width = 2 * classes
    side_sums = jnp.concatenate([sums[:, :width], sums[:, width:]], axis=0)
    side_sums = side_sums.reshape(node_count, 2, width)
    leaves = -side_sums[..., :classes] / (side_sums[..., classes:] + reg_lambda)
    row_side = (side_count > 0.5).astype(jnp.int32)
    slot_iota = jnp.arange(2 * node_count, dtype=jnp.int32)
    slot_hot = (node_ids[None, :] * 2 + row_side) == slot_iota[:, None]
    update = jnp.dot(
        leaves.reshape(2 * node_count, classes).T,
        slot_hot.astype(jnp.float32),
        precision=lax.Precision.HIGHEST,
    )
    return (logits_t + step_size * update).T, leaves


def local(logits, labels, node_ids, bin_codes, split_feature, split_bin, split_missing):
    rows_dev, classes = logits.shape
    feats_dev = bin_codes.shape[1]
    node_count = split_feature.shape[0]
    n_rows = lax.axis_size("rows")
    per_node = n_rows // node_count
    pairs_dev = feats_dev // per_node
    width = 2 * classes
    own = 8
    row_index = lax.axis_index("rows")
    feat_index = lax.axis_index("feat")
    splits = jnp.stack([split_feature - feat_index * feats_dev, split_bin, split_missing])
    logits_t = logits.T
    add = functools.partial(add_rows, classes, node_count, own)
    if feats_dev != own * n_rows or n_rows != 16:
        return by_groups(
            logits_t, labels, node_ids, bin_codes, splits, row_index, per_node, pairs_dev
        )

    starts = []
    for taker in [row_index ^ m for m in (0, 4, 8, 12)] + [z * 4 + row_index % 4 for z in range(4)]:
        takers = [taker ^ low for low in (3, 2, 1, 0)]
        starts.append(jnp.stack([t % per_node * pairs_dev + t // per_node * own for t in takers]))
    starts = jnp.stack(starts)
    blocks = (
        (True, ((0, 0), (0, 1), (0, 2), (0, 3))),
        (True, ((1, 0), (1, 1))),
        (True, ((2, 0), (2, 1))),
        (False, ((3, 0), (3, 1))),
        (False, tuple((4 + z, quarter) for z in range(4) for quarter in (2, 3))),
    )
    rows_0, rows_4, rows_8, codes_12, codes_late, flags = prepare(
        blocks, starts, logits_t, labels, node_ids, bin_codes, splits
    )

    def place(*lines):
        line = jnp.stack([row_index // 4 ^ m // 4 for m in lines])
        return jnp.stack([line, jnp.zeros_like(line) + row_index % 4])

    first, second, third, fourth = [classes + i * own for i in range(4)]
    rows_8 = swap(rows_8, "rows", 8)
    rows_4 = swap(rows_4, "rows", 4)
    codes_12 = swap(codes_12, "rows", 12)
    hist_a, hist_b, hist_c, hist_d = add(((0, 0, (first, second, third, fourth)),), place(0), [rows_0])
    hist_a, hist_b, codes_late, rows_8 = lax.optimization_barrier(
        (hist_a, hist_b, codes_late, rows_8)
    )
    lines = [[4 * z + low for z in range(4)] for low in range(4)]
    codes_late = lax.all_to_all(
        codes_late.reshape(4, 2 * own, rows_dev), "rows", 0, 0, tiled=True, axis_index_groups=lines
    )
    info_12 = swap(rows_8[:classes], "rows", 4)
    hists = add(((0, 0, (first, second)),), place(4), [rows_4], [hist_a, hist_b])
    hist_a, hist_b = add(((0, 0, (first, second)),), place(8), [rows_8], hists)
    (to_core,) = add(((0, 1, (0,)),), place(12), [codes_12, info_12], [hist_a])
    from_core = swap(to_core, "rows", 1)
    (to_plane,) = add(((0, 1, (own,)),), place(12), [codes_12, info_12], [hist_b], [from_core])
    to_plane, codes_late = lax.optimization_barrier((to_plane, codes_late))
    from_plane = swap(to_plane, "rows", 2)
    late = [codes_late, rows_4, rows_8, info_12]
    (to_core,) = add(tuple((0, i, (0,)) for i in (1, 2, 3)), place(4, 8, 12), late, [hist_c])
    from_core = swap(to_core, "rows", 1)
    (kept,) = add(tuple((0, i, (own,)) for i in (1, 2, 3)), place(4, 8, 12), late, [hist_d])

    pairs = node_count * width
    parts = from_core[pairs:] + from_plane[pairs:] + kept[pairs:]
    sums = jnp.sum(parts.reshape(4, node_count, -1, LANES), axis=(0, 2))
    children = jnp.concatenate([sums, flags.reshape(-1, LANES)], axis=0)
    children = sum_over(children, "feat")
    side_count = children[node_count:].reshape(1, rows_dev)
    new_logits, leaves = finish(logits_t, node_ids, side_count, children[:node_count], node_count)

    gains = pl.pallas_call(
        functools.partial(gain_kernel, classes, node_count),
        in_specs=[pl.BlockSpec(memory_space=pltpu.VMEM)] * 3,
        out_specs=pl.BlockSpec(memory_space=pltpu.VMEM),
        out_shape=jax.ShapeDtypeStruct((node_count, own, 2 * BINS), jnp.float32),
        scratch_shapes=[pltpu.VMEM((pairs, own * BINS), jnp.float32)],
        compiler_params=pltpu.CompilerParams(vmem_limit_bytes=16 * 1024 * 1024),
        cost_estimate=SMALL_COST,
    )(from_core, from_plane, kept)
    halves = [[h + n * per_node for n in range(node_count)] for h in range(per_node)]
    gain_rows = lax.all_to_all(gains, "rows", 0, 0, tiled=True, axis_index_groups=halves)
    return (new_logits, gain_rows.reshape(1, pairs_dev, 2 * BINS), leaves)


def by_groups(logits_t, labels, node_ids, bin_codes, splits, row_index, per_node, pairs_dev):
    classes, rows_dev = logits_t.shape
    feats_dev = bin_codes.shape[1]
    node_count = splits.shape[1]
    n_rows = lax.axis_size("rows")
    width = 2 * classes
    own = 8
    group = feats_dev // own
    group_count = n_rows // group
    starts = jnp.arange(group, dtype=jnp.int32)[:, None] * own
    blocks = tuple((True, ((r, 0),)) for r in range(group))
    *rows_out, flags = prepare(blocks, starts, logits_t, labels, node_ids, bin_codes, splits)
    members = [[g * group + r for r in range(group)] for g in range(group_count)]
    rows_in = lax.all_to_all(
        jnp.stack(rows_out), "rows", 0, 0, tiled=True, axis_index_groups=members
    )
    hists = []
    for r in range(group):
        held = [hists] if hists else []
        nowhere = jnp.full((2, 1), -1, jnp.int32) * jnp.array([[1], [0]], jnp.int32)
        hists = add_rows(
            classes, node_count, own, ((0, 0, (classes,)),), nowhere, [rows_in[r]], *held
        )
    sums = lax.psum(child_sums(rows_out[0], rows_dev, classes, node_count), ("rows", "feat"))
    side_count = lax.psum(flags, "feat")
    new_logits, leaves = finish(logits_t, node_ids, side_count, sums, node_count)

    cuts = own // pairs_dev
    hist = hists[0][: node_count * width]
    hist = hist.reshape(node_count, width, cuts, pairs_dev, BINS).transpose(0, 2, 3, 4, 1)
    peers = [[g * group + r for g in range(group_count)] for r in range(group)]
    owned = lax.psum_scatter(
        hist.reshape(group_count, pairs_dev, BINS, width),
        "rows",
        scatter_dimension=0,
        axis_index_groups=peers,
    )
    bin_iota = jnp.arange(BINS, dtype=jnp.int32)
    lower_mask = (
        (bin_iota[:, None] < bin_iota[None, :]) & (bin_iota[:, None] < BINS - 1)
    ).astype(jnp.float32)
    left_base = jnp.einsum("pbc,bt->ptc", owned, lower_mask, precision=lax.Precision.HIGHEST)
    node_total = jnp.sum(owned, axis=1, keepdims=True)
    left_miss = left_base + owned[:, BINS - 1 :, :]
    parent_score = split_score(node_total, classes)
    gain_left = (
        split_score(left_miss, classes)
        + split_score(node_total - left_miss, classes)
        - parent_score
    )
    gain_right = (
        split_score(left_base, classes)
        + split_score(node_total - left_base, classes)
        - parent_score
    )
    gain = jnp.concatenate([gain_left, gain_right], axis=1) / (2.0 * classes)
    moves = [
        (n * per_node + cut * group + r, n * per_node + r * cuts + cut)
        for n in range(node_count)
        for cut in range(cuts)
        for r in range(group)
    ]
    gain_rows = lax.ppermute(gain, "rows", moves)
    return (new_logits, gain_rows[None], leaves)


def solution(mesh):
    return jax.shard_map(
        local,
        mesh=mesh,
        in_specs=(P("rows", None), P("rows"), P("rows"), P("rows", "feat"), P(), P(), P()),
        out_specs=(P("rows", None), P("rows", "feat", None), P()),
        check_vma=False,
    )
```

```python
import functools

import jax
import jax.numpy as jnp
from jax import lax
from jax.experimental import pallas as pl
from jax.experimental.pallas import tpu as pltpu
from jax.sharding import PartitionSpec as P

BINS = 64
LANES = 128
SMALL_COST = pl.CostEstimate(flops=1000000, bytes_accessed=1000000, transcendentals=0)


reg_lambda = 1.0
step_size = 0.3


def split_score(sums, classes):
    grad_part = sums[..., :classes]
    hess_part = sums[..., classes:]
    return jnp.sum(grad_part * grad_part / (hess_part + reg_lambda), axis=-1)


def three_parts(x):
    first = x.astype(jnp.bfloat16)
    rest = x - first.astype(jnp.float32)
    second = rest.astype(jnp.bfloat16)
    third = (rest - second.astype(jnp.float32)).astype(jnp.bfloat16)
    return first, second, third


def threshold_masks():
    row = lax.broadcasted_iota(jnp.int32, (2 * BINS, 4 * BINS), 0)
    col = lax.broadcasted_iota(jnp.int32, (2 * BINS, 4 * BINS), 1)
    bin_of = row % BINS
    threshold = col % BINS
    first_dir = (col // BINS) % 2 == 0
    below = (bin_of < threshold) & (bin_of < BINS - 1)
    missing = (bin_of == BINS - 1) & first_dir
    same = row // BINS == col // (2 * BINS)
    return jnp.where((below | missing) & same, 1.0, 0.0).astype(jnp.bfloat16)


def half_width(rows):
    return rows // 2 + 2 * LANES


def read_info(halves, rows):
    half = rows // 2
    chunks = half // LANES
    prob = jnp.concatenate([info[:, :half] for info in halves], axis=1)
    label, node = (
        jnp.concatenate(
            [info[i : i + 1, low : low + LANES] for info in halves for i in range(chunks)], axis=1
        )
        for low in (half, half + LANES)
    )
    return prob, label, node


def child_sums(info, rows, node_count):
    return info[-node_count:, rows // 2 : rows // 2 + LANES]


def prep_kernel(
    own, blocks, starts_ref, split_ref, logits_ref, labels_ref, nodes_ref, codes_ref, *refs
):
    info_ref, half_ref, flag_ref = refs[:3]
    outs, turned = refs[3:-1], refs[-1]
    classes, rows = logits_ref.shape
    half, width = rows // 2, half_width(rows)
    chunks = half // LANES
    turned[...] = codes_ref[...].T
    for (with_info, pieces), out_ref in zip(blocks, outs):
        base = classes if with_info else 0
        for i, (taker, quarter) in enumerate(pieces):
            start = pl.multiple_of(starts_ref[taker, quarter], own)
            low = base + i * own
            out_ref[low : low + own, :rows] = turned[pl.ds(start, own), :].astype(out_ref.dtype)
            if with_info:
                out_ref[low : low + own, rows:] = jnp.zeros((own, 2 * width - rows), out_ref.dtype)
    expo_vals = jnp.exp(logits_ref[...])
    prob = expo_vals / jnp.sum(expo_vals, axis=0, keepdims=True)
    labels = labels_ref[...].astype(jnp.float32)
    nodes = nodes_ref[...].astype(jnp.float32)
    label = jnp.concatenate([labels[i : i + 1] for i in range(2 * chunks)], axis=1)
    node = jnp.concatenate([nodes[i : i + 1] for i in range(2 * chunks)], axis=1)

    feats = turned.shape[0]
    node_count = split_ref.shape[1]
    side = jnp.zeros((1, rows), jnp.float32)
    for n in range(node_count):
        col = split_ref[0, n]
        held = (col >= 0) & (col < feats)
        code = turned[pl.ds(jnp.clip(col, 0, feats - 1), 1), :]
        threshold = jnp.where(held, split_ref[1, n], -1)
        missing = jnp.where(held & (split_ref[2, n] == 1), BINS - 1, -1)
        left = (code < threshold) | (code == missing)
        value = jnp.where(left, 1.0, jnp.where(held, 2.0, 0.0))
        side = jnp.where(node == float(n), value, side)
    flag_ref[...] = jnp.where(side == 2.0, 1.0, 0.0)
    hot = jnp.concatenate(
        [
            jnp.where((node == float(slot // 2)) & (side == float(slot % 2 + 1)), 1.0, 0.0)
            for slot in range(2 * node_count)
        ],
        axis=0,
    ).astype(jnp.bfloat16)
    sums = lax.dot_general(
        hot,
        gradients(prob, label).astype(jnp.bfloat16),
        (((1,), (1,)), ((), ())),
        preferred_element_type=jnp.float32,
    )
    sums = jnp.concatenate([sums[:node_count], sums[node_count:]], axis=1)
    pad = jnp.zeros((classes - chunks - node_count, LANES), jnp.float32)
    long_pad = jnp.zeros((classes - chunks, LANES), jnp.float32)
    for h in range(2):
        some = slice(h * chunks, (h + 1) * chunks)
        info_ref[:, h * width : h * width + half] = prob[:, h * half : (h + 1) * half]
        info_ref[:, h * width + half : h * width + half + LANES] = jnp.concatenate(
            [labels[some], pad, sums], axis=0
        )
        info_ref[:, h * width + half + LANES : (h + 1) * width] = jnp.concatenate(
            [nodes[some], long_pad], axis=0
        )
    half_ref[...] = jnp.where(split_ref[3, 0] == 0, info_ref[:, :width], info_ref[:, width:])
    for (with_info, _), out_ref in zip(blocks, outs):
        if with_info:
            out_ref[:classes, :] = info_ref[...]


def gradients(prob, label):
    class_iota = lax.broadcasted_iota(jnp.int32, prob.shape, 0).astype(jnp.float32)
    target = jnp.where(class_iota == label, 1.0, 0.0)
    return jnp.concatenate([prob - target, prob * (1.0 - prob)], axis=0)


def masked_gradients(halves, rows, node_count):
    prob, label, node = read_info(halves, rows)
    grad_hess = gradients(prob, label)
    return jnp.concatenate(
        [jnp.where(node == float(n), grad_hess, 0.0).astype(jnp.bfloat16) for n in range(node_count)],
        axis=0,
    )


def one_hot(codes):
    feats, rows = codes.shape
    bin_iota = lax.broadcasted_iota(jnp.int32, (BINS, rows), 0).astype(codes.dtype)
    return jnp.concatenate(
        [
            jnp.where(codes[f : f + 1, :] == bin_iota, 1.0, 0.0).astype(jnp.bfloat16)
            for f in range(feats)
        ],
        axis=0,
    )


def write_gains(hist_ref, gain_ref, classes, node_count):
    masks = threshold_masks()
    ones = jnp.where(
        lax.broadcasted_iota(jnp.int32, (2 * BINS, 4 * BINS), 0) < BINS, 1.0, 0.0
    ).astype(jnp.bfloat16)

    def times(parts, right):
        return sum(jnp.dot(part, right, preferred_element_type=jnp.float32) for part in parts)

    total = times(three_parts(hist_ref[:, : 2 * BINS]), ones)
    for pair in range(gain_ref.shape[1] // 2):
        span = slice(pair * 2 * BINS, (pair + 1) * 2 * BINS)
        left = times(three_parts(hist_ref[:, span]), masks)
        right = total - left
        for n in range(node_count):
            grads = slice(n * 2 * classes, n * 2 * classes + classes)
            hesss = slice(n * 2 * classes + classes, (n + 1) * 2 * classes)
            score = (
                left[grads] * left[grads] / (left[hesss] + reg_lambda)
                + right[grads] * right[grads] / (right[hesss] + reg_lambda)
            )
            parent = total[grads] * total[grads] / (total[hesss] + reg_lambda)
            gain = (
                jnp.sum(score, axis=0, keepdims=True) - jnp.sum(parent, axis=0, keepdims=True)
            ) / (2.0 * classes)
            gain_ref[n, 2 * pair : 2 * pair + 1, :] = gain[:, : 2 * BINS]
            gain_ref[n, 2 * pair + 1 : 2 * pair + 2, :] = gain[:, 2 * BINS :]


def add_kernel(classes, node_count, own, plan, place_ref, *refs):
    outs = len(plan[0][2])
    arrays = 1 + max(max((c,) + i) for c, i, _ in plan)
    out_refs = refs[-outs:]
    held_refs = refs[arrays:-outs]
    pairs = 2 * classes * node_count
    for s, (codes_at, info_at, firsts) in enumerate(plan):
        codes_ref = refs[codes_at]
        if len(codes_ref.shape) == 3:
            codes_ref = codes_ref.at[place_ref[0, s]]
        if len(info_at) == 1:
            width = refs[info_at[0]].shape[1] // 2
            low, high = (refs[info_at[0]][:classes, h * width : (h + 1) * width] for h in range(2))
            sums_from = low
        else:
            width = refs[info_at[0]].shape[1]
            near, far = (refs[i][...] for i in info_at)
            low = jnp.where(place_ref[2, s] == 0, near, far)
            high = jnp.where(place_ref[2, s] == 0, far, near)
            sums_from = near
        rows = 2 * (width - 2 * LANES)
        masked = masked_gradients((low, high), rows, node_count)
        sums = child_sums(sums_from, rows, node_count)
        for i, first in enumerate(firsts):
            out_ref = out_refs[i]
            product = lax.dot_general(
                masked,
                one_hot(codes_ref[first : first + own, :rows]),
                (((1,), (1,)), ((), ())),
                preferred_element_type=jnp.float32,
            )
            if s == 0:
                if held_refs:
                    out_ref[...] = sum(ref[...] for ref in held_refs[i::outs])
                else:
                    out_ref[...] = jnp.zeros(out_ref.shape, out_ref.dtype)
            out_ref[:pairs, :] += product
            for line in range(out_ref.shape[1] // LANES):
                here = jnp.where(place_ref[0, s] == line, 1.0, 0.0)
                band = pl.ds(pl.multiple_of(pairs + place_ref[1, s] * node_count, node_count), node_count)
                out_ref[band, line * LANES : (line + 1) * LANES] += here * sums


def add_rows(classes, node_count, own, plan, places, arrays, *held):
    shape = (2 * classes * node_count + 4 * node_count, own * BINS)
    whole = pl.BlockSpec(memory_space=pltpu.VMEM)
    outs = len(plan[0][2])
    return pl.pallas_call(
        functools.partial(add_kernel, classes, node_count, own, plan),
        in_specs=[pl.BlockSpec(memory_space=pltpu.SMEM)]
        + [whole] * (len(arrays) + len(held) * outs),
        out_specs=[whole] * outs,
        out_shape=[jax.ShapeDtypeStruct(shape, jnp.float32)] * outs,
        compiler_params=pltpu.CompilerParams(vmem_limit_bytes=20 * 1024 * 1024),
        cost_estimate=SMALL_COST,
    )(places, *arrays, *[hist for hists in held for hist in hists])


def gain_kernel(classes, node_count, *refs):
    gain_ref, hist_ref = refs[-2:]
    hist_ref[...] = sum(ref[: hist_ref.shape[0], :] for ref in refs[:-2])
    write_gains(hist_ref, gain_ref, classes, node_count)


def swap(x, axis, bit):
    size = lax.axis_size(axis)
    return lax.ppermute(x, axis, [(i, i ^ bit) for i in range(size)])


def sum_over(x, axis):
    bit = 1
    while bit < lax.axis_size(axis):
        x = x + swap(x, axis, bit)
        bit *= 2
    return x


def prepare(blocks, starts, logits_t, labels, node_ids, bin_codes, splits):
    classes, rows_dev = logits_t.shape
    feats_dev = bin_codes.shape[1]
    own = 8
    whole = pl.BlockSpec(memory_space=pltpu.VMEM)
    scalars = pl.BlockSpec(memory_space=pltpu.SMEM)
    width = half_width(rows_dev)
    shapes = [
        jax.ShapeDtypeStruct((classes, 2 * width), jnp.float32),
        jax.ShapeDtypeStruct((classes, width), jnp.float32),
        jax.ShapeDtypeStruct((1, rows_dev), jnp.float32),
    ]
    for with_info, pieces in blocks:
        codes = len(pieces) * own
        if with_info:
            shapes.append(jax.ShapeDtypeStruct((classes + codes, 2 * width), jnp.float32))
        else:
            shapes.append(jax.ShapeDtypeStruct((codes, rows_dev), jnp.int32))
    return pl.pallas_call(
        functools.partial(prep_kernel, own, blocks),
        in_specs=[scalars, scalars] + [whole] * 4,
        out_specs=[whole] * len(shapes),
        out_shape=shapes,
        scratch_shapes=[pltpu.VMEM((feats_dev, rows_dev), jnp.int32)],
        compiler_params=pltpu.CompilerParams(vmem_limit_bytes=20 * 1024 * 1024),
        cost_estimate=SMALL_COST,
    )(
        starts,
        splits,
        logits_t,
        labels.reshape(-1, LANES),
        node_ids.reshape(-1, LANES),
        bin_codes,
    )


def finish(logits_t, node_ids, side_count, sums, node_count):
    classes = logits_t.shape[0]
    width = 2 * classes
    side_sums = jnp.concatenate([sums[:, :width], sums[:, width:]], axis=0)
    side_sums = side_sums.reshape(node_count, 2, width)
    leaves = -side_sums[..., :classes] / (side_sums[..., classes:] + reg_lambda)
    row_side = (side_count > 0.5).astype(jnp.int32)
    slot_iota = jnp.arange(2 * node_count, dtype=jnp.int32)
    slot_hot = (node_ids[None, :] * 2 + row_side) == slot_iota[:, None]
    update = jnp.dot(
        leaves.reshape(2 * node_count, classes).T,
        slot_hot.astype(jnp.float32),
        precision=lax.Precision.HIGHEST,
    )
    return (logits_t + step_size * update).T, leaves


def local(logits, labels, node_ids, bin_codes, split_feature, split_bin, split_missing):
    rows_dev, classes = logits.shape
    feats_dev = bin_codes.shape[1]
    node_count = split_feature.shape[0]
    n_rows = lax.axis_size("rows")
    per_node = n_rows // node_count
    pairs_dev = feats_dev // per_node
    width = 2 * classes
    own = 8
    row_index = lax.axis_index("rows")
    feat_index = lax.axis_index("feat")
    splits = jnp.stack(
        [
            split_feature - feat_index * feats_dev,
            split_bin,
            split_missing,
            jnp.zeros_like(split_bin) + feat_index,
        ]
    )
    logits_t = logits.T
    add = functools.partial(add_rows, classes, node_count, own)
    if feats_dev != own * n_rows or n_rows != 16 or lax.axis_size("feat") != 2:
        return by_groups(
            logits_t, labels, node_ids, bin_codes, splits, row_index, per_node, pairs_dev
        )

    starts = []
    for taker in [row_index ^ m for m in (0, 4, 8, 12)] + [z * 4 + row_index % 4 for z in range(4)]:
        takers = [taker ^ low for low in (3, 2, 1, 0)]
        starts.append(jnp.stack([t % per_node * pairs_dev + t // per_node * own for t in takers]))
    starts = jnp.stack(starts)
    blocks = (
        (False, ((0, 0), (0, 1), (0, 2), (0, 3))),
        (True, ((1, 0), (1, 1))),
        (False, ((2, 0), (2, 1))),
        (False, ((3, 0), (3, 1))),
        (False, tuple((4 + z, quarter) for z in range(4) for quarter in (2, 3))),
    )
    info, half, flags, codes_0, rows_4, codes_8, codes_12, codes_late = prepare(
        blocks, starts, logits_t, labels, node_ids, bin_codes, splits
    )

    def place(*lines):
        line = jnp.stack([row_index // 4 ^ m // 4 for m in lines])
        return jnp.stack([line, row_index % 4 + 0 * line, feat_index + 0 * line])

    near_8 = swap(half, "rows", 8)
    rows_4 = swap(rows_4, "rows", 4)
    codes_8 = swap(codes_8, "rows", 8)
    codes_12 = swap(codes_12, "rows", 12)
    near_12 = swap(near_8, "rows", 4)
    far_8 = swap(near_8, "feat", 1)
    far_12 = swap(near_12, "feat", 1)
    hist_a, hist_b, hist_c, hist_d = add(
        ((0, (1,), (0, own, 2 * own, 3 * own)),), place(0), [codes_0, info]
    )
    near_8, codes_late = lax.optimization_barrier((near_8, codes_late))
    lines = [[4 * z + low for z in range(4)] for low in range(4)]
    codes_late = lax.all_to_all(
        codes_late.reshape(4, 2 * own, rows_dev), "rows", 0, 0, tiled=True, axis_index_groups=lines
    )
    hists = add(((0, (0,), (classes, classes + own)),), place(4), [rows_4], [hist_a, hist_b])
    hist_a, hist_b = add(((0, (1, 2), (0, own)),), place(8), [codes_8, near_8, far_8], hists)
    (to_core,) = add(((0, (1, 2), (0,)),), place(12), [codes_12, near_12, far_12], [hist_a])
    from_core = swap(to_core, "rows", 1)
    (to_plane,) = add(
        ((0, (1, 2), (own,)),), place(12), [codes_12, near_12, far_12], [hist_b], [from_core]
    )
    to_plane, codes_late = lax.optimization_barrier((to_plane, codes_late))
    from_plane = swap(to_plane, "rows", 2)
    late = [codes_late, rows_4, near_8, far_8, near_12, far_12]
    to_core, kept = add(
        tuple((0, i, (0, own)) for i in ((1,), (2, 3), (4, 5))), place(4, 8, 12), late, [hist_c, hist_d]
    )
    middle = to_core.shape[0] // 2
    from_core = [swap(part, "rows", 1) for part in (to_core[:middle], to_core[middle:])]
    from_core = jnp.concatenate(from_core, axis=0)

    pairs = node_count * width
    gains = pl.pallas_call(
        functools.partial(gain_kernel, classes, node_count),
        in_specs=[pl.BlockSpec(memory_space=pltpu.VMEM)] * 3,
        out_specs=pl.BlockSpec(memory_space=pltpu.VMEM),
        out_shape=jax.ShapeDtypeStruct((node_count, own, 2 * BINS), jnp.float32),
        scratch_shapes=[pltpu.VMEM((pairs, own * BINS), jnp.float32)],
        compiler_params=pltpu.CompilerParams(vmem_limit_bytes=16 * 1024 * 1024),
        cost_estimate=SMALL_COST,
    )(from_core, from_plane, kept)
    gains, from_plane = lax.optimization_barrier((gains, from_plane))
    parts = from_core[pairs:] + from_plane[pairs:] + kept[pairs:]
    sums = jnp.sum(parts.reshape(4, node_count, -1, LANES), axis=(0, 2))
    children = jnp.concatenate([sums, flags.reshape(-1, LANES)], axis=0)
    children = sum_over(children, "feat")
    side_count = children[node_count:].reshape(1, rows_dev)
    new_logits, leaves = finish(logits_t, node_ids, side_count, children[:node_count], node_count)

    halves = [[h + n * per_node for n in range(node_count)] for h in range(per_node)]
    gain_rows = lax.all_to_all(gains, "rows", 0, 0, tiled=True, axis_index_groups=halves)
    return (new_logits, gain_rows.reshape(1, pairs_dev, 2 * BINS), leaves)


def by_groups(logits_t, labels, node_ids, bin_codes, splits, row_index, per_node, pairs_dev):
    classes, rows_dev = logits_t.shape
    feats_dev = bin_codes.shape[1]
    node_count = splits.shape[1]
    n_rows = lax.axis_size("rows")
    width = 2 * classes
    own = 8
    group = feats_dev // own
    group_count = n_rows // group
    starts = jnp.arange(group, dtype=jnp.int32)[:, None] * own
    blocks = tuple((True, ((r, 0),)) for r in range(group))
    info, _, flags, *rows_out = prepare(blocks, starts, logits_t, labels, node_ids, bin_codes, splits)
    members = [[g * group + r for r in range(group)] for g in range(group_count)]
    rows_in = lax.all_to_all(
        jnp.stack(rows_out), "rows", 0, 0, tiled=True, axis_index_groups=members
    )
    hists = []
    for r in range(group):
        held = [hists] if hists else []
        nowhere = jnp.full((2, 1), -1, jnp.int32) * jnp.array([[1], [0]], jnp.int32)
        hists = add_rows(
            classes, node_count, own, ((0, (0,), (classes,)),), nowhere, [rows_in[r]], *held
        )
    sums = lax.psum(child_sums(info[:, : half_width(rows_dev)], rows_dev, node_count), ("rows", "feat"))
    side_count = lax.psum(flags, "feat")
    new_logits, leaves = finish(logits_t, node_ids, side_count, sums, node_count)

    cuts = own // pairs_dev
    hist = hists[0][: node_count * width]
    hist = hist.reshape(node_count, width, cuts, pairs_dev, BINS).transpose(0, 2, 3, 4, 1)
    peers = [[g * group + r for g in range(group_count)] for r in range(group)]
    owned = lax.psum_scatter(
        hist.reshape(group_count, pairs_dev, BINS, width),
        "rows",
        scatter_dimension=0,
        axis_index_groups=peers,
    )
    bin_iota = jnp.arange(BINS, dtype=jnp.int32)
    lower_mask = (
        (bin_iota[:, None] < bin_iota[None, :]) & (bin_iota[:, None] < BINS - 1)
    ).astype(jnp.float32)
    left_base = jnp.einsum("pbc,bt->ptc", owned, lower_mask, precision=lax.Precision.HIGHEST)
    node_total = jnp.sum(owned, axis=1, keepdims=True)
    left_miss = left_base + owned[:, BINS - 1 :, :]
    parent_score = split_score(node_total, classes)
    gain_left = (
        split_score(left_miss, classes)
        + split_score(node_total - left_miss, classes)
        - parent_score
    )
    gain_right = (
        split_score(left_base, classes)
        + split_score(node_total - left_base, classes)
        - parent_score
    )
    gain = jnp.concatenate([gain_left, gain_right], axis=1) / (2.0 * classes)
    moves = [
        (n * per_node + cut * group + r, n * per_node + r * cuts + cut)
        for n in range(node_count)
        for cut in range(cuts)
        for r in range(group)
    ]
    gain_rows = lax.ppermute(gain, "rows", moves)
    return (new_logits, gain_rows[None], leaves)


def solution(mesh):
    return jax.shard_map(
        local,
        mesh=mesh,
        in_specs=(P("rows", None), P("rows"), P("rows"), P("rows", "feat"), P(), P(), P()),
        out_specs=(P("rows", None), P("rows", "feat", None), P()),
        check_vma=False,
    )
```

```python
import functools

import jax
import jax.numpy as jnp
from jax import lax
from jax.experimental import pallas as pl
from jax.experimental.pallas import tpu as pltpu
from jax.sharding import PartitionSpec as P

BINS = 64
LANES = 128
VMEM_BYTES = 12 * 1024 * 1024
SMALL_COST = pl.CostEstimate(flops=1000000, bytes_accessed=1000000, transcendentals=0)


reg_lambda = 1.0
step_size = 0.3


def split_score(sums, classes):
    grad_part = sums[..., :classes]
    hess_part = sums[..., classes:]
    return jnp.sum(grad_part * grad_part / (hess_part + reg_lambda), axis=-1)


def three_parts(x):
    first = x.astype(jnp.bfloat16)
    rest = x - first.astype(jnp.float32)
    second = rest.astype(jnp.bfloat16)
    third = (rest - second.astype(jnp.float32)).astype(jnp.bfloat16)
    return first, second, third


def threshold_masks():
    row = lax.broadcasted_iota(jnp.int32, (2 * BINS, 4 * BINS), 0)
    col = lax.broadcasted_iota(jnp.int32, (2 * BINS, 4 * BINS), 1)
    bin_of = row % BINS
    threshold = col % BINS
    first_dir = (col // BINS) % 2 == 0
    below = (bin_of < threshold) & (bin_of < BINS - 1)
    missing = (bin_of == BINS - 1) & first_dir
    same = row // BINS == col // (2 * BINS)
    return jnp.where((below | missing) & same, 1.0, 0.0).astype(jnp.bfloat16)


def half_width(rows):
    return rows // 2 + 2 * LANES


def read_info(halves, rows):
    half = rows // 2
    chunks = half // LANES
    prob = jnp.concatenate([info[:, :half] for info in halves], axis=1)
    label, node = (
        jnp.concatenate(
            [info[i : i + 1, low : low + LANES] for info in halves for i in range(chunks)], axis=1
        )
        for low in (half, half + LANES)
    )
    return prob, label, node


def child_sums(info, rows, node_count):
    return info[-node_count:, rows // 2 : rows // 2 + LANES]


def prep_kernel(
    own,
    blocks,
    ids_ref,
    feature_ref,
    bin_ref,
    missing_ref,
    logits_ref,
    labels_ref,
    nodes_ref,
    codes_ref,
    *refs,
):
    info_ref, half_ref, flag_ref = refs[:3]
    outs, turned = refs[3:-1], refs[-1]
    classes, rows = logits_ref.shape
    half, width = rows // 2, half_width(rows)
    chunks = half // LANES
    turned[...] = codes_ref[...].T
    for (infos, pieces), out_ref in zip(blocks, outs):
        for i, start_of in enumerate(pieces):
            start = pl.multiple_of(start_of(ids_ref[0]), own)
            if infos == 0:
                out_ref[i * own : (i + 1) * own, :] = turned[pl.ds(start, own), :]
                continue
            cut = rows * infos // 2
            for h in range(2 // infos):
                low = classes + (h * len(pieces) + i) * own
                part = turned[pl.ds(start, own), h * cut : (h + 1) * cut]
                out_ref[low : low + own, :cut] = part.astype(out_ref.dtype)
                out_ref[low : low + own, cut:] = jnp.zeros((own, infos * width - cut), out_ref.dtype)
    expo_vals = jnp.exp(logits_ref[...])
    prob = expo_vals / jnp.sum(expo_vals, axis=0, keepdims=True)
    labels = labels_ref[...].astype(jnp.float32)
    nodes = nodes_ref[...].astype(jnp.float32)
    label = jnp.concatenate([labels[i : i + 1] for i in range(2 * chunks)], axis=1)
    node = jnp.concatenate([nodes[i : i + 1] for i in range(2 * chunks)], axis=1)

    feats = turned.shape[0]
    node_count = feature_ref.shape[0]
    side = jnp.zeros((1, rows), jnp.float32)
    for n in range(node_count):
        col = feature_ref[n] - ids_ref[1] * feats
        held = (col >= 0) & (col < feats)
        code = turned[pl.ds(jnp.clip(col, 0, feats - 1), 1), :]
        threshold = jnp.where(held, bin_ref[n], -1)
        missing = jnp.where(held & (missing_ref[n] == 1), BINS - 1, -1)
        left = (code < threshold) | (code == missing)
        value = jnp.where(left, 1.0, jnp.where(held, 2.0, 0.0))
        side = jnp.where(node == float(n), value, side)
    flag_ref[...] = jnp.where(side == 2.0, 1.0, 0.0)
    hot = jnp.concatenate(
        [
            jnp.where((node == float(slot // 2)) & (side == float(slot % 2 + 1)), 1.0, 0.0)
            for slot in range(2 * node_count)
        ],
        axis=0,
    ).astype(jnp.bfloat16)
    sums = lax.dot_general(
        hot,
        gradients(prob, label).astype(jnp.bfloat16),
        (((1,), (1,)), ((), ())),
        preferred_element_type=jnp.float32,
    )
    sums = jnp.concatenate([sums[:node_count], sums[node_count:]], axis=1)
    pad = jnp.zeros((classes - chunks - node_count, LANES), jnp.float32)
    long_pad = jnp.zeros((classes - chunks, LANES), jnp.float32)
    for h in range(2):
        some = slice(h * chunks, (h + 1) * chunks)
        info_ref[:, h * width : h * width + half] = prob[:, h * half : (h + 1) * half]
        info_ref[:, h * width + half : h * width + half + LANES] = jnp.concatenate(
            [labels[some], pad, sums], axis=0
        )
        info_ref[:, h * width + half + LANES : (h + 1) * width] = jnp.concatenate(
            [nodes[some], long_pad], axis=0
        )
    half_ref[...] = jnp.where(ids_ref[1] == 0, info_ref[:, :width], info_ref[:, width:])
    for (infos, _), out_ref in zip(blocks, outs):
        if infos > 0:
            out_ref[:classes, :] = half_ref[...] if infos == 1 else info_ref[...]


def gradients(prob, label):
    class_iota = lax.broadcasted_iota(jnp.int32, prob.shape, 0).astype(jnp.float32)
    target = jnp.where(class_iota == label, 1.0, 0.0)
    return jnp.concatenate([prob - target, prob * (1.0 - prob)], axis=0)


def masked_gradients(halves, rows, node_count):
    prob, label, node = read_info(halves, rows)
    grad_hess = gradients(prob, label)
    return jnp.concatenate(
        [jnp.where(node == float(n), grad_hess, 0.0).astype(jnp.bfloat16) for n in range(node_count)],
        axis=0,
    )


def one_hot(codes):
    feats, rows = codes.shape
    bin_iota = lax.broadcasted_iota(jnp.int32, (BINS, rows), 0).astype(codes.dtype)
    return jnp.concatenate(
        [
            jnp.where(codes[f : f + 1, :] == bin_iota, 1.0, 0.0).astype(jnp.bfloat16)
            for f in range(feats)
        ],
        axis=0,
    )


def write_gains(hist_ref, gain_ref, classes, node_count):
    masks = threshold_masks()
    ones = jnp.where(
        lax.broadcasted_iota(jnp.int32, (2 * BINS, 4 * BINS), 0) < BINS, 1.0, 0.0
    ).astype(jnp.bfloat16)

    def times(parts, right):
        return sum(jnp.dot(part, right, preferred_element_type=jnp.float32) for part in parts)

    total = times(three_parts(hist_ref[:, : 2 * BINS]), ones)
    for pair in range(gain_ref.shape[1] // 2):
        span = slice(pair * 2 * BINS, (pair + 1) * 2 * BINS)
        left = times(three_parts(hist_ref[:, span]), masks)
        right = total - left
        for n in range(node_count):
            grads = slice(n * 2 * classes, n * 2 * classes + classes)
            hesss = slice(n * 2 * classes + classes, (n + 1) * 2 * classes)
            score = (
                left[grads] * left[grads] / (left[hesss] + reg_lambda)
                + right[grads] * right[grads] / (right[hesss] + reg_lambda)
            )
            parent = total[grads] * total[grads] / (total[hesss] + reg_lambda)
            gain = (
                jnp.sum(score, axis=0, keepdims=True) - jnp.sum(parent, axis=0, keepdims=True)
            ) / (2.0 * classes)
            gain_ref[n, 2 * pair : 2 * pair + 1, :] = gain[:, : 2 * BINS]
            gain_ref[n, 2 * pair + 1 : 2 * pair + 2, :] = gain[:, 2 * BINS :]


def add_kernel(classes, node_count, own, plan, carry, ids_ref, *refs):
    outs = len(plan[0][3])
    arrays = 1 + max(max((c,) + i) for _, c, i, _ in plan)
    out_refs = refs[-outs:]
    held_refs = refs[arrays:-outs]
    pairs = 2 * classes * node_count
    for s, (m, codes_at, info_at, firsts) in enumerate(plan):
        codes_ref = refs[codes_at]
        line = (ids_ref[0] >> 2) ^ (m >> 2)
        if len(codes_ref.shape) == 3:
            codes_ref = codes_ref.at[line]
        if len(info_at) == 1:
            width = refs[info_at[0]].shape[1] // 2
            low, high = (refs[info_at[0]][:classes, h * width : (h + 1) * width] for h in range(2))
            sums_from = low
        else:
            width = refs[info_at[0]].shape[1]
            near, far = (refs[i][:classes, :] for i in info_at)
            low = jnp.where(ids_ref[1] == 0, near, far)
            high = jnp.where(ids_ref[1] == 0, far, near)
            sums_from = near
        rows = 2 * (width - 2 * LANES)
        masked = masked_gradients((low, high), rows, node_count)
        sums = child_sums(sums_from, rows, node_count)
        for i, first in enumerate(firsts):
            out_ref = out_refs[i]
            if codes_ref.shape[1] < rows:
                second = first + (codes_ref.shape[0] - classes) // 2
                codes = jnp.concatenate(
                    [codes_ref[low : low + own, : rows // 2] for low in (first, second)], axis=1
                )
            else:
                codes = codes_ref[first : first + own, :rows]
            product = lax.dot_general(
                masked,
                one_hot(codes),
                (((1,), (1,)), ((), ())),
                preferred_element_type=jnp.float32,
            )
            if s == 0:
                if held_refs:
                    out_ref[...] = sum(ref[...] for ref in held_refs[i::outs])
                else:
                    out_ref[...] = jnp.zeros(out_ref.shape, out_ref.dtype)
            out_ref[:pairs, :] += product
            if not carry:
                continue
            low_row = pairs + (ids_ref[0] & 3) * node_count
            band = pl.ds(pl.multiple_of(low_row, node_count), node_count)
            for i in range(out_ref.shape[1] // LANES):
                here = jnp.where(line == i, 1.0, 0.0)
                out_ref[band, i * LANES : (i + 1) * LANES] += here * sums


def add_rows(classes, node_count, own, carry, ids, plan, arrays, *held):
    shape = (2 * classes * node_count + 4 * node_count, own * BINS)
    whole = pl.BlockSpec(memory_space=pltpu.VMEM)
    outs = len(plan[0][3])
    return pl.pallas_call(
        functools.partial(add_kernel, classes, node_count, own, plan, carry),
        in_specs=[pl.BlockSpec(memory_space=pltpu.SMEM)]
        + [whole] * (len(arrays) + len(held) * outs),
        out_specs=[whole] * outs,
        out_shape=[jax.ShapeDtypeStruct(shape, jnp.float32)] * outs,
        compiler_params=pltpu.CompilerParams(vmem_limit_bytes=VMEM_BYTES),
        cost_estimate=SMALL_COST,
    )(ids, *arrays, *[hist for hists in held for hist in hists])


def gain_kernel(classes, node_count, *refs):
    gain_ref, hist_ref = refs[-2:]
    hist_ref[...] = sum(ref[: hist_ref.shape[0], :] for ref in refs[:-2])
    write_gains(hist_ref, gain_ref, classes, node_count)


def swap(x, axis, bit):
    size = lax.axis_size(axis)
    return lax.ppermute(x, axis, [(i, i ^ bit) for i in range(size)])


def sum_over(x, axis):
    bit = 1
    while bit < lax.axis_size(axis):
        x = x + swap(x, axis, bit)
        bit *= 2
    return x


def prepare(blocks, ids, splits, logits_t, labels, node_ids, bin_codes):
    classes, rows_dev = logits_t.shape
    feats_dev = bin_codes.shape[1]
    own = 8
    whole = pl.BlockSpec(memory_space=pltpu.VMEM)
    scalars = pl.BlockSpec(memory_space=pltpu.SMEM)
    width = half_width(rows_dev)
    shapes = [
        jax.ShapeDtypeStruct((classes, 2 * width), jnp.float32),
        jax.ShapeDtypeStruct((classes, width), jnp.float32),
        jax.ShapeDtypeStruct((1, rows_dev), jnp.float32),
    ]
    for infos, pieces in blocks:
        codes = len(pieces) * own
        if infos == 0:
            shapes.append(jax.ShapeDtypeStruct((codes, rows_dev), jnp.int32))
        else:
            shape = (classes + codes * 2 // infos, infos * width)
            shapes.append(jax.ShapeDtypeStruct(shape, jnp.float32))
    return pl.pallas_call(
        functools.partial(prep_kernel, own, blocks),
        in_specs=[scalars] * 4 + [whole] * 4,
        out_specs=[whole] * len(shapes),
        out_shape=shapes,
        scratch_shapes=[pltpu.VMEM((feats_dev, rows_dev), jnp.int32)],
        compiler_params=pltpu.CompilerParams(vmem_limit_bytes=VMEM_BYTES),
        cost_estimate=SMALL_COST,
    )(
        ids,
        *splits,
        logits_t,
        labels.reshape(-1, LANES),
        node_ids.reshape(-1, LANES),
        bin_codes,
    )


def finish(logits_t, node_ids, side_count, sums, node_count):
    classes = logits_t.shape[0]
    width = 2 * classes
    side_sums = jnp.concatenate([sums[:, :width], sums[:, width:]], axis=0)
    side_sums = side_sums.reshape(node_count, 2, width)
    leaves = -side_sums[..., :classes] / (side_sums[..., classes:] + reg_lambda)
    row_side = (side_count > 0.5).astype(jnp.int32)
    slot_iota = jnp.arange(2 * node_count, dtype=jnp.int32)
    slot_hot = (node_ids[None, :] * 2 + row_side) == slot_iota[:, None]
    update = jnp.dot(
        leaves.reshape(2 * node_count, classes).T,
        slot_hot.astype(jnp.float32),
        precision=lax.Precision.HIGHEST,
    )
    return (logits_t + step_size * update).T, leaves


def local(logits, labels, node_ids, bin_codes, split_feature, split_bin, split_missing):
    rows_dev, classes = logits.shape
    feats_dev = bin_codes.shape[1]
    node_count = split_feature.shape[0]
    n_rows = lax.axis_size("rows")
    per_node = n_rows // node_count
    pairs_dev = feats_dev // per_node
    width = 2 * classes
    own = 8
    row_index = lax.axis_index("rows")
    feat_index = lax.axis_index("feat")
    ids = jnp.stack([row_index, feat_index]).astype(jnp.int32)
    splits = (split_feature, split_bin, split_missing)
    logits_t = logits.T
    if feats_dev != own * n_rows or n_rows != 16 or lax.axis_size("feat") != 2:
        return by_groups(logits_t, labels, node_ids, bin_codes, splits, ids, per_node, pairs_dev)
    add = functools.partial(add_rows, classes, node_count, own, True, ids)

    def start(taker):
        return (taker & 1) * pairs_dev + (taker >> 1) * own

    def quarters(m, which):
        return tuple(lambda row, low=m ^ 3 ^ q: start(row ^ low) for q in which)

    def line_quarters(which):
        return tuple(
            lambda row, z=z, low=3 ^ q: start((z * 4 + (row & 3)) ^ low) for z in range(4) for q in which
        )

    blocks = (
        (0, quarters(0, (0, 1, 2, 3))),
        (1, quarters(4, (0, 1))),
        (0, quarters(8, (0, 1))),
        (0, quarters(12, (0, 1))),
        (0, line_quarters((2, 3))),
    )
    info, half, flags, codes_0, rows_4, codes_8, codes_12, codes_late = prepare(
        blocks, ids, splits, logits_t, labels, node_ids, bin_codes
    )

    near_8 = swap(half, "rows", 8)
    rows_4 = swap(rows_4, "rows", 4)
    codes_8 = swap(codes_8, "rows", 8)
    codes_12 = swap(codes_12, "rows", 12)
    hist_a, hist_b, hist_c, hist_d = add(
        ((0, 0, (1,), (0, own, 2 * own, 3 * own)),), [codes_0, info]
    )
    near_8, hist_a, codes_late = lax.optimization_barrier((near_8, hist_a, codes_late))
    near_12 = swap(near_8, "rows", 4)
    far_8 = swap(near_8, "feat", 1)
    far_4 = swap(rows_4[:classes], "feat", 1)
    lines = [[4 * z + low for z in range(4)] for low in range(4)]
    codes_late = lax.all_to_all(
        codes_late.reshape(4, 2 * own, rows_dev), "rows", 0, 0, tiled=True, axis_index_groups=lines
    )
    hist_a, hist_b = add(
        ((4, 0, (0, 1), (classes, classes + own)),), [rows_4, far_4], [hist_a, hist_b]
    )
    near_12, codes_8, codes_12, hist_a = lax.optimization_barrier((near_12, codes_8, codes_12, hist_a))
    far_12 = swap(near_12, "feat", 1)
    hist_a, hist_b = add(((8, 0, (1, 2), (0, own)),), [codes_8, near_8, far_8], [hist_a, hist_b])
    (to_core,) = add(((12, 0, (1, 2), (0,)),), [codes_12, near_12, far_12], [hist_a])
    from_core = swap(to_core, "rows", 1)
    (to_plane,) = add(((12, 0, (1, 2), (own,)),), [codes_12, near_12, far_12], [hist_b], [from_core])
    to_plane, codes_late = lax.optimization_barrier((to_plane, codes_late))
    from_plane = swap(to_plane, "rows", 2)
    late = [codes_late, rows_4, far_4, near_8, far_8, near_12, far_12]
    to_core, kept = add(
        tuple((m, 0, i, (0, own)) for m, i in ((4, (1, 2)), (8, (3, 4)), (12, (5, 6)))),
        late,
        [hist_c, hist_d],
    )
    middle = to_core.shape[0] // 2
    from_core = [swap(part, "rows", 1) for part in (to_core[:middle], to_core[middle:])]
    from_core = jnp.concatenate(from_core, axis=0)

    pairs = node_count * width
    gains = pl.pallas_call(
        functools.partial(gain_kernel, classes, node_count),
        in_specs=[pl.BlockSpec(memory_space=pltpu.VMEM)] * 3,
        out_specs=pl.BlockSpec(memory_space=pltpu.VMEM),
        out_shape=jax.ShapeDtypeStruct((node_count, own, 2 * BINS), jnp.float32),
        scratch_shapes=[pltpu.VMEM((pairs, own * BINS), jnp.float32)],
        compiler_params=pltpu.CompilerParams(vmem_limit_bytes=VMEM_BYTES),
        cost_estimate=SMALL_COST,
    )(from_core, from_plane, kept)
    gains, from_plane = lax.optimization_barrier((gains, from_plane))
    parts = from_core[pairs:] + from_plane[pairs:] + kept[pairs:]
    sums = jnp.sum(parts.reshape(4, node_count, -1, LANES), axis=(0, 2))
    children = jnp.concatenate([sums, flags.reshape(-1, LANES)], axis=0)
    children = sum_over(children, "feat")
    side_count = children[node_count:].reshape(1, rows_dev)
    new_logits, leaves = finish(logits_t, node_ids, side_count, children[:node_count], node_count)

    halves = [[h + n * per_node for n in range(node_count)] for h in range(per_node)]
    gain_rows = lax.all_to_all(gains, "rows", 0, 0, tiled=True, axis_index_groups=halves)
    return (new_logits, gain_rows.reshape(1, pairs_dev, 2 * BINS), leaves)


def by_groups(logits_t, labels, node_ids, bin_codes, splits, ids, per_node, pairs_dev):
    classes, rows_dev = logits_t.shape
    feats_dev = bin_codes.shape[1]
    node_count = splits[0].shape[0]
    n_rows = lax.axis_size("rows")
    width = 2 * classes
    own = 8
    group = feats_dev // own
    group_count = n_rows // group
    blocks = tuple((2, (lambda row, r=r: r * own,)) for r in range(group))
    info, _, flags, *rows_out = prepare(blocks, ids, splits, logits_t, labels, node_ids, bin_codes)
    members = [[g * group + r for r in range(group)] for g in range(group_count)]
    rows_in = lax.all_to_all(
        jnp.stack(rows_out), "rows", 0, 0, tiled=True, axis_index_groups=members
    )
    hists = []
    for r in range(group):
        held = [hists] if hists else []
        hists = add_rows(
            classes, node_count, own, False, ids, ((0, 0, (0,), (classes,)),), [rows_in[r]], *held
        )
    sums = lax.psum(child_sums(info[:, : half_width(rows_dev)], rows_dev, node_count), ("rows", "feat"))
    side_count = lax.psum(flags, "feat")
    new_logits, leaves = finish(logits_t, node_ids, side_count, sums, node_count)

    cuts = own // pairs_dev
    hist = hists[0][: node_count * width]
    hist = hist.reshape(node_count, width, cuts, pairs_dev, BINS).transpose(0, 2, 3, 4, 1)
    peers = [[g * group + r for g in range(group_count)] for r in range(group)]
    owned = lax.psum_scatter(
        hist.reshape(group_count, pairs_dev, BINS, width),
        "rows",
        scatter_dimension=0,
        axis_index_groups=peers,
    )
    bin_iota = jnp.arange(BINS, dtype=jnp.int32)
    lower_mask = (
        (bin_iota[:, None] < bin_iota[None, :]) & (bin_iota[:, None] < BINS - 1)
    ).astype(jnp.float32)
    left_base = jnp.einsum("pbc,bt->ptc", owned, lower_mask, precision=lax.Precision.HIGHEST)
    node_total = jnp.sum(owned, axis=1, keepdims=True)
    left_miss = left_base + owned[:, BINS - 1 :, :]
    parent_score = split_score(node_total, classes)
    gain_left = (
        split_score(left_miss, classes)
        + split_score(node_total - left_miss, classes)
        - parent_score
    )
    gain_right = (
        split_score(left_base, classes)
        + split_score(node_total - left_base, classes)
        - parent_score
    )
    gain = jnp.concatenate([gain_left, gain_right], axis=1) / (2.0 * classes)
    moves = [
        (n * per_node + cut * group + r, n * per_node + r * cuts + cut)
        for n in range(node_count)
        for cut in range(cuts)
        for r in range(group)
    ]
    gain_rows = lax.ppermute(gain, "rows", moves)
    return (new_logits, gain_rows[None], leaves)


def solution(mesh):
    return jax.shard_map(
        local,
        mesh=mesh,
        in_specs=(P("rows", None), P("rows"), P("rows"), P("rows", "feat"), P(), P(), P()),
        out_specs=(P("rows", None), P("rows", "feat", None), P()),
        check_vma=False,
    )
```

```python
import functools

import jax
import jax.numpy as jnp
from jax import lax
from jax.experimental import pallas as pl
from jax.experimental.pallas import tpu as pltpu
from jax.sharding import PartitionSpec as P

BINS = 64
LANES = 128
VMEM_BYTES = 12 * 1024 * 1024
PREP_VMEM_BYTES = 60 * 1024 * 1024
SMALL_COST = pl.CostEstimate(flops=1000000, bytes_accessed=1000000, transcendentals=0)


reg_lambda = 1.0
step_size = 0.3


def split_score(sums, classes):
    grad_part = sums[..., :classes]
    hess_part = sums[..., classes:]
    return jnp.sum(grad_part * grad_part / (hess_part + reg_lambda), axis=-1)


def three_parts(x):
    first = x.astype(jnp.bfloat16)
    rest = x - first.astype(jnp.float32)
    second = rest.astype(jnp.bfloat16)
    third = (rest - second.astype(jnp.float32)).astype(jnp.bfloat16)
    return first, second, third


def threshold_masks():
    row = lax.broadcasted_iota(jnp.int32, (2 * BINS, 4 * BINS), 0)
    col = lax.broadcasted_iota(jnp.int32, (2 * BINS, 4 * BINS), 1)
    bin_of = row % BINS
    threshold = col % BINS
    first_dir = (col // BINS) % 2 == 0
    below = (bin_of < threshold) & (bin_of < BINS - 1)
    missing = (bin_of == BINS - 1) & first_dir
    same = row // BINS == col // (2 * BINS)
    return jnp.where((below | missing) & same, 1.0, 0.0).astype(jnp.bfloat16)


def half_width(rows):
    return rows // 2 + 2 * LANES


def read_info(halves, rows):
    half = rows // 2
    chunks = half // LANES
    prob = jnp.concatenate([info[:, :half] for info in halves], axis=1)
    label, node = (
        jnp.concatenate(
            [info[i : i + 1, low : low + LANES] for info in halves for i in range(chunks)], axis=1
        )
        for low in (half, half + LANES)
    )
    return prob, label, node


def child_sums(info, rows, node_count):
    return info[-node_count:, rows // 2 : rows // 2 + LANES]


def prep_kernel(
    own,
    blocks,
    *refs,
):
    operands, rest = refs[:7], refs[7:]
    info_ref, half_ref, flag_ref = rest[:3]
    outs = rest[3 : 3 + len(blocks)]
    turned, *buffers, sems = rest[3 + len(blocks) :]
    copies = [
        pltpu.make_async_copy(operand, buffer, sems.at[i])
        for i, (operand, buffer) in enumerate(zip(operands, buffers))
    ]
    for copy in copies:
        copy.start()
    for copy in copies:
        copy.wait()
    codes_ref, logits_ref, labels_ref, nodes_ref, feature_ref, bin_ref, missing_ref = buffers
    row_index, feat_index = lax.axis_index("rows"), lax.axis_index("feat")
    classes, rows = logits_ref.shape
    half, width = rows // 2, half_width(rows)
    chunks = half // LANES
    turned[...] = codes_ref[...].T
    for (infos, pieces), out_ref in zip(blocks, outs):
        for i, start_of in enumerate(pieces):
            start = pl.multiple_of(start_of(row_index), own)
            if infos == 0:
                out_ref[i * own : (i + 1) * own, :] = turned[pl.ds(start, own), :]
                continue
            cut = rows * infos // 2
            for h in range(2 // infos):
                low = classes + (h * len(pieces) + i) * own
                part = turned[pl.ds(start, own), h * cut : (h + 1) * cut]
                out_ref[low : low + own, :cut] = part.astype(out_ref.dtype)
                out_ref[low : low + own, cut:] = jnp.zeros((own, infos * width - cut), out_ref.dtype)
    expo_vals = jnp.exp(logits_ref[...])
    prob = expo_vals / jnp.sum(expo_vals, axis=0, keepdims=True)
    labels = labels_ref[...].astype(jnp.float32)
    nodes = nodes_ref[...].astype(jnp.float32)
    label = jnp.concatenate([labels[i : i + 1] for i in range(2 * chunks)], axis=1)
    node = jnp.concatenate([nodes[i : i + 1] for i in range(2 * chunks)], axis=1)

    feats = turned.shape[0]
    node_count = feature_ref.shape[0]
    side = jnp.zeros((1, rows), jnp.float32)
    for n in range(node_count):
        col = feature_ref[n] - feat_index * feats
        held = (col >= 0) & (col < feats)
        code = turned[pl.ds(jnp.clip(col, 0, feats - 1), 1), :]
        threshold = jnp.where(held, bin_ref[n], -1)
        missing = jnp.where(held & (missing_ref[n] == 1), BINS - 1, -1)
        left = (code < threshold) | (code == missing)
        value = jnp.where(left, 1.0, jnp.where(held, 2.0, 0.0))
        side = jnp.where(node == float(n), value, side)
    flag_ref[...] = jnp.where(side == 2.0, 1.0, 0.0)
    hot = jnp.concatenate(
        [
            jnp.where((node == float(slot // 2)) & (side == float(slot % 2 + 1)), 1.0, 0.0)
            for slot in range(2 * node_count)
        ],
        axis=0,
    ).astype(jnp.bfloat16)
    sums = lax.dot_general(
        hot,
        gradients(prob, label).astype(jnp.bfloat16),
        (((1,), (1,)), ((), ())),
        preferred_element_type=jnp.float32,
    )
    sums = jnp.concatenate([sums[:node_count], sums[node_count:]], axis=1)
    pad = jnp.zeros((classes - chunks - node_count, LANES), jnp.float32)
    long_pad = jnp.zeros((classes - chunks, LANES), jnp.float32)
    for h in range(2):
        some = slice(h * chunks, (h + 1) * chunks)
        info_ref[:, h * width : h * width + half] = prob[:, h * half : (h + 1) * half]
        info_ref[:, h * width + half : h * width + half + LANES] = jnp.concatenate(
            [labels[some], pad, sums], axis=0
        )
        info_ref[:, h * width + half + LANES : (h + 1) * width] = jnp.concatenate(
            [nodes[some], long_pad], axis=0
        )
    half_ref[...] = jnp.where(feat_index == 0, info_ref[:, :width], info_ref[:, width:])
    for (infos, _), out_ref in zip(blocks, outs):
        if infos > 0:
            out_ref[:classes, :] = half_ref[...] if infos == 1 else info_ref[...]


def gradients(prob, label):
    class_iota = lax.broadcasted_iota(jnp.int32, prob.shape, 0).astype(jnp.float32)
    target = jnp.where(class_iota == label, 1.0, 0.0)
    return jnp.concatenate([prob - target, prob * (1.0 - prob)], axis=0)


def masked_gradients(halves, rows, node_count):
    prob, label, node = read_info(halves, rows)
    grad_hess = gradients(prob, label)
    return jnp.concatenate(
        [jnp.where(node == float(n), grad_hess, 0.0).astype(jnp.bfloat16) for n in range(node_count)],
        axis=0,
    )


def one_hot(codes):
    feats, rows = codes.shape
    bin_iota = lax.broadcasted_iota(jnp.int32, (BINS, rows), 0).astype(codes.dtype)
    return jnp.concatenate(
        [
            jnp.where(codes[f : f + 1, :] == bin_iota, 1.0, 0.0).astype(jnp.bfloat16)
            for f in range(feats)
        ],
        axis=0,
    )


def write_gains(hist_ref, gain_ref, classes, node_count):
    masks = threshold_masks()
    ones = jnp.where(
        lax.broadcasted_iota(jnp.int32, (2 * BINS, 4 * BINS), 0) < BINS, 1.0, 0.0
    ).astype(jnp.bfloat16)

    def times(parts, right):
        return sum(jnp.dot(part, right, preferred_element_type=jnp.float32) for part in parts)

    total = times(three_parts(hist_ref[:, : 2 * BINS]), ones)
    for pair in range(gain_ref.shape[1] // 2):
        span = slice(pair * 2 * BINS, (pair + 1) * 2 * BINS)
        left = times(three_parts(hist_ref[:, span]), masks)
        right = total - left
        for n in range(node_count):
            grads = slice(n * 2 * classes, n * 2 * classes + classes)
            hesss = slice(n * 2 * classes + classes, (n + 1) * 2 * classes)
            score = (
                left[grads] * left[grads] / (left[hesss] + reg_lambda)
                + right[grads] * right[grads] / (right[hesss] + reg_lambda)
            )
            parent = total[grads] * total[grads] / (total[hesss] + reg_lambda)
            gain = (
                jnp.sum(score, axis=0, keepdims=True) - jnp.sum(parent, axis=0, keepdims=True)
            ) / (2.0 * classes)
            gain_ref[n, 2 * pair : 2 * pair + 1, :] = gain[:, : 2 * BINS]
            gain_ref[n, 2 * pair + 1 : 2 * pair + 2, :] = gain[:, 2 * BINS :]


def add_kernel(classes, node_count, own, plan, carry, *refs):
    outs = len(plan[0][3])
    arrays = 1 + max(max((c,) + i) for _, c, i, _ in plan)
    out_refs = refs[-outs:]
    held_refs = refs[arrays:-outs]
    pairs = 2 * classes * node_count
    row_index, feat_index = lax.axis_index("rows"), lax.axis_index("feat")
    for s, (m, codes_at, info_at, firsts) in enumerate(plan):
        codes_ref = refs[codes_at]
        line = (row_index >> 2) ^ (m >> 2)
        if len(info_at) == 1:
            width = refs[info_at[0]].shape[1] // 2
            low, high = (refs[info_at[0]][:classes, h * width : (h + 1) * width] for h in range(2))
            sums_from = low
        else:
            width = refs[info_at[0]].shape[1]
            near, far = (refs[i][:classes, :] for i in info_at)
            low = jnp.where(feat_index == 0, near, far)
            high = jnp.where(feat_index == 0, far, near)
            sums_from = near
        rows = 2 * (width - 2 * LANES)
        masked = masked_gradients((low, high), rows, node_count)
        sums = child_sums(sums_from, rows, node_count)
        for i, first in enumerate(firsts):
            out_ref = out_refs[i]
            if codes_ref.shape[1] < rows:
                second = first + (codes_ref.shape[0] - classes) // 2
                codes = jnp.concatenate(
                    [codes_ref[low : low + own, : rows // 2] for low in (first, second)], axis=1
                )
            else:
                codes = codes_ref[first : first + own, :rows]
            product = lax.dot_general(
                masked,
                one_hot(codes),
                (((1,), (1,)), ((), ())),
                preferred_element_type=jnp.float32,
            )
            if s == 0:
                if held_refs:
                    out_ref[...] = sum(ref[...] for ref in held_refs[i::outs])
                else:
                    out_ref[...] = jnp.zeros(out_ref.shape, out_ref.dtype)
            out_ref[:pairs, :] += product
            if not carry:
                continue
            low_row = pairs + (row_index & 3) * node_count
            band = pl.ds(pl.multiple_of(low_row, node_count), node_count)
            for i in range(out_ref.shape[1] // LANES):
                here = jnp.where(line == i, 1.0, 0.0)
                out_ref[band, i * LANES : (i + 1) * LANES] += here * sums


def add_rows(classes, node_count, own, carry, plan, arrays, *held):
    shape = (2 * classes * node_count + 4 * node_count, own * BINS)
    whole = pl.BlockSpec(memory_space=pltpu.VMEM)
    outs = len(plan[0][3])
    return pl.pallas_call(
        functools.partial(add_kernel, classes, node_count, own, plan, carry),
        in_specs=[whole] * (len(arrays) + len(held) * outs),
        out_specs=[whole] * outs,
        out_shape=[jax.ShapeDtypeStruct(shape, jnp.float32)] * outs,
        compiler_params=pltpu.CompilerParams(vmem_limit_bytes=VMEM_BYTES),
        cost_estimate=SMALL_COST,
    )(*arrays, *[hist for hists in held for hist in hists])


def gain_kernel(classes, node_count, *refs):
    gain_ref, hist_ref = refs[-2:]
    hist_ref[...] = sum(ref[: hist_ref.shape[0], :] for ref in refs[:-2])
    write_gains(hist_ref, gain_ref, classes, node_count)


def swap(x, axis, bit):
    size = lax.axis_size(axis)
    return lax.ppermute(x, axis, [(i, i ^ bit) for i in range(size)])


def sum_over(x, axis):
    bit = 1
    while bit < lax.axis_size(axis):
        x = x + swap(x, axis, bit)
        bit *= 2
    return x


def prepare(blocks, splits, logits_t, labels, node_ids, bin_codes):
    classes, rows_dev = logits_t.shape
    feats_dev = bin_codes.shape[1]
    own = 8
    whole = pl.BlockSpec(memory_space=pltpu.VMEM)
    width = half_width(rows_dev)
    shapes = [
        jax.ShapeDtypeStruct((classes, 2 * width), jnp.float32),
        jax.ShapeDtypeStruct((classes, width), jnp.float32),
        jax.ShapeDtypeStruct((1, rows_dev), jnp.float32),
    ]
    for infos, pieces in blocks:
        codes = len(pieces) * own
        if infos == 0:
            shapes.append(jax.ShapeDtypeStruct((codes, rows_dev), jnp.int32))
        else:
            shape = (classes + codes * 2 // infos, infos * width)
            shapes.append(jax.ShapeDtypeStruct(shape, jnp.float32))
    operands = (
        bin_codes,
        logits_t,
        labels.reshape(-1, LANES),
        node_ids.reshape(-1, LANES),
        *splits,
    )
    spaces = [pltpu.VMEM] * 4 + [pltpu.SMEM] * 3
    return pl.pallas_call(
        functools.partial(prep_kernel, own, blocks),
        in_specs=[pl.BlockSpec(memory_space=pltpu.HBM)] * len(operands),
        out_specs=[whole] * len(shapes),
        out_shape=shapes,
        scratch_shapes=[pltpu.VMEM((feats_dev, rows_dev), jnp.int32)]
        + [space(x.shape, x.dtype) for space, x in zip(spaces, operands)]
        + [pltpu.SemaphoreType.DMA((len(operands),))],
        compiler_params=pltpu.CompilerParams(vmem_limit_bytes=PREP_VMEM_BYTES),
        cost_estimate=SMALL_COST,
    )(*operands)


def finish(logits_t, node_ids, side_count, sums, node_count):
    classes = logits_t.shape[0]
    width = 2 * classes
    side_sums = jnp.concatenate([sums[:, :width], sums[:, width:]], axis=0)
    side_sums = side_sums.reshape(node_count, 2, width)
    leaves = -side_sums[..., :classes] / (side_sums[..., classes:] + reg_lambda)
    row_side = (side_count > 0.5).astype(jnp.int32)
    slot_iota = jnp.arange(2 * node_count, dtype=jnp.int32)
    slot_hot = (node_ids[None, :] * 2 + row_side) == slot_iota[:, None]
    update = jnp.dot(
        leaves.reshape(2 * node_count, classes).T,
        slot_hot.astype(jnp.float32),
        precision=lax.Precision.HIGHEST,
    )
    return (logits_t + step_size * update).T, leaves


def local(logits, labels, node_ids, bin_codes, split_feature, split_bin, split_missing):
    rows_dev, classes = logits.shape
    feats_dev = bin_codes.shape[1]
    node_count = split_feature.shape[0]
    n_rows = lax.axis_size("rows")
    per_node = n_rows // node_count
    pairs_dev = feats_dev // per_node
    width = 2 * classes
    own = 8
    splits = (split_feature, split_bin, split_missing)
    logits_t = logits.T
    if feats_dev != own * n_rows or n_rows != 16 or lax.axis_size("feat") != 2:
        return by_groups(logits_t, labels, node_ids, bin_codes, splits, per_node, pairs_dev)
    add = functools.partial(add_rows, classes, node_count, own, True)

    def start(taker):
        return (taker & 1) * pairs_dev + (taker >> 1) * own

    def quarters(m, which):
        return tuple(lambda row, low=m ^ 3 ^ q: start(row ^ low) for q in which)

    blocks = (
        (0, quarters(0, (0, 1, 2, 3))),
        (1, quarters(4, (0, 1))),
        (0, quarters(8, (0, 1, 2, 3))),
        (0, quarters(12, (0, 1))),
        (0, quarters(4, (2, 3))),
        (0, quarters(12, (2, 3))),
    )
    info, half, flags, codes_0, rows_4, codes_8, codes_12, late_4, late_12 = prepare(
        blocks, splits, logits_t, labels, node_ids, bin_codes
    )

    near_8 = swap(half, "rows", 8)
    rows_4 = swap(rows_4, "rows", 4)
    codes_8 = swap(codes_8, "rows", 8)
    codes_12 = swap(codes_12, "rows", 12)
    hist_a, hist_b, hist_c, hist_d = add(
        ((0, 0, (1,), (0, own, 2 * own, 3 * own)),), [codes_0, info]
    )
    near_8, rows_4, hist_a = lax.optimization_barrier((near_8, rows_4, hist_a))
    near_12 = swap(near_8, "rows", 4)
    far_8 = swap(near_8, "feat", 1)
    far_4 = swap(rows_4[:classes], "feat", 1)
    late_4 = swap(late_4, "rows", 4)
    late_12 = swap(late_12, "rows", 12)
    hist_a, hist_b = add(
        ((4, 0, (0, 1), (classes, classes + own)),), [rows_4, far_4], [hist_a, hist_b]
    )
    near_12, codes_8, codes_12, hist_a = lax.optimization_barrier((near_12, codes_8, codes_12, hist_a))
    far_12 = swap(near_12, "feat", 1)
    hist_a, hist_b = add(((8, 0, (1, 2), (0, own)),), [codes_8, near_8, far_8], [hist_a, hist_b])
    (to_core,) = add(((12, 0, (1, 2), (0,)),), [codes_12, near_12, far_12], [hist_a])
    from_core = swap(to_core, "rows", 1)
    (to_plane,) = add(((12, 0, (1, 2), (own,)),), [codes_12, near_12, far_12], [hist_b], [from_core])
    from_plane = swap(to_plane, "rows", 2)
    _, codes_8 = lax.optimization_barrier((to_plane, codes_8))
    late = [late_4, codes_8, late_12, rows_4, far_4, near_8, far_8, near_12, far_12]
    to_core, kept = add(
        (
            (8, 1, (5, 6), (2 * own, 3 * own)),
            (4, 0, (3, 4), (0, own)),
            (12, 2, (7, 8), (0, own)),
        ),
        late,
        [hist_c, hist_d],
    )
    middle = to_core.shape[0] // 2
    from_core = [swap(part, "rows", 1) for part in (to_core[:middle], to_core[middle:])]
    from_core = jnp.concatenate(from_core, axis=0)

    pairs = node_count * width
    gains = pl.pallas_call(
        functools.partial(gain_kernel, classes, node_count),
        in_specs=[pl.BlockSpec(memory_space=pltpu.VMEM)] * 3,
        out_specs=pl.BlockSpec(memory_space=pltpu.VMEM),
        out_shape=jax.ShapeDtypeStruct((node_count, own, 2 * BINS), jnp.float32),
        scratch_shapes=[pltpu.VMEM((pairs, own * BINS), jnp.float32)],
        compiler_params=pltpu.CompilerParams(vmem_limit_bytes=VMEM_BYTES),
        cost_estimate=SMALL_COST,
    )(from_core, from_plane, kept)
    def gather(parts):
        return jnp.sum(parts.reshape(4, node_count, -1, LANES), axis=(0, 2))

    gains, from_plane = lax.optimization_barrier((gains, from_plane))
    sums = gather(from_core[pairs:] + from_plane[pairs:] + kept[pairs:])
    children = jnp.concatenate([sums, flags.reshape(-1, LANES)], axis=0)
    children = sum_over(children, "feat")
    side_count = children[node_count:].reshape(1, rows_dev)
    sums = children[:node_count]
    new_logits, leaves = finish(logits_t, node_ids, side_count, sums, node_count)

    halves = [[h + n * per_node for n in range(node_count)] for h in range(per_node)]
    gain_rows = lax.all_to_all(gains, "rows", 0, 0, tiled=True, axis_index_groups=halves)
    return (new_logits, gain_rows.reshape(1, pairs_dev, 2 * BINS), leaves)


def by_groups(logits_t, labels, node_ids, bin_codes, splits, per_node, pairs_dev):
    classes, rows_dev = logits_t.shape
    feats_dev = bin_codes.shape[1]
    node_count = splits[0].shape[0]
    n_rows = lax.axis_size("rows")
    width = 2 * classes
    own = 8
    group = feats_dev // own
    group_count = n_rows // group
    blocks = tuple((2, (lambda row, r=r: r * own,)) for r in range(group))
    info, _, flags, *rows_out = prepare(blocks, splits, logits_t, labels, node_ids, bin_codes)
    members = [[g * group + r for r in range(group)] for g in range(group_count)]
    rows_in = lax.all_to_all(
        jnp.stack(rows_out), "rows", 0, 0, tiled=True, axis_index_groups=members
    )
    hists = []
    for r in range(group):
        held = [hists] if hists else []
        hists = add_rows(
            classes, node_count, own, False, ((0, 0, (0,), (classes,)),), [rows_in[r]], *held
        )
    sums = lax.psum(child_sums(info[:, : half_width(rows_dev)], rows_dev, node_count), ("rows", "feat"))
    side_count = lax.psum(flags, "feat")
    new_logits, leaves = finish(logits_t, node_ids, side_count, sums, node_count)

    cuts = own // pairs_dev
    hist = hists[0][: node_count * width]
    hist = hist.reshape(node_count, width, cuts, pairs_dev, BINS).transpose(0, 2, 3, 4, 1)
    peers = [[g * group + r for g in range(group_count)] for r in range(group)]
    owned = lax.psum_scatter(
        hist.reshape(group_count, pairs_dev, BINS, width),
        "rows",
        scatter_dimension=0,
        axis_index_groups=peers,
    )
    bin_iota = jnp.arange(BINS, dtype=jnp.int32)
    lower_mask = (
        (bin_iota[:, None] < bin_iota[None, :]) & (bin_iota[:, None] < BINS - 1)
    ).astype(jnp.float32)
    left_base = jnp.einsum("pbc,bt->ptc", owned, lower_mask, precision=lax.Precision.HIGHEST)
    node_total = jnp.sum(owned, axis=1, keepdims=True)
    left_miss = left_base + owned[:, BINS - 1 :, :]
    parent_score = split_score(node_total, classes)
    gain_left = (
        split_score(left_miss, classes)
        + split_score(node_total - left_miss, classes)
        - parent_score
    )
    gain_right = (
        split_score(left_base, classes)
        + split_score(node_total - left_base, classes)
        - parent_score
    )
    gain = jnp.concatenate([gain_left, gain_right], axis=1) / (2.0 * classes)
    moves = [
        (n * per_node + cut * group + r, n * per_node + r * cuts + cut)
        for n in range(node_count)
        for cut in range(cuts)
        for r in range(group)
    ]
    gain_rows = lax.ppermute(gain, "rows", moves)
    return (new_logits, gain_rows[None], leaves)


def solution(mesh):
    return jax.shard_map(
        local,
        mesh=mesh,
        in_specs=(P("rows", None), P("rows"), P("rows"), P("rows", "feat"), P(), P(), P()),
        out_specs=(P("rows", None), P("rows", "feat", None), P()),
        check_vma=False,
    )
```

```python
import functools

import jax
import jax.numpy as jnp
from jax import lax
from jax.experimental import pallas as pl
from jax.experimental.pallas import tpu as pltpu
from jax.sharding import PartitionSpec as P

BINS = 64
LANES = 128
VMEM_BYTES = 12 * 1024 * 1024
PREP_VMEM_BYTES = 60 * 1024 * 1024
SMALL_COST = pl.CostEstimate(flops=1000000, bytes_accessed=1000000, transcendentals=0)


reg_lambda = 1.0
step_size = 0.3


def split_score(sums, classes):
    grad_part = sums[..., :classes]
    hess_part = sums[..., classes:]
    return jnp.sum(grad_part * grad_part / (hess_part + reg_lambda), axis=-1)


def three_parts(x):
    first = x.astype(jnp.bfloat16)
    rest = x - first.astype(jnp.float32)
    second = rest.astype(jnp.bfloat16)
    third = (rest - second.astype(jnp.float32)).astype(jnp.bfloat16)
    return first, second, third


def threshold_masks():
    row = lax.broadcasted_iota(jnp.int32, (2 * BINS, 4 * BINS), 0)
    col = lax.broadcasted_iota(jnp.int32, (2 * BINS, 4 * BINS), 1)
    bin_of = row % BINS
    threshold = col % BINS
    first_dir = (col // BINS) % 2 == 0
    below = (bin_of < threshold) & (bin_of < BINS - 1)
    missing = (bin_of == BINS - 1) & first_dir
    same = row // BINS == col // (2 * BINS)
    return jnp.where((below | missing) & same, 1.0, 0.0).astype(jnp.bfloat16)


def half_width(rows):
    return rows // 2 + 2 * LANES


def read_info(halves, rows):
    half = rows // 2
    chunks = half // LANES
    prob = jnp.concatenate([info[:, :half] for info in halves], axis=1)
    label, node = (
        jnp.concatenate(
            [info[i : i + 1, low : low + LANES] for info in halves for i in range(chunks)], axis=1
        )
        for low in (half, half + LANES)
    )
    return prob, label, node


def child_sums(info, rows, node_count):
    return info[-node_count:, rows // 2 : rows // 2 + LANES]


def prep_kernel(
    own,
    blocks,
    *refs,
):
    operands, rest = refs[:7], refs[7:]
    info_ref, half_ref, flag_ref = rest[:3]
    outs = rest[3 : 3 + len(blocks)]
    turned, *buffers, sems = rest[3 + len(blocks) :]
    copies = [
        pltpu.make_async_copy(operand, buffer, sems.at[i])
        for i, (operand, buffer) in enumerate(zip(operands, buffers))
    ]
    for copy in copies:
        copy.start()
    for copy in copies:
        copy.wait()
    codes_ref, logits_ref, labels_ref, nodes_ref, feature_ref, bin_ref, missing_ref = buffers
    row_index, feat_index = lax.axis_index("rows"), lax.axis_index("feat")
    classes, rows = logits_ref.shape
    half, width = rows // 2, half_width(rows)
    chunks = half // LANES
    turned[...] = codes_ref[...].T
    for (infos, pieces), out_ref in zip(blocks, outs):
        for i, start_of in enumerate(pieces):
            start = pl.multiple_of(start_of(row_index), own)
            if infos == 0:
                out_ref[i * own : (i + 1) * own, :] = turned[pl.ds(start, own), :]
                continue
            cut = rows * infos // 2
            for h in range(2 // infos):
                low = classes + (h * len(pieces) + i) * own
                part = turned[pl.ds(start, own), h * cut : (h + 1) * cut]
                out_ref[low : low + own, :cut] = part.astype(out_ref.dtype)
                out_ref[low : low + own, cut:] = jnp.zeros((own, infos * width - cut), out_ref.dtype)
    expo_vals = jnp.exp(logits_ref[...])
    prob = expo_vals / jnp.sum(expo_vals, axis=0, keepdims=True)
    labels = labels_ref[...].astype(jnp.float32)
    nodes = nodes_ref[...].astype(jnp.float32)
    label = jnp.concatenate([labels[i : i + 1] for i in range(2 * chunks)], axis=1)
    node = jnp.concatenate([nodes[i : i + 1] for i in range(2 * chunks)], axis=1)

    feats = turned.shape[0]
    node_count = feature_ref.shape[0]
    side = jnp.zeros((1, rows), jnp.float32)
    for n in range(node_count):
        col = feature_ref[n] - feat_index * feats
        held = (col >= 0) & (col < feats)
        code = turned[pl.ds(jnp.clip(col, 0, feats - 1), 1), :]
        threshold = jnp.where(held, bin_ref[n], -1)
        missing = jnp.where(held & (missing_ref[n] == 1), BINS - 1, -1)
        left = (code < threshold) | (code == missing)
        value = jnp.where(left, 1.0, jnp.where(held, 2.0, 0.0))
        side = jnp.where(node == float(n), value, side)
    flag_ref[...] = jnp.where(side == 2.0, 1.0, 0.0)
    hot = jnp.concatenate(
        [
            jnp.where((node == float(slot // 2)) & (side == float(slot % 2 + 1)), 1.0, 0.0)
            for slot in range(2 * node_count)
        ],
        axis=0,
    ).astype(jnp.bfloat16)
    sums = lax.dot_general(
        hot,
        gradients(prob, label).astype(jnp.bfloat16),
        (((1,), (1,)), ((), ())),
        preferred_element_type=jnp.float32,
    )
    sums = jnp.concatenate([sums[:node_count], sums[node_count:]], axis=1)
    pad = jnp.zeros((classes - chunks - node_count, LANES), jnp.float32)
    long_pad = jnp.zeros((classes - chunks, LANES), jnp.float32)
    for h in range(2):
        some = slice(h * chunks, (h + 1) * chunks)
        info_ref[:, h * width : h * width + half] = prob[:, h * half : (h + 1) * half]
        info_ref[:, h * width + half : h * width + half + LANES] = jnp.concatenate(
            [labels[some], pad, sums], axis=0
        )
        info_ref[:, h * width + half + LANES : (h + 1) * width] = jnp.concatenate(
            [nodes[some], long_pad], axis=0
        )
    half_ref[...] = jnp.where(feat_index == 0, info_ref[:, :width], info_ref[:, width:])
    for (infos, _), out_ref in zip(blocks, outs):
        if infos > 0:
            out_ref[:classes, :] = half_ref[...] if infos == 1 else info_ref[...]


def gradients(prob, label):
    class_iota = lax.broadcasted_iota(jnp.int32, prob.shape, 0).astype(jnp.float32)
    target = jnp.where(class_iota == label, 1.0, 0.0)
    return jnp.concatenate([prob - target, prob * (1.0 - prob)], axis=0)


def masked_gradients(halves, rows, node_count):
    prob, label, node = read_info(halves, rows)
    grad_hess = gradients(prob, label)
    return jnp.concatenate(
        [jnp.where(node == float(n), grad_hess, 0.0).astype(jnp.bfloat16) for n in range(node_count)],
        axis=0,
    )


def one_hot(codes):
    feats, rows = codes.shape
    bin_iota = lax.broadcasted_iota(jnp.int32, (BINS, rows), 0).astype(codes.dtype)
    return jnp.concatenate(
        [
            jnp.where(codes[f : f + 1, :] == bin_iota, 1.0, 0.0).astype(jnp.bfloat16)
            for f in range(feats)
        ],
        axis=0,
    )


def write_gains(hist_ref, gain_ref, classes, node_count):
    masks = threshold_masks()
    ones = jnp.where(
        lax.broadcasted_iota(jnp.int32, (2 * BINS, 4 * BINS), 0) < BINS, 1.0, 0.0
    ).astype(jnp.bfloat16)

    def times(parts, right):
        return sum(jnp.dot(part, right, preferred_element_type=jnp.float32) for part in parts)

    total = times(three_parts(hist_ref[:, : 2 * BINS]), ones)
    for pair in range(gain_ref.shape[1] // 2):
        span = slice(pair * 2 * BINS, (pair + 1) * 2 * BINS)
        left = times(three_parts(hist_ref[:, span]), masks)
        right = total - left
        for n in range(node_count):
            grads = slice(n * 2 * classes, n * 2 * classes + classes)
            hesss = slice(n * 2 * classes + classes, (n + 1) * 2 * classes)
            score = (
                left[grads] * left[grads] / (left[hesss] + reg_lambda)
                + right[grads] * right[grads] / (right[hesss] + reg_lambda)
            )
            parent = total[grads] * total[grads] / (total[hesss] + reg_lambda)
            gain = (
                jnp.sum(score, axis=0, keepdims=True) - jnp.sum(parent, axis=0, keepdims=True)
            ) / (2.0 * classes)
            gain_ref[n, 2 * pair : 2 * pair + 1, :] = gain[:, : 2 * BINS]
            gain_ref[n, 2 * pair + 1 : 2 * pair + 2, :] = gain[:, 2 * BINS :]


def add_kernel(classes, node_count, own, plan, carry, *refs):
    outs = len(plan[0][3])
    arrays = 1 + max(max((c,) + i) for _, c, i, _ in plan)
    out_refs = refs[-outs:]
    held_refs = refs[arrays:-outs]
    pairs = 2 * classes * node_count
    row_index, feat_index = lax.axis_index("rows"), lax.axis_index("feat")
    for s, (m, codes_at, info_at, firsts) in enumerate(plan):
        codes_ref = refs[codes_at]
        line = (row_index >> 2) ^ (m >> 2)
        if len(info_at) == 1:
            width = refs[info_at[0]].shape[1] // 2
            low, high = (refs[info_at[0]][:classes, h * width : (h + 1) * width] for h in range(2))
            sums_from = low
        else:
            width = refs[info_at[0]].shape[1]
            near, far = (refs[i][:classes, :] for i in info_at)
            low = jnp.where(feat_index == 0, near, far)
            high = jnp.where(feat_index == 0, far, near)
            sums_from = near
        rows = 2 * (width - 2 * LANES)
        masked = masked_gradients((low, high), rows, node_count)
        sums = child_sums(sums_from, rows, node_count)
        for i, first in enumerate(firsts):
            out_ref = out_refs[i]
            if codes_ref.shape[1] < rows:
                second = first + (codes_ref.shape[0] - classes) // 2
                codes = jnp.concatenate(
                    [codes_ref[low : low + own, : rows // 2] for low in (first, second)], axis=1
                )
            else:
                codes = codes_ref[first : first + own, :rows]
            product = lax.dot_general(
                masked,
                one_hot(codes),
                (((1,), (1,)), ((), ())),
                preferred_element_type=jnp.float32,
            )
            if s == 0:
                if held_refs:
                    out_ref[...] = sum(ref[...] for ref in held_refs[i::outs])
                else:
                    out_ref[...] = jnp.zeros(out_ref.shape, out_ref.dtype)
            out_ref[:pairs, :] += product
            if not carry:
                continue
            low_row = pairs + (row_index & 3) * node_count
            band = pl.ds(pl.multiple_of(low_row, node_count), node_count)
            for i in range(out_ref.shape[1] // LANES):
                here = jnp.where(line == i, 1.0, 0.0)
                out_ref[band, i * LANES : (i + 1) * LANES] += here * sums


def add_rows(classes, node_count, own, carry, plan, arrays, *held):
    shape = (2 * classes * node_count + 4 * node_count, own * BINS)
    whole = pl.BlockSpec(memory_space=pltpu.VMEM)
    outs = len(plan[0][3])
    return pl.pallas_call(
        functools.partial(add_kernel, classes, node_count, own, plan, carry),
        in_specs=[whole] * (len(arrays) + len(held) * outs),
        out_specs=[whole] * outs,
        out_shape=[jax.ShapeDtypeStruct(shape, jnp.float32)] * outs,
        compiler_params=pltpu.CompilerParams(vmem_limit_bytes=VMEM_BYTES),
        cost_estimate=SMALL_COST,
    )(*arrays, *[hist for hists in held for hist in hists])


def gain_kernel(classes, node_count, *refs):
    gain_ref, hist_ref = refs[-2:]
    hist_ref[...] = sum(ref[: hist_ref.shape[0], :] for ref in refs[:-2])
    write_gains(hist_ref, gain_ref, classes, node_count)


def swap(x, axis, bit):
    size = lax.axis_size(axis)
    return lax.ppermute(x, axis, [(i, i ^ bit) for i in range(size)])


def sum_over(x, axis):
    bit = 1
    while bit < lax.axis_size(axis):
        x = x + swap(x, axis, bit)
        bit *= 2
    return x


def prepare(blocks, splits, logits_t, labels, node_ids, bin_codes):
    classes, rows_dev = logits_t.shape
    feats_dev = bin_codes.shape[1]
    own = 8
    whole = pl.BlockSpec(memory_space=pltpu.VMEM)
    width = half_width(rows_dev)
    shapes = [
        jax.ShapeDtypeStruct((classes, 2 * width), jnp.float32),
        jax.ShapeDtypeStruct((classes, width), jnp.float32),
        jax.ShapeDtypeStruct((1, rows_dev), jnp.float32),
    ]
    for infos, pieces in blocks:
        codes = len(pieces) * own
        if infos == 0:
            shapes.append(jax.ShapeDtypeStruct((codes, rows_dev), jnp.int32))
        else:
            shape = (classes + codes * 2 // infos, infos * width)
            shapes.append(jax.ShapeDtypeStruct(shape, jnp.float32))
    operands = (
        bin_codes,
        logits_t,
        labels.reshape(-1, LANES),
        node_ids.reshape(-1, LANES),
        *splits,
    )
    spaces = [pltpu.VMEM] * 4 + [pltpu.SMEM] * 3
    return pl.pallas_call(
        functools.partial(prep_kernel, own, blocks),
        in_specs=[pl.BlockSpec(memory_space=pltpu.HBM)] * len(operands),
        out_specs=[whole] * len(shapes),
        out_shape=shapes,
        scratch_shapes=[pltpu.VMEM((feats_dev, rows_dev), jnp.int32)]
        + [space(x.shape, x.dtype) for space, x in zip(spaces, operands)]
        + [pltpu.SemaphoreType.DMA((len(operands),))],
        compiler_params=pltpu.CompilerParams(vmem_limit_bytes=PREP_VMEM_BYTES),
        cost_estimate=SMALL_COST,
    )(*operands)


def finish(logits_t, node_ids, side_count, sums, node_count):
    classes = logits_t.shape[0]
    width = 2 * classes
    side_sums = jnp.concatenate([sums[:, :width], sums[:, width:]], axis=0)
    side_sums = side_sums.reshape(node_count, 2, width)
    leaves = -side_sums[..., :classes] / (side_sums[..., classes:] + reg_lambda)
    row_side = (side_count > 0.5).astype(jnp.int32)
    slot_iota = jnp.arange(2 * node_count, dtype=jnp.int32)
    slot_hot = (node_ids[None, :] * 2 + row_side) == slot_iota[:, None]
    update = jnp.dot(
        leaves.reshape(2 * node_count, classes).T,
        slot_hot.astype(jnp.float32),
        precision=lax.Precision.HIGHEST,
    )
    return (logits_t + step_size * update).T, leaves


def local(logits, labels, node_ids, bin_codes, split_feature, split_bin, split_missing):
    rows_dev, classes = logits.shape
    feats_dev = bin_codes.shape[1]
    node_count = split_feature.shape[0]
    n_rows = lax.axis_size("rows")
    per_node = n_rows // node_count
    pairs_dev = feats_dev // per_node
    width = 2 * classes
    own = 8
    splits = (split_feature, split_bin, split_missing)
    logits_t = logits.T
    if feats_dev != own * n_rows or n_rows != 16 or lax.axis_size("feat") != 2:
        return by_groups(logits_t, labels, node_ids, bin_codes, splits, per_node, pairs_dev)
    add = functools.partial(add_rows, classes, node_count, own, True)

    def start(taker):
        return (taker & 1) * pairs_dev + (taker >> 1) * own

    def quarters(m, which):
        return tuple(lambda row, low=m ^ 3 ^ q: start(row ^ low) for q in which)

    blocks = (
        (0, quarters(0, (0, 1, 2, 3))),
        (1, quarters(4, (0, 1))),
        (0, quarters(8, (0, 1))),
        (0, quarters(12, (0, 1))),
        (0, quarters(4, (2, 3))),
        (0, quarters(8, (2, 3))),
        (0, quarters(12, (2, 3))),
    )
    info, half, flags, codes_0, rows_4, codes_8, codes_12, late_4, late_8, late_12 = prepare(
        blocks, splits, logits_t, labels, node_ids, bin_codes
    )

    near_8 = swap(half, "rows", 8)
    rows_4 = swap(rows_4, "rows", 4)
    codes_8 = swap(codes_8, "rows", 8)
    codes_12 = swap(codes_12, "rows", 12)
    hist_a, hist_b, hist_c, hist_d = add(
        ((0, 0, (1,), (0, own, 2 * own, 3 * own)),), [codes_0, info]
    )
    near_8, rows_4, hist_a = lax.optimization_barrier((near_8, rows_4, hist_a))
    near_12 = swap(near_8, "rows", 4)
    far_8 = swap(near_8, "feat", 1)
    far_4 = swap(rows_4[:classes], "feat", 1)
    late_4 = swap(late_4, "rows", 4)
    late_8 = swap(late_8, "rows", 8)
    late_12 = swap(late_12, "rows", 12)
    hist_a, hist_b = add(
        ((4, 0, (0, 1), (classes, classes + own)),), [rows_4, far_4], [hist_a, hist_b]
    )
    near_12, codes_8, codes_12, hist_a = lax.optimization_barrier((near_12, codes_8, codes_12, hist_a))
    far_12 = swap(near_12, "feat", 1)
    hist_a, hist_b = add(((8, 0, (1, 2), (0, own)),), [codes_8, near_8, far_8], [hist_a, hist_b])
    (to_core,) = add(((12, 0, (1, 2), (0,)),), [codes_12, near_12, far_12], [hist_a])
    from_core = swap(to_core, "rows", 1)
    (to_plane,) = add(((12, 0, (1, 2), (own,)),), [codes_12, near_12, far_12], [hist_b], [from_core])
    from_plane = swap(to_plane, "rows", 2)
    _, late_4 = lax.optimization_barrier((to_plane, late_4))
    hists = add(((4, 0, (1, 2), (0, own)),), [late_4, rows_4, far_4], [hist_c, hist_d])
    to_core, kept = add(
        ((8, 0, (2, 3), (0, own)), (12, 1, (4, 5), (0, own))),
        [late_8, late_12, near_8, far_8, near_12, far_12],
        hists,
    )
    middle = to_core.shape[0] // 2
    from_core = [swap(part, "rows", 1) for part in (to_core[:middle], to_core[middle:])]
    from_core = jnp.concatenate(from_core, axis=0)

    pairs = node_count * width
    gains = pl.pallas_call(
        functools.partial(gain_kernel, classes, node_count),
        in_specs=[pl.BlockSpec(memory_space=pltpu.VMEM)] * 3,
        out_specs=pl.BlockSpec(memory_space=pltpu.VMEM),
        out_shape=jax.ShapeDtypeStruct((node_count, own, 2 * BINS), jnp.float32),
        scratch_shapes=[pltpu.VMEM((pairs, own * BINS), jnp.float32)],
        compiler_params=pltpu.CompilerParams(vmem_limit_bytes=VMEM_BYTES),
        cost_estimate=SMALL_COST,
    )(from_core, from_plane, kept)
    def gather(parts):
        return jnp.sum(parts.reshape(4, node_count, -1, LANES), axis=(0, 2))

    gains, from_plane = lax.optimization_barrier((gains, from_plane))
    sums = gather(from_core[pairs:] + from_plane[pairs:] + kept[pairs:])
    children = jnp.concatenate([sums, flags.reshape(-1, LANES)], axis=0)
    children = sum_over(children, "feat")
    side_count = children[node_count:].reshape(1, rows_dev)
    sums = children[:node_count]
    new_logits, leaves = finish(logits_t, node_ids, side_count, sums, node_count)

    halves = [[h + n * per_node for n in range(node_count)] for h in range(per_node)]
    gain_rows = lax.all_to_all(gains, "rows", 0, 0, tiled=True, axis_index_groups=halves)
    return (new_logits, gain_rows.reshape(1, pairs_dev, 2 * BINS), leaves)


def by_groups(logits_t, labels, node_ids, bin_codes, splits, per_node, pairs_dev):
    classes, rows_dev = logits_t.shape
    feats_dev = bin_codes.shape[1]
    node_count = splits[0].shape[0]
    n_rows = lax.axis_size("rows")
    width = 2 * classes
    own = 8
    group = feats_dev // own
    group_count = n_rows // group
    blocks = tuple((2, (lambda row, r=r: r * own,)) for r in range(group))
    info, _, flags, *rows_out = prepare(blocks, splits, logits_t, labels, node_ids, bin_codes)
    members = [[g * group + r for r in range(group)] for g in range(group_count)]
    rows_in = lax.all_to_all(
        jnp.stack(rows_out), "rows", 0, 0, tiled=True, axis_index_groups=members
    )
    hists = []
    for r in range(group):
        held = [hists] if hists else []
        hists = add_rows(
            classes, node_count, own, False, ((0, 0, (0,), (classes,)),), [rows_in[r]], *held
        )
    sums = lax.psum(child_sums(info[:, : half_width(rows_dev)], rows_dev, node_count), ("rows", "feat"))
    side_count = lax.psum(flags, "feat")
    new_logits, leaves = finish(logits_t, node_ids, side_count, sums, node_count)

    cuts = own // pairs_dev
    hist = hists[0][: node_count * width]
    hist = hist.reshape(node_count, width, cuts, pairs_dev, BINS).transpose(0, 2, 3, 4, 1)
    peers = [[g * group + r for g in range(group_count)] for r in range(group)]
    owned = lax.psum_scatter(
        hist.reshape(group_count, pairs_dev, BINS, width),
        "rows",
        scatter_dimension=0,
        axis_index_groups=peers,
    )
    bin_iota = jnp.arange(BINS, dtype=jnp.int32)
    lower_mask = (
        (bin_iota[:, None] < bin_iota[None, :]) & (bin_iota[:, None] < BINS - 1)
    ).astype(jnp.float32)
    left_base = jnp.einsum("pbc,bt->ptc", owned, lower_mask, precision=lax.Precision.HIGHEST)
    node_total = jnp.sum(owned, axis=1, keepdims=True)
    left_miss = left_base + owned[:, BINS - 1 :, :]
    parent_score = split_score(node_total, classes)
    gain_left = (
        split_score(left_miss, classes)
        + split_score(node_total - left_miss, classes)
        - parent_score
    )
    gain_right = (
        split_score(left_base, classes)
        + split_score(node_total - left_base, classes)
        - parent_score
    )
    gain = jnp.concatenate([gain_left, gain_right], axis=1) / (2.0 * classes)
    moves = [
        (n * per_node + cut * group + r, n * per_node + r * cuts + cut)
        for n in range(node_count)
        for cut in range(cuts)
        for r in range(group)
    ]
    gain_rows = lax.ppermute(gain, "rows", moves)
    return (new_logits, gain_rows[None], leaves)


def solution(mesh):
    return jax.shard_map(
        local,
        mesh=mesh,
        in_specs=(P("rows", None), P("rows"), P("rows"), P("rows", "feat"), P(), P(), P()),
        out_specs=(P("rows", None), P("rows", "feat", None), P()),
        check_vma=False,
    )
```

```python
import functools

import jax
import jax.numpy as jnp
from jax import lax
from jax.experimental import pallas as pl
from jax.experimental.pallas import tpu as pltpu
from jax.sharding import PartitionSpec as P

BINS = 64
LANES = 128
VMEM_BYTES = 12 * 1024 * 1024
PREP_VMEM_BYTES = 60 * 1024 * 1024
SMALL_COST = pl.CostEstimate(flops=1000000, bytes_accessed=1000000, transcendentals=0)


reg_lambda = 1.0
step_size = 0.3


def split_score(sums, classes):
    grad_part = sums[..., :classes]
    hess_part = sums[..., classes:]
    return jnp.sum(grad_part * grad_part / (hess_part + reg_lambda), axis=-1)


def three_parts(x):
    first = x.astype(jnp.bfloat16)
    rest = x - first.astype(jnp.float32)
    second = rest.astype(jnp.bfloat16)
    third = (rest - second.astype(jnp.float32)).astype(jnp.bfloat16)
    return first, second, third


def threshold_masks():
    row = lax.broadcasted_iota(jnp.int32, (2 * BINS, 4 * BINS), 0)
    col = lax.broadcasted_iota(jnp.int32, (2 * BINS, 4 * BINS), 1)
    bin_of = row % BINS
    threshold = col % BINS
    first_dir = (col // BINS) % 2 == 0
    below = (bin_of < threshold) & (bin_of < BINS - 1)
    missing = (bin_of == BINS - 1) & first_dir
    same = row // BINS == col // (2 * BINS)
    return jnp.where((below | missing) & same, 1.0, 0.0).astype(jnp.bfloat16)


def half_width(rows):
    return rows // 2 + LANES


def read_info(halves, rows):
    half = rows // 2
    chunks = half // LANES
    prob = jnp.concatenate([info[:, :half] for info in halves], axis=1)
    label, node = (
        jnp.concatenate(
            [info[i : i + 1, half:] for info in halves for i in range(low, low + chunks)], axis=1
        )
        for low in (0, chunks)
    )
    return prob, label, node


def child_sums(info, rows, node_count):
    return info[-node_count:, rows // 2 :]


def prep_kernel(
    own,
    blocks,
    *refs,
):
    operands, rest = refs[:7], refs[7:]
    info_ref, half_ref, flag_ref = rest[:3]
    outs = rest[3 : 3 + len(blocks)]
    turned, *buffers, sems = rest[3 + len(blocks) :]
    copies = [
        pltpu.make_async_copy(operand, buffer, sems.at[i])
        for i, (operand, buffer) in enumerate(zip(operands, buffers))
    ]
    for copy in copies:
        copy.start()
    for copy in copies:
        copy.wait()
    codes_ref, logits_ref, labels_ref, nodes_ref, feature_ref, bin_ref, missing_ref = buffers
    row_index, feat_index = lax.axis_index("rows"), lax.axis_index("feat")
    classes, rows = logits_ref.shape
    half, width = rows // 2, half_width(rows)
    chunks = half // LANES
    turned[...] = codes_ref[...].T
    for (infos, pieces, _), out_ref in zip(blocks, outs):
        if infos == 0 and out_ref.shape[1] > rows:
            out_ref[:, rows:] = jnp.zeros((out_ref.shape[0], out_ref.shape[1] - rows), out_ref.dtype)
        for i, start_of in enumerate(pieces):
            start = pl.multiple_of(start_of(row_index), own)
            if infos == 0:
                out_ref[i * own : (i + 1) * own, :rows] = turned[pl.ds(start, own), :]
                continue
            cut = rows * infos // 2
            for h in range(2 // infos):
                low = classes + (h * len(pieces) + i) * own
                part = turned[pl.ds(start, own), h * cut : (h + 1) * cut]
                out_ref[low : low + own, :cut] = part.astype(out_ref.dtype)
                out_ref[low : low + own, cut:] = jnp.zeros((own, infos * width - cut), out_ref.dtype)
    expo_vals = jnp.exp(logits_ref[...])
    prob = expo_vals / jnp.sum(expo_vals, axis=0, keepdims=True)
    labels = labels_ref[...].astype(jnp.float32)
    nodes = nodes_ref[...].astype(jnp.float32)
    label = jnp.concatenate([labels[i : i + 1] for i in range(2 * chunks)], axis=1)
    node = jnp.concatenate([nodes[i : i + 1] for i in range(2 * chunks)], axis=1)

    feats = turned.shape[0]
    node_count = feature_ref.shape[0]
    side = jnp.zeros((1, rows), jnp.float32)
    for n in range(node_count):
        col = feature_ref[n] - feat_index * feats
        held = (col >= 0) & (col < feats)
        code = turned[pl.ds(jnp.clip(col, 0, feats - 1), 1), :]
        threshold = jnp.where(held, bin_ref[n], -1)
        missing = jnp.where(held & (missing_ref[n] == 1), BINS - 1, -1)
        left = (code < threshold) | (code == missing)
        value = jnp.where(left, 1.0, jnp.where(held, 2.0, 0.0))
        side = jnp.where(node == float(n), value, side)
    flag_ref[...] = jnp.where(side == 2.0, 1.0, 0.0)
    hot = jnp.concatenate(
        [
            jnp.where((node == float(slot // 2)) & (side == float(slot % 2 + 1)), 1.0, 0.0)
            for slot in range(2 * node_count)
        ],
        axis=0,
    ).astype(jnp.bfloat16)
    sums = lax.dot_general(
        hot,
        gradients(prob, label).astype(jnp.bfloat16),
        (((1,), (1,)), ((), ())),
        preferred_element_type=jnp.float32,
    )
    sums = jnp.concatenate([sums[:node_count], sums[node_count:]], axis=1)
    pad = [jnp.zeros((classes - 2 * chunks - node_count, LANES), jnp.float32)]
    pad = pad if pad[0].shape[0] > 0 else []
    for h in range(2):
        some = slice(h * chunks, (h + 1) * chunks)
        info_ref[:, h * width : h * width + half] = prob[:, h * half : (h + 1) * half]
        info_ref[:, h * width + half : (h + 1) * width] = jnp.concatenate(
            [labels[some], nodes[some]] + pad + [sums], axis=0
        )
    half_ref[...] = jnp.where(feat_index == 0, info_ref[:, :width], info_ref[:, width:])
    for (infos, _, _), out_ref in zip(blocks, outs):
        if infos > 0:
            out_ref[:classes, :] = half_ref[...] if infos == 1 else info_ref[...]


def gradients(prob, label):
    class_iota = lax.broadcasted_iota(jnp.int32, prob.shape, 0).astype(jnp.float32)
    target = jnp.where(class_iota == label, 1.0, 0.0)
    return jnp.concatenate([prob - target, prob * (1.0 - prob)], axis=0)


def masked_gradients(halves, rows, node_count):
    prob, label, node = read_info(halves, rows)
    grad_hess = gradients(prob, label)
    return jnp.concatenate(
        [jnp.where(node == float(n), grad_hess, 0.0).astype(jnp.bfloat16) for n in range(node_count)],
        axis=0,
    )


def one_hot(codes):
    feats, rows = codes.shape
    bin_iota = lax.broadcasted_iota(jnp.int32, (BINS, rows), 0).astype(codes.dtype)
    return jnp.concatenate(
        [
            jnp.where(codes[f : f + 1, :] == bin_iota, 1.0, 0.0).astype(jnp.bfloat16)
            for f in range(feats)
        ],
        axis=0,
    )


def write_gains(hist_ref, gain_ref, classes, node_count):
    masks = threshold_masks()
    ones = jnp.where(
        lax.broadcasted_iota(jnp.int32, (2 * BINS, 4 * BINS), 0) < BINS, 1.0, 0.0
    ).astype(jnp.bfloat16)

    def times(parts, right):
        return sum(jnp.dot(part, right, preferred_element_type=jnp.float32) for part in parts)

    total = times(three_parts(hist_ref[:, : 2 * BINS]), ones)
    for pair in range(gain_ref.shape[1] // 2):
        span = slice(pair * 2 * BINS, (pair + 1) * 2 * BINS)
        left = times(three_parts(hist_ref[:, span]), masks)
        right = total - left
        for n in range(node_count):
            grads = slice(n * 2 * classes, n * 2 * classes + classes)
            hesss = slice(n * 2 * classes + classes, (n + 1) * 2 * classes)
            score = (
                left[grads] * left[grads] / (left[hesss] + reg_lambda)
                + right[grads] * right[grads] / (right[hesss] + reg_lambda)
            )
            parent = total[grads] * total[grads] / (total[hesss] + reg_lambda)
            gain = (
                jnp.sum(score, axis=0, keepdims=True) - jnp.sum(parent, axis=0, keepdims=True)
            ) / (2.0 * classes)
            gain_ref[n, 2 * pair : 2 * pair + 1, :] = gain[:, : 2 * BINS]
            gain_ref[n, 2 * pair + 1 : 2 * pair + 2, :] = gain[:, 2 * BINS :]


def add_kernel(classes, node_count, own, plan, carry, *refs):
    outs = len(plan[0][3])
    arrays = 1 + max(max((c,) + i) for _, c, i, _ in plan)
    out_refs = refs[-outs:]
    held_refs = refs[arrays:-outs]
    pairs = 2 * classes * node_count
    row_index, feat_index = lax.axis_index("rows"), lax.axis_index("feat")
    for s, (m, codes_at, info_at, firsts) in enumerate(plan):
        codes_ref = refs[codes_at]
        line = (row_index >> 2) ^ (m >> 2)
        if len(info_at) == 1:
            width = refs[info_at[0]].shape[1] // 2
            low, high = (refs[info_at[0]][:classes, h * width : (h + 1) * width] for h in range(2))
            sums_from = low
        else:
            width = refs[info_at[0]].shape[1]
            near, far = (refs[i][:classes, :] for i in info_at)
            low = jnp.where(feat_index == 0, near, far)
            high = jnp.where(feat_index == 0, far, near)
            sums_from = near
        rows = 2 * (width - LANES)
        masked = masked_gradients((low, high), rows, node_count)
        sums = child_sums(sums_from, rows, node_count)
        for i, first in enumerate(firsts):
            out_ref = out_refs[i]
            if codes_ref.shape[1] < rows:
                second = first + (codes_ref.shape[0] - classes) // 2
                codes = jnp.concatenate(
                    [codes_ref[low : low + own, : rows // 2] for low in (first, second)], axis=1
                )
            else:
                codes = codes_ref[first : first + own, :rows]
            product = lax.dot_general(
                masked,
                one_hot(codes),
                (((1,), (1,)), ((), ())),
                preferred_element_type=jnp.float32,
            )
            if s == 0:
                if held_refs:
                    out_ref[...] = sum(ref[...] for ref in held_refs[i::outs])
                else:
                    out_ref[...] = jnp.zeros(out_ref.shape, out_ref.dtype)
            out_ref[:pairs, :] += product
            if not carry:
                continue
            low_row = pairs + (row_index & 3) * node_count
            band = pl.ds(pl.multiple_of(low_row, node_count), node_count)
            for i in range(out_ref.shape[1] // LANES):
                here = jnp.where(line == i, 1.0, 0.0)
                out_ref[band, i * LANES : (i + 1) * LANES] += here * sums


def add_rows(classes, node_count, own, carry, plan, arrays, *held):
    shape = (2 * classes * node_count + 4 * node_count, own * BINS)
    whole = pl.BlockSpec(memory_space=pltpu.VMEM)
    outs = len(plan[0][3])
    return pl.pallas_call(
        functools.partial(add_kernel, classes, node_count, own, plan, carry),
        in_specs=[whole] * (len(arrays) + len(held) * outs),
        out_specs=[whole] * outs,
        out_shape=[jax.ShapeDtypeStruct(shape, jnp.float32)] * outs,
        compiler_params=pltpu.CompilerParams(vmem_limit_bytes=VMEM_BYTES),
        cost_estimate=SMALL_COST,
    )(*arrays, *[hist for hists in held for hist in hists])


def gain_kernel(classes, node_count, *refs):
    gain_ref, hist_ref = refs[-2:]
    hist_ref[...] = sum(ref[: hist_ref.shape[0], :] for ref in refs[:-2])
    write_gains(hist_ref, gain_ref, classes, node_count)


def swap(x, axis, bit):
    size = lax.axis_size(axis)
    return lax.ppermute(x, axis, [(i, i ^ bit) for i in range(size)])


def sum_over(x, axis):
    bit = 1
    while bit < lax.axis_size(axis):
        x = x + swap(x, axis, bit)
        bit *= 2
    return x


def prepare(blocks, splits, logits_t, labels, node_ids, bin_codes):
    classes, rows_dev = logits_t.shape
    feats_dev = bin_codes.shape[1]
    own = 8
    whole = pl.BlockSpec(memory_space=pltpu.VMEM)
    width = half_width(rows_dev)
    shapes = [
        jax.ShapeDtypeStruct((classes, 2 * width), jnp.float32),
        jax.ShapeDtypeStruct((classes, width), jnp.float32),
        jax.ShapeDtypeStruct((1, rows_dev), jnp.float32),
    ]
    for infos, pieces, spare in blocks:
        codes = len(pieces) * own
        if infos == 0:
            shapes.append(jax.ShapeDtypeStruct((codes, rows_dev + spare), jnp.int32))
        else:
            shape = (classes + codes * 2 // infos, infos * width)
            shapes.append(jax.ShapeDtypeStruct(shape, jnp.float32))
    operands = (
        bin_codes,
        logits_t,
        labels.reshape(-1, LANES),
        node_ids.reshape(-1, LANES),
        *splits,
    )
    spaces = [pltpu.VMEM] * 4 + [pltpu.SMEM] * 3
    return pl.pallas_call(
        functools.partial(prep_kernel, own, blocks),
        in_specs=[pl.BlockSpec(memory_space=pltpu.HBM)] * len(operands),
        out_specs=[whole] * len(shapes),
        out_shape=shapes,
        scratch_shapes=[pltpu.VMEM((feats_dev, rows_dev), jnp.int32)]
        + [space(x.shape, x.dtype) for space, x in zip(spaces, operands)]
        + [pltpu.SemaphoreType.DMA((len(operands),))],
        compiler_params=pltpu.CompilerParams(vmem_limit_bytes=PREP_VMEM_BYTES),
        cost_estimate=SMALL_COST,
    )(*operands)


def finish(logits_t, node_ids, side_count, sums, node_count):
    classes = logits_t.shape[0]
    width = 2 * classes
    side_sums = jnp.concatenate([sums[:, :width], sums[:, width:]], axis=0)
    side_sums = side_sums.reshape(node_count, 2, width)
    leaves = -side_sums[..., :classes] / (side_sums[..., classes:] + reg_lambda)
    row_side = (side_count > 0.5).astype(jnp.int32)
    slot_iota = jnp.arange(2 * node_count, dtype=jnp.int32)
    slot_hot = (node_ids[None, :] * 2 + row_side) == slot_iota[:, None]
    update = jnp.dot(
        leaves.reshape(2 * node_count, classes).T,
        slot_hot.astype(jnp.float32),
        precision=lax.Precision.HIGHEST,
    )
    return (logits_t + step_size * update).T, leaves


def local(logits, labels, node_ids, bin_codes, split_feature, split_bin, split_missing):
    rows_dev, classes = logits.shape
    feats_dev = bin_codes.shape[1]
    node_count = split_feature.shape[0]
    n_rows = lax.axis_size("rows")
    per_node = n_rows // node_count
    pairs_dev = feats_dev // per_node
    width = 2 * classes
    own = 8
    splits = (split_feature, split_bin, split_missing)
    logits_t = logits.T
    if feats_dev != own * n_rows or n_rows != 16 or lax.axis_size("feat") != 2:
        return by_groups(logits_t, labels, node_ids, bin_codes, splits, per_node, pairs_dev)
    add = functools.partial(add_rows, classes, node_count, own, True)

    def start(taker):
        return (taker & 1) * pairs_dev + (taker >> 1) * own

    def quarters(m, which):
        return tuple(lambda row, low=m ^ 3 ^ q: start(row ^ low) for q in which)

    blocks = (
        (0, quarters(0, (0, 1, 2, 3)), 0),
        (1, quarters(4, (0, 1)), 0),
        (0, quarters(8, (0, 1)), 4 * LANES),
        (0, quarters(12, (0, 1)), 4 * LANES),
        (0, quarters(4, (2, 3)), 0),
        (0, quarters(8, (2, 3)), 0),
        (0, quarters(12, (2, 3)), 0),
    )
    info, half, flags, codes_0, rows_4, codes_8, codes_12, late_4, late_8, late_12 = prepare(
        blocks, splits, logits_t, labels, node_ids, bin_codes
    )

    near_8 = swap(half, "rows", 8)
    rows_4 = swap(rows_4, "rows", 4)
    codes_8 = swap(codes_8, "rows", 8)
    codes_12 = swap(codes_12, "rows", 12)
    hist_a, hist_b, hist_c, hist_d = add(
        ((0, 0, (1,), (0, own, 2 * own, 3 * own)),), [codes_0, info]
    )
    near_8, rows_4, hist_a = lax.optimization_barrier((near_8, rows_4, hist_a))
    near_12 = swap(near_8, "rows", 4)
    far_8 = swap(near_8, "feat", 1)
    far_4 = swap(rows_4[:classes], "feat", 1)
    late_4 = swap(late_4, "rows", 4)
    late_8 = swap(late_8, "rows", 8)
    late_12 = swap(late_12, "rows", 12)
    hist_a, hist_b = add(
        ((4, 0, (0, 1), (classes, classes + own)),), [rows_4, far_4], [hist_a, hist_b]
    )
    near_12, codes_8, codes_12, hist_a = lax.optimization_barrier((near_12, codes_8, codes_12, hist_a))
    far_12 = swap(near_12, "feat", 1)
    hist_a, hist_b = add(((8, 0, (1, 2), (0, own)),), [codes_8, near_8, far_8], [hist_a, hist_b])
    (to_core,) = add(((12, 0, (1, 2), (0,)),), [codes_12, near_12, far_12], [hist_a])
    from_core = swap(to_core, "rows", 1)
    (to_plane,) = add(((12, 0, (1, 2), (own,)),), [codes_12, near_12, far_12], [hist_b], [from_core])
    from_plane = swap(to_plane, "rows", 2)
    _, late_4 = lax.optimization_barrier((to_plane, late_4))
    hists = add(((4, 0, (1, 2), (0, own)),), [late_4, rows_4, far_4], [hist_c, hist_d])
    to_core, kept = add(
        ((8, 0, (2, 3), (0, own)), (12, 1, (4, 5), (0, own))),
        [late_8, late_12, near_8, far_8, near_12, far_12],
        hists,
    )
    middle = to_core.shape[0] // 2
    from_core = [swap(part, "rows", 1) for part in (to_core[:middle], to_core[middle:])]
    from_core = jnp.concatenate(from_core, axis=0)

    pairs = node_count * width
    gains = pl.pallas_call(
        functools.partial(gain_kernel, classes, node_count),
        in_specs=[pl.BlockSpec(memory_space=pltpu.VMEM)] * 3,
        out_specs=pl.BlockSpec(memory_space=pltpu.VMEM),
        out_shape=jax.ShapeDtypeStruct((node_count, own, 2 * BINS), jnp.float32),
        scratch_shapes=[pltpu.VMEM((pairs, own * BINS), jnp.float32)],
        compiler_params=pltpu.CompilerParams(vmem_limit_bytes=VMEM_BYTES),
        cost_estimate=SMALL_COST,
    )(from_core, from_plane, kept)
    def gather(parts):
        return jnp.sum(parts.reshape(4, node_count, -1, LANES), axis=(0, 2))

    gains, from_plane = lax.optimization_barrier((gains, from_plane))
    sums = gather(from_core[pairs:] + from_plane[pairs:] + kept[pairs:])
    children = jnp.concatenate([sums, flags.reshape(-1, LANES)], axis=0)
    children = sum_over(children, "feat")
    side_count = children[node_count:].reshape(1, rows_dev)
    sums = children[:node_count]
    new_logits, leaves = finish(logits_t, node_ids, side_count, sums, node_count)

    halves = [[h + n * per_node for n in range(node_count)] for h in range(per_node)]
    gain_rows = lax.all_to_all(gains, "rows", 0, 0, tiled=True, axis_index_groups=halves)
    return (new_logits, gain_rows.reshape(1, pairs_dev, 2 * BINS), leaves)


def by_groups(logits_t, labels, node_ids, bin_codes, splits, per_node, pairs_dev):
    classes, rows_dev = logits_t.shape
    feats_dev = bin_codes.shape[1]
    node_count = splits[0].shape[0]
    n_rows = lax.axis_size("rows")
    width = 2 * classes
    own = 8
    group = feats_dev // own
    group_count = n_rows // group
    blocks = tuple((2, (lambda row, r=r: r * own,), 0) for r in range(group))
    info, _, flags, *rows_out = prepare(blocks, splits, logits_t, labels, node_ids, bin_codes)
    members = [[g * group + r for r in range(group)] for g in range(group_count)]
    rows_in = lax.all_to_all(
        jnp.stack(rows_out), "rows", 0, 0, tiled=True, axis_index_groups=members
    )
    hists = []
    for r in range(group):
        held = [hists] if hists else []
        hists = add_rows(
            classes, node_count, own, False, ((0, 0, (0,), (classes,)),), [rows_in[r]], *held
        )
    sums = lax.psum(child_sums(info[:, : half_width(rows_dev)], rows_dev, node_count), ("rows", "feat"))
    side_count = lax.psum(flags, "feat")
    new_logits, leaves = finish(logits_t, node_ids, side_count, sums, node_count)

    cuts = own // pairs_dev
    hist = hists[0][: node_count * width]
    hist = hist.reshape(node_count, width, cuts, pairs_dev, BINS).transpose(0, 2, 3, 4, 1)
    peers = [[g * group + r for g in range(group_count)] for r in range(group)]
    owned = lax.psum_scatter(
        hist.reshape(group_count, pairs_dev, BINS, width),
        "rows",
        scatter_dimension=0,
        axis_index_groups=peers,
    )
    bin_iota = jnp.arange(BINS, dtype=jnp.int32)
    lower_mask = (
        (bin_iota[:, None] < bin_iota[None, :]) & (bin_iota[:, None] < BINS - 1)
    ).astype(jnp.float32)
    left_base = jnp.einsum("pbc,bt->ptc", owned, lower_mask, precision=lax.Precision.HIGHEST)
    node_total = jnp.sum(owned, axis=1, keepdims=True)
    left_miss = left_base + owned[:, BINS - 1 :, :]
    parent_score = split_score(node_total, classes)
    gain_left = (
        split_score(left_miss, classes)
        + split_score(node_total - left_miss, classes)
        - parent_score
    )
    gain_right = (
        split_score(left_base, classes)
        + split_score(node_total - left_base, classes)
        - parent_score
    )
    gain = jnp.concatenate([gain_left, gain_right], axis=1) / (2.0 * classes)
    moves = [
        (n * per_node + cut * group + r, n * per_node + r * cuts + cut)
        for n in range(node_count)
        for cut in range(cuts)
        for r in range(group)
    ]
    gain_rows = lax.ppermute(gain, "rows", moves)
    return (new_logits, gain_rows[None], leaves)


def solution(mesh):
    return jax.shard_map(
        local,
        mesh=mesh,
        in_specs=(P("rows", None), P("rows"), P("rows"), P("rows", "feat"), P(), P(), P()),
        out_specs=(P("rows", None), P("rows", "feat", None), P()),
        check_vma=False,
    )
```

```python
import functools

import jax
import jax.numpy as jnp
from jax import lax
from jax.experimental import pallas as pl
from jax.experimental.pallas import tpu as pltpu
from jax.sharding import PartitionSpec as P

BINS = 64
LANES = 128
VMEM_BYTES = 12 * 1024 * 1024
PREP_VMEM_BYTES = 60 * 1024 * 1024
SMALL_COST = pl.CostEstimate(flops=1000000, bytes_accessed=1000000, transcendentals=0)


reg_lambda = 1.0
step_size = 0.3


def split_score(sums, classes):
    grad_part = sums[..., :classes]
    hess_part = sums[..., classes:]
    return jnp.sum(grad_part * grad_part / (hess_part + reg_lambda), axis=-1)


def three_parts(x):
    first = x.astype(jnp.bfloat16)
    rest = x - first.astype(jnp.float32)
    second = rest.astype(jnp.bfloat16)
    third = (rest - second.astype(jnp.float32)).astype(jnp.bfloat16)
    return first, second, third


def threshold_masks():
    row = lax.broadcasted_iota(jnp.int32, (2 * BINS, 4 * BINS), 0)
    col = lax.broadcasted_iota(jnp.int32, (2 * BINS, 4 * BINS), 1)
    bin_of = row % BINS
    threshold = col % BINS
    first_dir = (col // BINS) % 2 == 0
    below = (bin_of < threshold) & (bin_of < BINS - 1)
    missing = (bin_of == BINS - 1) & first_dir
    same = row // BINS == col // (2 * BINS)
    return jnp.where((below | missing) & same, 1.0, 0.0).astype(jnp.bfloat16)


def half_width(rows):
    return rows // 2 + LANES


def read_info(halves, rows):
    half = rows // 2
    chunks = half // LANES
    prob = jnp.concatenate([info[:, :half] for info in halves], axis=1)
    label, node = (
        jnp.concatenate(
            [info[i : i + 1, half:] for info in halves for i in range(low, low + chunks)], axis=1
        )
        for low in (0, chunks)
    )
    return prob, label, node


def child_sums(info, rows, node_count):
    return info[-node_count:, rows // 2 :]


def prep_kernel(
    own,
    blocks,
    *refs,
):
    operands, rest = refs[:7], refs[7:]
    info_ref, half_ref, flag_ref = rest[:3]
    outs = rest[3 : 3 + len(blocks)]
    turned, *buffers, sems = rest[3 + len(blocks) :]
    copies = [
        pltpu.make_async_copy(operand, buffer, sems.at[i])
        for i, (operand, buffer) in enumerate(zip(operands, buffers))
    ]
    for copy in copies:
        copy.start()
    for copy in copies:
        copy.wait()
    codes_ref, logits_ref, labels_ref, nodes_ref, feature_ref, bin_ref, missing_ref = buffers
    row_index, feat_index = lax.axis_index("rows"), lax.axis_index("feat")
    classes, rows = logits_ref.shape
    half, width = rows // 2, half_width(rows)
    chunks = half // LANES
    turned[...] = codes_ref[...].T
    for (infos, pieces, _), out_ref in zip(blocks, outs):
        if infos == 0 and out_ref.shape[1] > rows:
            out_ref[:, rows:] = jnp.zeros((out_ref.shape[0], out_ref.shape[1] - rows), out_ref.dtype)
        for i, start_of in enumerate(pieces):
            start = pl.multiple_of(start_of(row_index), own)
            if infos == 0:
                out_ref[i * own : (i + 1) * own, :rows] = turned[pl.ds(start, own), :]
                continue
            cut = rows * infos // 2
            for h in range(2 // infos):
                low = classes + (h * len(pieces) + i) * own
                part = turned[pl.ds(start, own), h * cut : (h + 1) * cut]
                out_ref[low : low + own, :cut] = part.astype(out_ref.dtype)
                out_ref[low : low + own, cut:] = jnp.zeros((own, infos * width - cut), out_ref.dtype)
    expo_vals = jnp.exp(logits_ref[...])
    prob = expo_vals / jnp.sum(expo_vals, axis=0, keepdims=True)
    labels = labels_ref[...].astype(jnp.float32)
    nodes = nodes_ref[...].astype(jnp.float32)
    label = jnp.concatenate([labels[i : i + 1] for i in range(2 * chunks)], axis=1)
    node = jnp.concatenate([nodes[i : i + 1] for i in range(2 * chunks)], axis=1)

    feats = turned.shape[0]
    node_count = feature_ref.shape[0]
    side = jnp.zeros((1, rows), jnp.float32)
    for n in range(node_count):
        col = feature_ref[n] - feat_index * feats
        held = (col >= 0) & (col < feats)
        code = turned[pl.ds(jnp.clip(col, 0, feats - 1), 1), :]
        threshold = jnp.where(held, bin_ref[n], -1)
        missing = jnp.where(held & (missing_ref[n] == 1), BINS - 1, -1)
        left = (code < threshold) | (code == missing)
        value = jnp.where(left, 1.0, jnp.where(held, 2.0, 0.0))
        side = jnp.where(node == float(n), value, side)
    flag_ref[...] = jnp.where(side == 2.0, 1.0, 0.0)
    hot = jnp.concatenate(
        [
            jnp.where((node == float(slot // 2)) & (side == float(slot % 2 + 1)), 1.0, 0.0)
            for slot in range(2 * node_count)
        ],
        axis=0,
    ).astype(jnp.bfloat16)
    sums = lax.dot_general(
        hot,
        gradients(prob, label).astype(jnp.bfloat16),
        (((1,), (1,)), ((), ())),
        preferred_element_type=jnp.float32,
    )
    sums = jnp.concatenate([sums[:node_count], sums[node_count:]], axis=1)
    pad = [jnp.zeros((classes - 2 * chunks - node_count, LANES), jnp.float32)]
    pad = pad if pad[0].shape[0] > 0 else []
    for h in range(2):
        some = slice(h * chunks, (h + 1) * chunks)
        info_ref[:, h * width : h * width + half] = prob[:, h * half : (h + 1) * half]
        info_ref[:, h * width + half : (h + 1) * width] = jnp.concatenate(
            [labels[some], nodes[some]] + pad + [sums], axis=0
        )
    half_ref[...] = jnp.where(feat_index == 0, info_ref[:, :width], info_ref[:, width:])
    for (infos, _, _), out_ref in zip(blocks, outs):
        if infos > 0:
            out_ref[:classes, :] = half_ref[...] if infos == 1 else info_ref[...]


def gradients(prob, label):
    class_iota = lax.broadcasted_iota(jnp.int32, prob.shape, 0).astype(jnp.float32)
    target = jnp.where(class_iota == label, 1.0, 0.0)
    return jnp.concatenate([prob - target, prob * (1.0 - prob)], axis=0)


def masked_gradients(halves, rows, node_count):
    prob, label, node = read_info(halves, rows)
    grad_hess = gradients(prob, label)
    return jnp.concatenate(
        [jnp.where(node == float(n), grad_hess, 0.0).astype(jnp.bfloat16) for n in range(node_count)],
        axis=0,
    )


def one_hot(codes):
    feats, rows = codes.shape
    bin_iota = lax.broadcasted_iota(jnp.int32, (BINS, rows), 0).astype(codes.dtype)
    return jnp.concatenate(
        [
            jnp.where(codes[f : f + 1, :] == bin_iota, 1.0, 0.0).astype(jnp.bfloat16)
            for f in range(feats)
        ],
        axis=0,
    )


def write_gains(hist_ref, gain_ref, classes, node_count):
    masks = threshold_masks()
    ones = jnp.where(
        lax.broadcasted_iota(jnp.int32, (2 * BINS, 4 * BINS), 0) < BINS, 1.0, 0.0
    ).astype(jnp.bfloat16)

    def times(parts, right):
        return sum(jnp.dot(part, right, preferred_element_type=jnp.float32) for part in parts)

    total = times(three_parts(hist_ref[:, : 2 * BINS]), ones)
    for pair in range(gain_ref.shape[1] // 2):
        span = slice(pair * 2 * BINS, (pair + 1) * 2 * BINS)
        left = times(three_parts(hist_ref[:, span]), masks)
        right = total - left
        for n in range(node_count):
            grads = slice(n * 2 * classes, n * 2 * classes + classes)
            hesss = slice(n * 2 * classes + classes, (n + 1) * 2 * classes)
            score = (
                left[grads] * left[grads] / (left[hesss] + reg_lambda)
                + right[grads] * right[grads] / (right[hesss] + reg_lambda)
            )
            parent = total[grads] * total[grads] / (total[hesss] + reg_lambda)
            gain = (
                jnp.sum(score, axis=0, keepdims=True) - jnp.sum(parent, axis=0, keepdims=True)
            ) / (2.0 * classes)
            gain_ref[n, 2 * pair : 2 * pair + 1, :] = gain[:, : 2 * BINS]
            gain_ref[n, 2 * pair + 1 : 2 * pair + 2, :] = gain[:, 2 * BINS :]


def add_kernel(classes, node_count, own, plan, carry, *refs):
    outs = len(plan[0][3])
    arrays = 1 + max(max((c,) + tuple(j for j in i if j is not None)) for _, c, i, _ in plan)
    out_refs = refs[-outs:]
    held_refs = refs[arrays:-outs]
    pairs = 2 * classes * node_count
    row_index, feat_index = lax.axis_index("rows"), lax.axis_index("feat")
    for s, (m, codes_at, info_at, firsts) in enumerate(plan):
        codes_ref = refs[codes_at]
        line = (row_index >> 2) ^ (m >> 2)
        cut = None
        if len(info_at) == 1:
            width = refs[info_at[0]].shape[1] // 2
            halves = [refs[info_at[0]][:classes, h * width : (h + 1) * width] for h in range(2)]
            sums_from = halves[0]
        elif None in info_at:
            near_only = info_at[1] is None
            info_ref = refs[info_at[0] if near_only else info_at[1]]
            width = info_ref.shape[1]
            halves = [info_ref[:classes, :]]
            sums_from = halves[0] if near_only else None
            which = feat_index if near_only else 1 - feat_index
            cut = pl.ds(pl.multiple_of(which * (width - LANES), LANES), width - LANES)
        else:
            width = refs[info_at[0]].shape[1]
            near, far = (refs[i][:classes, :] for i in info_at)
            halves = [
                jnp.where(feat_index == 0, near, far),
                jnp.where(feat_index == 0, far, near),
            ]
            sums_from = near
        rows = 2 * (width - LANES)
        masked = masked_gradients(halves, rows, node_count)
        sums = None if sums_from is None else child_sums(sums_from, rows, node_count)
        for i, first in enumerate(firsts):
            out_ref = out_refs[i]
            if cut is not None:
                codes = codes_ref[first : first + own, cut]
            elif codes_ref.shape[1] < rows:
                second = first + (codes_ref.shape[0] - classes) // 2
                codes = jnp.concatenate(
                    [codes_ref[low : low + own, : rows // 2] for low in (first, second)], axis=1
                )
            else:
                codes = codes_ref[first : first + own, :rows]
            product = lax.dot_general(
                masked,
                one_hot(codes),
                (((1,), (1,)), ((), ())),
                preferred_element_type=jnp.float32,
            )
            if s == 0:
                if held_refs:
                    out_ref[...] = sum(ref[...] for ref in held_refs[i::outs])
                else:
                    out_ref[...] = jnp.zeros(out_ref.shape, out_ref.dtype)
            out_ref[:pairs, :] += product
            if not carry or sums is None:
                continue
            low_row = pairs + (row_index & 3) * node_count
            band = pl.ds(pl.multiple_of(low_row, node_count), node_count)
            for i in range(out_ref.shape[1] // LANES):
                here = jnp.where(line == i, 1.0, 0.0)
                out_ref[band, i * LANES : (i + 1) * LANES] += here * sums


def add_rows(classes, node_count, own, carry, plan, arrays, *held):
    shape = (2 * classes * node_count + 4 * node_count, own * BINS)
    whole = pl.BlockSpec(memory_space=pltpu.VMEM)
    outs = len(plan[0][3])
    return pl.pallas_call(
        functools.partial(add_kernel, classes, node_count, own, plan, carry),
        in_specs=[whole] * (len(arrays) + len(held) * outs),
        out_specs=[whole] * outs,
        out_shape=[jax.ShapeDtypeStruct(shape, jnp.float32)] * outs,
        compiler_params=pltpu.CompilerParams(vmem_limit_bytes=VMEM_BYTES),
        cost_estimate=SMALL_COST,
    )(*arrays, *[hist for hists in held for hist in hists])


def gain_kernel(classes, node_count, *refs):
    gain_ref, hist_ref = refs[-2:]
    out_refs = refs[-2 - node_count : -2]
    hist_ref[...] = sum(ref[: hist_ref.shape[0], :] for ref in refs[: -2 - node_count])
    write_gains(hist_ref, gain_ref, classes, node_count)
    for i, out_ref in enumerate(out_refs):
        out_ref[...] = gain_ref[(lax.axis_index("rows") >> 1) ^ i]


def place_kernel(*refs):
    out_ref = refs[-1]
    own = refs[0].shape[0]
    for i, ref in enumerate(refs[:-1]):
        start = ((lax.axis_index("rows") >> 1) ^ i) * own
        out_ref[0, pl.ds(pl.multiple_of(start, own), own), :] = ref[...]


def swap(x, axis, bit):
    size = lax.axis_size(axis)
    return lax.ppermute(x, axis, [(i, i ^ bit) for i in range(size)])


def sum_over(x, axis):
    bit = 1
    while bit < lax.axis_size(axis):
        x = x + swap(x, axis, bit)
        bit *= 2
    return x


def prepare(blocks, splits, logits_t, labels, node_ids, bin_codes):
    classes, rows_dev = logits_t.shape
    feats_dev = bin_codes.shape[1]
    own = 8
    whole = pl.BlockSpec(memory_space=pltpu.VMEM)
    width = half_width(rows_dev)
    shapes = [
        jax.ShapeDtypeStruct((classes, 2 * width), jnp.float32),
        jax.ShapeDtypeStruct((classes, width), jnp.float32),
        jax.ShapeDtypeStruct((1, rows_dev), jnp.float32),
    ]
    for infos, pieces, spare in blocks:
        codes = len(pieces) * own
        if infos == 0:
            shapes.append(jax.ShapeDtypeStruct((codes, rows_dev + spare), jnp.int32))
        else:
            shape = (classes + codes * 2 // infos, infos * width)
            shapes.append(jax.ShapeDtypeStruct(shape, jnp.float32))
    operands = (
        bin_codes,
        logits_t,
        labels.reshape(-1, LANES),
        node_ids.reshape(-1, LANES),
        *splits,
    )
    spaces = [pltpu.VMEM] * 4 + [pltpu.SMEM] * 3
    return pl.pallas_call(
        functools.partial(prep_kernel, own, blocks),
        in_specs=[pl.BlockSpec(memory_space=pltpu.HBM)] * len(operands),
        out_specs=[whole] * len(shapes),
        out_shape=shapes,
        scratch_shapes=[pltpu.VMEM((feats_dev, rows_dev), jnp.int32)]
        + [space(x.shape, x.dtype) for space, x in zip(spaces, operands)]
        + [pltpu.SemaphoreType.DMA((len(operands),))],
        compiler_params=pltpu.CompilerParams(vmem_limit_bytes=PREP_VMEM_BYTES),
        cost_estimate=SMALL_COST,
    )(*operands)


def finish(logits_t, node_ids, side_count, sums, node_count):
    classes = logits_t.shape[0]
    width = 2 * classes
    side_sums = jnp.concatenate([sums[:, :width], sums[:, width:]], axis=0)
    side_sums = side_sums.reshape(node_count, 2, width)
    leaves = -side_sums[..., :classes] / (side_sums[..., classes:] + reg_lambda)
    row_side = (side_count > 0.5).astype(jnp.int32)
    slot_iota = jnp.arange(2 * node_count, dtype=jnp.int32)
    slot_hot = (node_ids[None, :] * 2 + row_side) == slot_iota[:, None]
    update = jnp.dot(
        leaves.reshape(2 * node_count, classes).T,
        slot_hot.astype(jnp.float32),
        precision=lax.Precision.HIGHEST,
    )
    return (logits_t + step_size * update).T, leaves


def local(logits, labels, node_ids, bin_codes, split_feature, split_bin, split_missing):
    rows_dev, classes = logits.shape
    feats_dev = bin_codes.shape[1]
    node_count = split_feature.shape[0]
    n_rows = lax.axis_size("rows")
    per_node = n_rows // node_count
    pairs_dev = feats_dev // per_node
    width = 2 * classes
    own = 8
    splits = (split_feature, split_bin, split_missing)
    logits_t = logits.T
    if feats_dev != own * n_rows or n_rows != 16 or lax.axis_size("feat") != 2:
        return by_groups(logits_t, labels, node_ids, bin_codes, splits, per_node, pairs_dev)
    add = functools.partial(add_rows, classes, node_count, own, True)

    def start(taker):
        return (taker & 1) * pairs_dev + (taker >> 1) * own

    def quarters(m, which):
        return tuple(lambda row, low=m ^ 3 ^ q: start(row ^ low) for q in which)

    blocks = (
        (0, quarters(0, (0, 1, 2, 3)), 0),
        (1, quarters(4, (0, 1)), 0),
        (0, quarters(8, (0, 1)), 4 * LANES),
        (0, quarters(12, (0, 1)), 4 * LANES),
        (0, quarters(4, (2, 3)), 0),
        (0, quarters(8, (2, 3)), 0),
        (0, quarters(12, (2, 3)), 0),
    )
    info, half, flags, codes_0, rows_4, codes_8, codes_12, late_4, late_8, late_12 = prepare(
        blocks, splits, logits_t, labels, node_ids, bin_codes
    )

    near_8 = swap(half, "rows", 8)
    rows_4 = swap(rows_4, "rows", 4)
    codes_8 = swap(codes_8, "rows", 8)
    codes_12 = swap(codes_12, "rows", 12)
    hist_a, hist_b, hist_c, hist_d = add(
        ((0, 0, (1,), (0, own, 2 * own, 3 * own)),), [codes_0, info]
    )
    near_8, rows_4, hist_a = lax.optimization_barrier((near_8, rows_4, hist_a))
    near_12 = swap(near_8, "rows", 4)
    far_8 = swap(near_8, "feat", 1)
    far_4 = swap(rows_4[:classes], "feat", 1)
    late_4 = swap(late_4, "rows", 4)
    late_8 = swap(late_8, "rows", 8)
    late_12 = swap(late_12, "rows", 12)
    hist_a, hist_b = add(
        ((4, 0, (0, 1), (classes, classes + own)),), [rows_4, far_4], [hist_a, hist_b]
    )
    near_12, codes_8, codes_12, hist_a = lax.optimization_barrier((near_12, codes_8, codes_12, hist_a))
    far_12 = swap(near_12, "feat", 1)
    hist_a, hist_b = add(((8, 0, (1, 2), (0, own)),), [codes_8, near_8, far_8], [hist_a, hist_b])
    hist_a, hist_b = add(((12, 0, (1, None), (0, own)),), [codes_12, near_12], [hist_a, hist_b])
    (to_core,) = add(((12, 0, (None, 1), (0,)),), [codes_12, far_12], [hist_a])
    from_core = swap(to_core, "rows", 1)
    (to_plane,) = add(((12, 0, (None, 1), (own,)),), [codes_12, far_12], [hist_b], [from_core])
    from_plane = swap(to_plane, "rows", 2)
    _, late_4 = lax.optimization_barrier((to_plane, late_4))
    hists = add(((4, 0, (1, 2), (0, own)),), [late_4, rows_4, far_4], [hist_c, hist_d])
    hists = add(((8, 0, (1, 2), (0, own)),), [late_8, near_8, far_8], hists)
    to_core, kept = add(((12, 0, (1, 2), (0, own)),), [late_12, near_12, far_12], hists)
    middle = to_core.shape[0] // 2
    from_core = [swap(part, "rows", 1) for part in (to_core[:middle], to_core[middle:])]
    from_core = jnp.concatenate(from_core, axis=0)

    pairs = node_count * width
    whole = pl.BlockSpec(memory_space=pltpu.VMEM)
    gains = pl.pallas_call(
        functools.partial(gain_kernel, classes, node_count),
        in_specs=[whole] * 3,
        out_specs=[whole] * node_count,
        out_shape=[jax.ShapeDtypeStruct((own, 2 * BINS), jnp.float32)] * node_count,
        scratch_shapes=[
            pltpu.VMEM((node_count, own, 2 * BINS), jnp.float32),
            pltpu.VMEM((pairs, own * BINS), jnp.float32),
        ],
        compiler_params=pltpu.CompilerParams(vmem_limit_bytes=VMEM_BYTES),
        cost_estimate=SMALL_COST,
    )(from_core, from_plane, kept)
    def gather(parts):
        return jnp.sum(parts.reshape(4, node_count, -1, LANES), axis=(0, 2))

    gains, from_plane = lax.optimization_barrier((gains, from_plane))
    sums = gather(from_core[pairs:] + from_plane[pairs:] + kept[pairs:])
    children = jnp.concatenate([sums, flags.reshape(-1, LANES)], axis=0)
    children = sum_over(children, "feat")
    side_count = children[node_count:].reshape(1, rows_dev)
    sums = children[:node_count]
    new_logits, leaves = finish(logits_t, node_ids, side_count, sums, node_count)

    gains = [gains[0]] + [swap(gains[i], "rows", 2 * i) for i in range(1, node_count)]
    gains, new_logits = lax.optimization_barrier((gains, new_logits))
    gain_rows = pl.pallas_call(
        place_kernel,
        in_specs=[whole] * node_count,
        out_specs=whole,
        out_shape=jax.ShapeDtypeStruct((1, pairs_dev, 2 * BINS), jnp.float32),
        compiler_params=pltpu.CompilerParams(vmem_limit_bytes=VMEM_BYTES),
        cost_estimate=SMALL_COST,
    )(*gains)
    return (new_logits, gain_rows, leaves)


def by_groups(logits_t, labels, node_ids, bin_codes, splits, per_node, pairs_dev):
    classes, rows_dev = logits_t.shape
    feats_dev = bin_codes.shape[1]
    node_count = splits[0].shape[0]
    n_rows = lax.axis_size("rows")
    width = 2 * classes
    own = 8
    group = feats_dev // own
    group_count = n_rows // group
    blocks = tuple((2, (lambda row, r=r: r * own,), 0) for r in range(group))
    info, _, flags, *rows_out = prepare(blocks, splits, logits_t, labels, node_ids, bin_codes)
    members = [[g * group + r for r in range(group)] for g in range(group_count)]
    rows_in = lax.all_to_all(
        jnp.stack(rows_out), "rows", 0, 0, tiled=True, axis_index_groups=members
    )
    hists = []
    for r in range(group):
        held = [hists] if hists else []
        hists = add_rows(
            classes, node_count, own, False, ((0, 0, (0,), (classes,)),), [rows_in[r]], *held
        )
    sums = lax.psum(child_sums(info[:, : half_width(rows_dev)], rows_dev, node_count), ("rows", "feat"))
    side_count = lax.psum(flags, "feat")
    new_logits, leaves = finish(logits_t, node_ids, side_count, sums, node_count)

    cuts = own // pairs_dev
    hist = hists[0][: node_count * width]
    hist = hist.reshape(node_count, width, cuts, pairs_dev, BINS).transpose(0, 2, 3, 4, 1)
    peers = [[g * group + r for g in range(group_count)] for r in range(group)]
    owned = lax.psum_scatter(
        hist.reshape(group_count, pairs_dev, BINS, width),
        "rows",
        scatter_dimension=0,
        axis_index_groups=peers,
    )
    bin_iota = jnp.arange(BINS, dtype=jnp.int32)
    lower_mask = (
        (bin_iota[:, None] < bin_iota[None, :]) & (bin_iota[:, None] < BINS - 1)
    ).astype(jnp.float32)
    left_base = jnp.einsum("pbc,bt->ptc", owned, lower_mask, precision=lax.Precision.HIGHEST)
    node_total = jnp.sum(owned, axis=1, keepdims=True)
    left_miss = left_base + owned[:, BINS - 1 :, :]
    parent_score = split_score(node_total, classes)
    gain_left = (
        split_score(left_miss, classes)
        + split_score(node_total - left_miss, classes)
        - parent_score
    )
    gain_right = (
        split_score(left_base, classes)
        + split_score(node_total - left_base, classes)
        - parent_score
    )
    gain = jnp.concatenate([gain_left, gain_right], axis=1) / (2.0 * classes)
    moves = [
        (n * per_node + cut * group + r, n * per_node + r * cuts + cut)
        for n in range(node_count)
        for cut in range(cuts)
        for r in range(group)
    ]
    gain_rows = lax.ppermute(gain, "rows", moves)
    return (new_logits, gain_rows[None], leaves)


def solution(mesh):
    return jax.shard_map(
        local,
        mesh=mesh,
        in_specs=(P("rows", None), P("rows"), P("rows"), P("rows", "feat"), P(), P(), P()),
        out_specs=(P("rows", None), P("rows", "feat", None), P()),
        check_vma=False,
    )
```

```python
import functools

import jax
import jax.numpy as jnp
from jax import lax
from jax.experimental import pallas as pl
from jax.experimental.pallas import tpu as pltpu
from jax.sharding import PartitionSpec as P

BINS = 64
LANES = 128
VMEM_BYTES = 12 * 1024 * 1024
PREP_VMEM_BYTES = 60 * 1024 * 1024
SMALL_COST = pl.CostEstimate(flops=1000000, bytes_accessed=1000000, transcendentals=0)


reg_lambda = 1.0
step_size = 0.3


def split_score(sums, classes):
    grad_part = sums[..., :classes]
    hess_part = sums[..., classes:]
    return jnp.sum(grad_part * grad_part / (hess_part + reg_lambda), axis=-1)


def three_parts(x):
    first = x.astype(jnp.bfloat16)
    rest = x - first.astype(jnp.float32)
    second = rest.astype(jnp.bfloat16)
    third = (rest - second.astype(jnp.float32)).astype(jnp.bfloat16)
    return first, second, third


def threshold_masks():
    row = lax.broadcasted_iota(jnp.int32, (2 * BINS, 4 * BINS), 0)
    col = lax.broadcasted_iota(jnp.int32, (2 * BINS, 4 * BINS), 1)
    bin_of = row % BINS
    threshold = col % BINS
    first_dir = (col // BINS) % 2 == 0
    below = (bin_of < threshold) & (bin_of < BINS - 1)
    missing = (bin_of == BINS - 1) & first_dir
    same = row // BINS == col // (2 * BINS)
    return jnp.where((below | missing) & same, 1.0, 0.0).astype(jnp.bfloat16)


def half_width(rows):
    return rows // 2 + LANES


def read_info(halves, rows):
    half = rows // 2
    chunks = half // LANES
    prob = jnp.concatenate([info[:, :half] for info in halves], axis=1)
    label, node = (
        jnp.concatenate(
            [info[i : i + 1, half:] for info in halves for i in range(low, low + chunks)], axis=1
        )
        for low in (0, chunks)
    )
    return prob, label, node


def child_sums(info, rows, node_count):
    return info[-node_count:, rows // 2 :]


def prep_kernel(
    own,
    blocks,
    *refs,
):
    operands, rest = refs[:7], refs[7:]
    info_ref, half_ref, flag_ref = rest[:3]
    outs = rest[3 : 3 + len(blocks)]
    turned, *buffers, sems = rest[3 + len(blocks) :]
    copies = [
        pltpu.make_async_copy(operand, buffer, sems.at[i])
        for i, (operand, buffer) in enumerate(zip(operands, buffers))
    ]
    for copy in copies:
        copy.start()
    for copy in copies:
        copy.wait()
    codes_ref, logits_ref, labels_ref, nodes_ref, feature_ref, bin_ref, missing_ref = buffers
    row_index, feat_index = lax.axis_index("rows"), lax.axis_index("feat")
    classes, rows = logits_ref.shape
    half, width = rows // 2, half_width(rows)
    chunks = half // LANES
    turned[...] = codes_ref[...].T
    for (infos, pieces, _), out_ref in zip(blocks, outs):
        if infos == 0 and out_ref.shape[1] > rows:
            out_ref[:, rows:] = jnp.zeros((out_ref.shape[0], out_ref.shape[1] - rows), out_ref.dtype)
        for i, start_of in enumerate(pieces):
            start = pl.multiple_of(start_of(row_index), own)
            if infos == 0:
                out_ref[i * own : (i + 1) * own, :rows] = turned[pl.ds(start, own), :]
                continue
            cut = rows * infos // 2
            for h in range(2 // infos):
                low = classes + (h * len(pieces) + i) * own
                part = turned[pl.ds(start, own), h * cut : (h + 1) * cut]
                out_ref[low : low + own, :cut] = part.astype(out_ref.dtype)
                out_ref[low : low + own, cut:] = jnp.zeros((own, infos * width - cut), out_ref.dtype)
    expo_vals = jnp.exp(logits_ref[...])
    prob = expo_vals / jnp.sum(expo_vals, axis=0, keepdims=True)
    labels = labels_ref[...].astype(jnp.float32)
    nodes = nodes_ref[...].astype(jnp.float32)
    label = jnp.concatenate([labels[i : i + 1] for i in range(2 * chunks)], axis=1)
    node = jnp.concatenate([nodes[i : i + 1] for i in range(2 * chunks)], axis=1)

    feats = turned.shape[0]
    node_count = feature_ref.shape[0]
    side = jnp.zeros((1, rows), jnp.float32)
    for n in range(node_count):
        col = feature_ref[n] - feat_index * feats
        held = (col >= 0) & (col < feats)
        code = turned[pl.ds(jnp.clip(col, 0, feats - 1), 1), :]
        threshold = jnp.where(held, bin_ref[n], -1)
        missing = jnp.where(held & (missing_ref[n] == 1), BINS - 1, -1)
        left = (code < threshold) | (code == missing)
        value = jnp.where(left, 1.0, jnp.where(held, 2.0, 0.0))
        side = jnp.where(node == float(n), value, side)
    flag_ref[...] = jnp.where(side == 2.0, 1.0, 0.0)
    hot = jnp.concatenate(
        [
            jnp.where((node == float(slot // 2)) & (side == float(slot % 2 + 1)), 1.0, 0.0)
            for slot in range(2 * node_count)
        ],
        axis=0,
    ).astype(jnp.bfloat16)
    sums = lax.dot_general(
        hot,
        gradients(prob, label).astype(jnp.bfloat16),
        (((1,), (1,)), ((), ())),
        preferred_element_type=jnp.float32,
    )
    sums = jnp.concatenate([sums[:node_count], sums[node_count:]], axis=1)
    pad = [jnp.zeros((classes - 2 * chunks - node_count, LANES), jnp.float32)]
    pad = pad if pad[0].shape[0] > 0 else []
    for h in range(2):
        some = slice(h * chunks, (h + 1) * chunks)
        info_ref[:, h * width : h * width + half] = prob[:, h * half : (h + 1) * half]
        info_ref[:, h * width + half : (h + 1) * width] = jnp.concatenate(
            [labels[some], nodes[some]] + pad + [sums], axis=0
        )
    half_ref[...] = jnp.where(feat_index == 0, info_ref[:, :width], info_ref[:, width:])
    for (infos, _, _), out_ref in zip(blocks, outs):
        if infos > 0:
            out_ref[:classes, :] = half_ref[...] if infos == 1 else info_ref[...]


def gradients(prob, label):
    class_iota = lax.broadcasted_iota(jnp.int32, prob.shape, 0).astype(jnp.float32)
    target = jnp.where(class_iota == label, 1.0, 0.0)
    return jnp.concatenate([prob - target, prob * (1.0 - prob)], axis=0)


def masked_gradients(halves, rows, node_count):
    prob, label, node = read_info(halves, rows)
    grad_hess = gradients(prob, label)
    return jnp.concatenate(
        [jnp.where(node == float(n), grad_hess, 0.0).astype(jnp.bfloat16) for n in range(node_count)],
        axis=0,
    )


def one_hot(codes):
    feats, rows = codes.shape
    bin_iota = lax.broadcasted_iota(jnp.int32, (BINS, rows), 0).astype(codes.dtype)
    return jnp.concatenate(
        [
            jnp.where(codes[f : f + 1, :] == bin_iota, 1.0, 0.0).astype(jnp.bfloat16)
            for f in range(feats)
        ],
        axis=0,
    )


def write_gains(hist_ref, gain_ref, classes, node_count):
    masks = threshold_masks()
    ones = jnp.where(
        lax.broadcasted_iota(jnp.int32, (2 * BINS, 4 * BINS), 0) < BINS, 1.0, 0.0
    ).astype(jnp.bfloat16)

    def times(parts, right):
        return sum(jnp.dot(part, right, preferred_element_type=jnp.float32) for part in parts)

    total = times(three_parts(hist_ref[:, : 2 * BINS]), ones)
    for pair in range(gain_ref.shape[1] // 2):
        span = slice(pair * 2 * BINS, (pair + 1) * 2 * BINS)
        left = times(three_parts(hist_ref[:, span]), masks)
        right = total - left
        for n in range(node_count):
            grads = slice(n * 2 * classes, n * 2 * classes + classes)
            hesss = slice(n * 2 * classes + classes, (n + 1) * 2 * classes)
            score = (
                left[grads] * left[grads] / (left[hesss] + reg_lambda)
                + right[grads] * right[grads] / (right[hesss] + reg_lambda)
            )
            parent = total[grads] * total[grads] / (total[hesss] + reg_lambda)
            gain = (
                jnp.sum(score, axis=0, keepdims=True) - jnp.sum(parent, axis=0, keepdims=True)
            ) / (2.0 * classes)
            gain_ref[n, 2 * pair : 2 * pair + 1, :] = gain[:, : 2 * BINS]
            gain_ref[n, 2 * pair + 1 : 2 * pair + 2, :] = gain[:, 2 * BINS :]


def add_kernel(classes, node_count, own, plan, carry, *refs):
    outs = len(plan[0][3])
    arrays = 1 + max(max((c,) + tuple(j for j in i if j is not None)) for _, c, i, _ in plan)
    out_refs = refs[-outs:]
    held_refs = refs[arrays:-outs]
    pairs = 2 * classes * node_count
    row_index, feat_index = lax.axis_index("rows"), lax.axis_index("feat")
    for s, (m, codes_at, info_at, firsts) in enumerate(plan):
        codes_ref = refs[codes_at]
        line = (row_index >> 2) ^ (m >> 2)
        cut = None
        if len(info_at) == 1:
            width = refs[info_at[0]].shape[1] // 2
            halves = [refs[info_at[0]][:classes, h * width : (h + 1) * width] for h in range(2)]
            sums_from = halves[0]
        elif None in info_at:
            near_only = info_at[1] is None
            info_ref = refs[info_at[0] if near_only else info_at[1]]
            width = info_ref.shape[1]
            halves = [info_ref[:classes, :]]
            sums_from = halves[0] if near_only else None
            which = feat_index if near_only else 1 - feat_index
            cut = pl.ds(pl.multiple_of(which * (width - LANES), LANES), width - LANES)
        else:
            width = refs[info_at[0]].shape[1]
            near, far = (refs[i][:classes, :] for i in info_at)
            halves = [
                jnp.where(feat_index == 0, near, far),
                jnp.where(feat_index == 0, far, near),
            ]
            sums_from = near
        rows = 2 * (width - LANES)
        masked = masked_gradients(halves, rows, node_count)
        sums = None if sums_from is None else child_sums(sums_from, rows, node_count)
        for i, first in enumerate(firsts):
            out_ref = out_refs[i]
            if cut is not None:
                codes = codes_ref[first : first + own, cut]
            elif codes_ref.shape[1] < rows:
                second = first + (codes_ref.shape[0] - classes) // 2
                codes = jnp.concatenate(
                    [codes_ref[low : low + own, : rows // 2] for low in (first, second)], axis=1
                )
            else:
                codes = codes_ref[first : first + own, :rows]
            product = lax.dot_general(
                masked,
                one_hot(codes),
                (((1,), (1,)), ((), ())),
                preferred_element_type=jnp.float32,
            )
            if s == 0:
                if held_refs:
                    out_ref[...] = sum(ref[...] for ref in held_refs[i::outs])
                else:
                    out_ref[...] = jnp.zeros(out_ref.shape, out_ref.dtype)
            out_ref[:pairs, :] += product
            if not carry or sums is None:
                continue
            low_row = pairs + (row_index & 3) * node_count
            band = pl.ds(pl.multiple_of(low_row, node_count), node_count)
            for i in range(out_ref.shape[1] // LANES):
                here = jnp.where(line == i, 1.0, 0.0)
                out_ref[band, i * LANES : (i + 1) * LANES] += here * sums


def add_rows(classes, node_count, own, carry, plan, arrays, *held):
    shape = (2 * classes * node_count + 4 * node_count, own * BINS)
    whole = pl.BlockSpec(memory_space=pltpu.VMEM)
    outs = len(plan[0][3])
    return pl.pallas_call(
        functools.partial(add_kernel, classes, node_count, own, plan, carry),
        in_specs=[whole] * (len(arrays) + len(held) * outs),
        out_specs=[whole] * outs,
        out_shape=[jax.ShapeDtypeStruct(shape, jnp.float32)] * outs,
        compiler_params=pltpu.CompilerParams(vmem_limit_bytes=VMEM_BYTES),
        cost_estimate=SMALL_COST,
    )(*arrays, *[hist for hists in held for hist in hists])


def gain_kernel(classes, node_count, *refs):
    gain_ref, hist_ref = refs[-2:]
    hist_ref[...] = sum(ref[: hist_ref.shape[0], :] for ref in refs[:-2])
    write_gains(hist_ref, gain_ref, classes, node_count)


def swap(x, axis, bit):
    size = lax.axis_size(axis)
    return lax.ppermute(x, axis, [(i, i ^ bit) for i in range(size)])


def sum_over(x, axis):
    bit = 1
    while bit < lax.axis_size(axis):
        x = x + swap(x, axis, bit)
        bit *= 2
    return x


def prepare(blocks, splits, logits_t, labels, node_ids, bin_codes):
    classes, rows_dev = logits_t.shape
    feats_dev = bin_codes.shape[1]
    own = 8
    whole = pl.BlockSpec(memory_space=pltpu.VMEM)
    width = half_width(rows_dev)
    shapes = [
        jax.ShapeDtypeStruct((classes, 2 * width), jnp.float32),
        jax.ShapeDtypeStruct((classes, width), jnp.float32),
        jax.ShapeDtypeStruct((1, rows_dev), jnp.float32),
    ]
    for infos, pieces, spare in blocks:
        codes = len(pieces) * own
        if infos == 0:
            shapes.append(jax.ShapeDtypeStruct((codes, rows_dev + spare), jnp.int32))
        else:
            shape = (classes + codes * 2 // infos, infos * width)
            shapes.append(jax.ShapeDtypeStruct(shape, jnp.float32))
    operands = (
        bin_codes,
        logits_t,
        labels.reshape(-1, LANES),
        node_ids.reshape(-1, LANES),
        *splits,
    )
    spaces = [pltpu.VMEM] * 4 + [pltpu.SMEM] * 3
    return pl.pallas_call(
        functools.partial(prep_kernel, own, blocks),
        in_specs=[pl.BlockSpec(memory_space=pltpu.HBM)] * len(operands),
        out_specs=[whole] * len(shapes),
        out_shape=shapes,
        scratch_shapes=[pltpu.VMEM((feats_dev, rows_dev), jnp.int32)]
        + [space(x.shape, x.dtype) for space, x in zip(spaces, operands)]
        + [pltpu.SemaphoreType.DMA((len(operands),))],
        compiler_params=pltpu.CompilerParams(vmem_limit_bytes=PREP_VMEM_BYTES),
        cost_estimate=SMALL_COST,
    )(*operands)


def finish(logits_t, node_ids, side_count, sums, node_count):
    classes = logits_t.shape[0]
    width = 2 * classes
    side_sums = jnp.concatenate([sums[:, :width], sums[:, width:]], axis=0)
    side_sums = side_sums.reshape(node_count, 2, width)
    leaves = -side_sums[..., :classes] / (side_sums[..., classes:] + reg_lambda)
    row_side = (side_count > 0.5).astype(jnp.int32)
    slot_iota = jnp.arange(2 * node_count, dtype=jnp.int32)
    slot_hot = (node_ids[None, :] * 2 + row_side) == slot_iota[:, None]
    update = jnp.dot(
        leaves.reshape(2 * node_count, classes).T,
        slot_hot.astype(jnp.float32),
        precision=lax.Precision.HIGHEST,
    )
    return (logits_t + step_size * update).T, leaves


def local(logits, labels, node_ids, bin_codes, split_feature, split_bin, split_missing):
    rows_dev, classes = logits.shape
    feats_dev = bin_codes.shape[1]
    node_count = split_feature.shape[0]
    n_rows = lax.axis_size("rows")
    per_node = n_rows // node_count
    pairs_dev = feats_dev // per_node
    width = 2 * classes
    own = 8
    splits = (split_feature, split_bin, split_missing)
    logits_t = logits.T
    if feats_dev != own * n_rows or n_rows != 16 or lax.axis_size("feat") != 2:
        return by_groups(logits_t, labels, node_ids, bin_codes, splits, per_node, pairs_dev)
    add = functools.partial(add_rows, classes, node_count, own, True)

    def start(taker):
        return (taker & 1) * pairs_dev + (taker >> 1) * own

    def quarters(m, which):
        return tuple(lambda row, low=m ^ 3 ^ q: start(row ^ low) for q in which)

    blocks = (
        (0, quarters(0, (0, 1, 2, 3)), 0),
        (1, quarters(4, (0, 1)), 0),
        (0, quarters(8, (0, 1)), 3 * LANES),
        (0, quarters(12, (0, 1)), 3 * LANES),
        (0, quarters(4, (2, 3)), 0),
        (0, quarters(8, (2, 3)), 0),
        (0, quarters(12, (2, 3)), 0),
    )
    info, half, flags, codes_0, rows_4, codes_8, codes_12, late_4, late_8, late_12 = prepare(
        blocks, splits, logits_t, labels, node_ids, bin_codes
    )

    near_8 = swap(half, "rows", 8)
    rows_4 = swap(rows_4, "rows", 4)
    codes_8 = swap(codes_8, "rows", 8)
    codes_12 = swap(codes_12, "rows", 12)
    hist_a, hist_b, hist_c, hist_d = add(
        ((0, 0, (1,), (0, own, 2 * own, 3 * own)),), [codes_0, info]
    )
    near_8, rows_4, hist_a = lax.optimization_barrier((near_8, rows_4, hist_a))
    near_12 = swap(near_8, "rows", 4)
    far_8 = swap(near_8, "feat", 1)
    far_4 = swap(rows_4[:classes], "feat", 1)
    late_4 = swap(late_4, "rows", 4)
    late_8 = swap(late_8, "rows", 8)
    late_12 = swap(late_12, "rows", 12)
    hist_a, hist_b = add(
        ((4, 0, (0, 1), (classes, classes + own)),), [rows_4, far_4], [hist_a, hist_b]
    )
    near_12, codes_8, codes_12, hist_a = lax.optimization_barrier((near_12, codes_8, codes_12, hist_a))
    far_12 = swap(near_12, "feat", 1)
    hist_a, hist_b = add(((8, 0, (1, 2), (0, own)),), [codes_8, near_8, far_8], [hist_a, hist_b])
    hist_a, hist_b = add(((12, 0, (1, None), (0, own)),), [codes_12, near_12], [hist_a, hist_b])
    (to_core,) = add(((12, 0, (None, 1), (0,)),), [codes_12, far_12], [hist_a])
    from_core = swap(to_core, "rows", 1)
    (to_plane,) = add(((12, 0, (None, 1), (own,)),), [codes_12, far_12], [hist_b], [from_core])
    from_plane = swap(to_plane, "rows", 2)
    _, late_4 = lax.optimization_barrier((to_plane, late_4))
    hists = add(((4, 0, (1, 2), (0, own)),), [late_4, rows_4, far_4], [hist_c, hist_d])
    hists = add(((8, 0, (1, 2), (0, own)),), [late_8, near_8, far_8], hists)
    to_core, kept = add(((12, 0, (1, 2), (0, own)),), [late_12, near_12, far_12], hists)
    middle = to_core.shape[0] // 2
    from_core = [swap(part, "rows", 1) for part in (to_core[:middle], to_core[middle:])]
    from_core = jnp.concatenate(from_core, axis=0)

    pairs = node_count * width
    gains = pl.pallas_call(
        functools.partial(gain_kernel, classes, node_count),
        in_specs=[pl.BlockSpec(memory_space=pltpu.VMEM)] * 3,
        out_specs=pl.BlockSpec(memory_space=pltpu.VMEM),
        out_shape=jax.ShapeDtypeStruct((node_count, own, 2 * BINS), jnp.float32),
        scratch_shapes=[pltpu.VMEM((pairs, own * BINS), jnp.float32)],
        compiler_params=pltpu.CompilerParams(vmem_limit_bytes=VMEM_BYTES),
        cost_estimate=SMALL_COST,
    )(from_core, from_plane, kept)
    def gather(parts):
        return jnp.sum(parts.reshape(4, node_count, -1, LANES), axis=(0, 2))

    gains, from_plane = lax.optimization_barrier((gains, from_plane))
    sums = gather(from_core[pairs:] + from_plane[pairs:] + kept[pairs:])
    children = jnp.concatenate([sums, flags.reshape(-1, LANES)], axis=0)
    children = sum_over(children, "feat")
    side_count = children[node_count:].reshape(1, rows_dev)
    sums = children[:node_count]
    new_logits, leaves = finish(logits_t, node_ids, side_count, sums, node_count)

    halves = [[h + n * per_node for n in range(node_count)] for h in range(per_node)]
    gain_rows = lax.all_to_all(gains, "rows", 0, 0, tiled=True, axis_index_groups=halves)
    return (new_logits, gain_rows.reshape(1, pairs_dev, 2 * BINS), leaves)


def by_groups(logits_t, labels, node_ids, bin_codes, splits, per_node, pairs_dev):
    classes, rows_dev = logits_t.shape
    feats_dev = bin_codes.shape[1]
    node_count = splits[0].shape[0]
    n_rows = lax.axis_size("rows")
    width = 2 * classes
    own = 8
    group = feats_dev // own
    group_count = n_rows // group
    blocks = tuple((2, (lambda row, r=r: r * own,), 0) for r in range(group))
    info, _, flags, *rows_out = prepare(blocks, splits, logits_t, labels, node_ids, bin_codes)
    members = [[g * group + r for r in range(group)] for g in range(group_count)]
    rows_in = lax.all_to_all(
        jnp.stack(rows_out), "rows", 0, 0, tiled=True, axis_index_groups=members
    )
    hists = []
    for r in range(group):
        held = [hists] if hists else []
        hists = add_rows(
            classes, node_count, own, False, ((0, 0, (0,), (classes,)),), [rows_in[r]], *held
        )
    sums = lax.psum(child_sums(info[:, : half_width(rows_dev)], rows_dev, node_count), ("rows", "feat"))
    side_count = lax.psum(flags, "feat")
    new_logits, leaves = finish(logits_t, node_ids, side_count, sums, node_count)

    cuts = own // pairs_dev
    hist = hists[0][: node_count * width]
    hist = hist.reshape(node_count, width, cuts, pairs_dev, BINS).transpose(0, 2, 3, 4, 1)
    peers = [[g * group + r for g in range(group_count)] for r in range(group)]
    owned = lax.psum_scatter(
        hist.reshape(group_count, pairs_dev, BINS, width),
        "rows",
        scatter_dimension=0,
        axis_index_groups=peers,
    )
    bin_iota = jnp.arange(BINS, dtype=jnp.int32)
    lower_mask = (
        (bin_iota[:, None] < bin_iota[None, :]) & (bin_iota[:, None] < BINS - 1)
    ).astype(jnp.float32)
    left_base = jnp.einsum("pbc,bt->ptc", owned, lower_mask, precision=lax.Precision.HIGHEST)
    node_total = jnp.sum(owned, axis=1, keepdims=True)
    left_miss = left_base + owned[:, BINS - 1 :, :]
    parent_score = split_score(node_total, classes)
    gain_left = (
        split_score(left_miss, classes)
        + split_score(node_total - left_miss, classes)
        - parent_score
    )
    gain_right = (
        split_score(left_base, classes)
        + split_score(node_total - left_base, classes)
        - parent_score
    )
    gain = jnp.concatenate([gain_left, gain_right], axis=1) / (2.0 * classes)
    moves = [
        (n * per_node + cut * group + r, n * per_node + r * cuts + cut)
        for n in range(node_count)
        for cut in range(cuts)
        for r in range(group)
    ]
    gain_rows = lax.ppermute(gain, "rows", moves)
    return (new_logits, gain_rows[None], leaves)


def solution(mesh):
    return jax.shard_map(
        local,
        mesh=mesh,
        in_specs=(P("rows", None), P("rows"), P("rows"), P("rows", "feat"), P(), P(), P()),
        out_specs=(P("rows", None), P("rows", "feat", None), P()),
        check_vma=False,
    )
```

```python
import functools

import jax
import jax.numpy as jnp
from jax import lax
from jax.experimental import pallas as pl
from jax.experimental.pallas import tpu as pltpu
from jax.sharding import PartitionSpec as P

BINS = 64
LANES = 128
VMEM_BYTES = 12 * 1024 * 1024
PREP_VMEM_BYTES = 60 * 1024 * 1024
SMALL_COST = pl.CostEstimate(flops=1000000, bytes_accessed=1000000, transcendentals=0)


reg_lambda = 1.0
step_size = 0.3


def split_score(sums, classes):
    grad_part = sums[..., :classes]
    hess_part = sums[..., classes:]
    return jnp.sum(grad_part * grad_part / (hess_part + reg_lambda), axis=-1)


def three_parts(x):
    first = x.astype(jnp.bfloat16)
    rest = x - first.astype(jnp.float32)
    second = rest.astype(jnp.bfloat16)
    third = (rest - second.astype(jnp.float32)).astype(jnp.bfloat16)
    return first, second, third


def threshold_masks():
    row = lax.broadcasted_iota(jnp.int32, (2 * BINS, 4 * BINS), 0)
    col = lax.broadcasted_iota(jnp.int32, (2 * BINS, 4 * BINS), 1)
    bin_of = row % BINS
    threshold = col % BINS
    first_dir = (col // BINS) % 2 == 0
    below = (bin_of < threshold) & (bin_of < BINS - 1)
    missing = (bin_of == BINS - 1) & first_dir
    same = row // BINS == col // (2 * BINS)
    return jnp.where((below | missing) & same, 1.0, 0.0).astype(jnp.bfloat16)


def half_width(rows):
    return rows // 2 + LANES


def read_info(halves, rows):
    half = rows // 2
    chunks = half // LANES
    prob = jnp.concatenate([info[:, :half] for info in halves], axis=1)
    label, node = (
        jnp.concatenate(
            [info[i : i + 1, half:] for info in halves for i in range(low, low + chunks)], axis=1
        )
        for low in (0, chunks)
    )
    return prob, label, node


def child_sums(info, rows, node_count):
    return info[-node_count:, rows // 2 :]


def prep_kernel(
    own,
    blocks,
    *refs,
):
    operands, rest = refs[:7], refs[7:]
    info_ref, half_ref, flag_ref = rest[:3]
    outs = rest[3 : 3 + len(blocks)]
    turned, *buffers, sems = rest[3 + len(blocks) :]
    copies = [
        pltpu.make_async_copy(operand, buffer, sems.at[i])
        for i, (operand, buffer) in enumerate(zip(operands, buffers))
    ]
    for copy in copies:
        copy.start()
    codes_ref, logits_ref, labels_ref, nodes_ref, feature_ref, bin_ref, missing_ref = buffers
    row_index, feat_index = lax.axis_index("rows"), lax.axis_index("feat")
    classes, rows = logits_ref.shape
    half, width = rows // 2, half_width(rows)
    chunks = half // LANES
    for copy in copies[1:]:
        copy.wait()
    expo_vals = jnp.exp(logits_ref[...])
    prob = expo_vals / jnp.sum(expo_vals, axis=0, keepdims=True)
    for h in range(2):
        info_ref[:, h * width : h * width + half] = prob[:, h * half : (h + 1) * half]
    copies[0].wait()
    turned[...] = codes_ref[...].T
    for (infos, pieces, _), out_ref in zip(blocks, outs):
        if infos == 0 and out_ref.shape[1] > rows:
            out_ref[:, rows:] = jnp.zeros((out_ref.shape[0], out_ref.shape[1] - rows), out_ref.dtype)
        for i, start_of in enumerate(pieces):
            start = pl.multiple_of(start_of(row_index), own)
            if infos == 0:
                out_ref[i * own : (i + 1) * own, :rows] = turned[pl.ds(start, own), :]
                continue
            cut = rows * infos // 2
            for h in range(2 // infos):
                low = classes + (h * len(pieces) + i) * own
                part = turned[pl.ds(start, own), h * cut : (h + 1) * cut]
                out_ref[low : low + own, :cut] = part.astype(out_ref.dtype)
                out_ref[low : low + own, cut:] = jnp.zeros((own, infos * width - cut), out_ref.dtype)
    labels = labels_ref[...].astype(jnp.float32)
    nodes = nodes_ref[...].astype(jnp.float32)
    label = jnp.concatenate([labels[i : i + 1] for i in range(2 * chunks)], axis=1)
    node = jnp.concatenate([nodes[i : i + 1] for i in range(2 * chunks)], axis=1)

    feats = turned.shape[0]
    node_count = feature_ref.shape[0]
    side = jnp.zeros((1, rows), jnp.float32)
    for n in range(node_count):
        col = feature_ref[n] - feat_index * feats
        held = (col >= 0) & (col < feats)
        code = turned[pl.ds(jnp.clip(col, 0, feats - 1), 1), :]
        threshold = jnp.where(held, bin_ref[n], -1)
        missing = jnp.where(held & (missing_ref[n] == 1), BINS - 1, -1)
        left = (code < threshold) | (code == missing)
        value = jnp.where(left, 1.0, jnp.where(held, 2.0, 0.0))
        side = jnp.where(node == float(n), value, side)
    flag_ref[...] = jnp.where(side == 2.0, 1.0, 0.0)
    hot = jnp.concatenate(
        [
            jnp.where((node == float(slot // 2)) & (side == float(slot % 2 + 1)), 1.0, 0.0)
            for slot in range(2 * node_count)
        ],
        axis=0,
    ).astype(jnp.bfloat16)
    sums = lax.dot_general(
        hot,
        gradients(prob, label).astype(jnp.bfloat16),
        (((1,), (1,)), ((), ())),
        preferred_element_type=jnp.float32,
    )
    sums = jnp.concatenate([sums[:node_count], sums[node_count:]], axis=1)
    pad = [jnp.zeros((classes - 2 * chunks - node_count, LANES), jnp.float32)]
    pad = pad if pad[0].shape[0] > 0 else []
    for h in range(2):
        some = slice(h * chunks, (h + 1) * chunks)
        info_ref[:, h * width + half : (h + 1) * width] = jnp.concatenate(
            [labels[some], nodes[some]] + pad + [sums], axis=0
        )
    half_ref[...] = jnp.where(feat_index == 0, info_ref[:, :width], info_ref[:, width:])
    for (infos, _, _), out_ref in zip(blocks, outs):
        if infos > 0:
            out_ref[:classes, :] = half_ref[...] if infos == 1 else info_ref[...]


def gradients(prob, label):
    class_iota = lax.broadcasted_iota(jnp.int32, prob.shape, 0).astype(jnp.float32)
    target = jnp.where(class_iota == label, 1.0, 0.0)
    return jnp.concatenate([prob - target, prob * (1.0 - prob)], axis=0)


def masked_gradients(halves, rows, node_count):
    prob, label, node = read_info(halves, rows)
    grad_hess = gradients(prob, label)
    return jnp.concatenate(
        [jnp.where(node == float(n), grad_hess, 0.0).astype(jnp.bfloat16) for n in range(node_count)],
        axis=0,
    )


def one_hot(codes):
    feats, rows = codes.shape
    bin_iota = lax.broadcasted_iota(jnp.int32, (BINS, rows), 0).astype(codes.dtype)
    return jnp.concatenate(
        [
            jnp.where(codes[f : f + 1, :] == bin_iota, 1.0, 0.0).astype(jnp.bfloat16)
            for f in range(feats)
        ],
        axis=0,
    )


def write_gains(hist_ref, gain_ref, classes, node_count):
    masks = threshold_masks()
    ones = jnp.where(
        lax.broadcasted_iota(jnp.int32, (2 * BINS, 4 * BINS), 0) < BINS, 1.0, 0.0
    ).astype(jnp.bfloat16)

    def times(parts, right):
        return sum(jnp.dot(part, right, preferred_element_type=jnp.float32) for part in parts)

    total = times(three_parts(hist_ref[:, : 2 * BINS]), ones)
    for pair in range(gain_ref.shape[1] // 2):
        span = slice(pair * 2 * BINS, (pair + 1) * 2 * BINS)
        left = times(three_parts(hist_ref[:, span]), masks)
        right = total - left
        for n in range(node_count):
            grads = slice(n * 2 * classes, n * 2 * classes + classes)
            hesss = slice(n * 2 * classes + classes, (n + 1) * 2 * classes)
            score = (
                left[grads] * left[grads] / (left[hesss] + reg_lambda)
                + right[grads] * right[grads] / (right[hesss] + reg_lambda)
            )
            parent = total[grads] * total[grads] / (total[hesss] + reg_lambda)
            gain = (
                jnp.sum(score, axis=0, keepdims=True) - jnp.sum(parent, axis=0, keepdims=True)
            ) / (2.0 * classes)
            gain_ref[n, 2 * pair : 2 * pair + 1, :] = gain[:, : 2 * BINS]
            gain_ref[n, 2 * pair + 1 : 2 * pair + 2, :] = gain[:, 2 * BINS :]


def add_kernel(classes, node_count, own, plan, carry, *refs):
    outs = len(plan[0][3])
    arrays = 1 + max(max((c,) + tuple(j for j in i if j is not None)) for _, c, i, _ in plan)
    out_refs = refs[-outs:]
    held_refs = refs[arrays:-outs]
    pairs = 2 * classes * node_count
    row_index, feat_index = lax.axis_index("rows"), lax.axis_index("feat")
    for s, (m, codes_at, info_at, firsts) in enumerate(plan):
        codes_ref = refs[codes_at]
        line = (row_index >> 2) ^ (m >> 2)
        cut = None
        if len(info_at) == 1:
            width = refs[info_at[0]].shape[1] // 2
            halves = [refs[info_at[0]][:classes, h * width : (h + 1) * width] for h in range(2)]
            sums_from = halves[0]
        elif None in info_at:
            near_only = info_at[1] is None
            info_ref = refs[info_at[0] if near_only else info_at[1]]
            width = info_ref.shape[1]
            halves = [info_ref[:classes, :]]
            sums_from = halves[0] if near_only else None
            which = feat_index if near_only else 1 - feat_index
            cut = pl.ds(pl.multiple_of(which * (width - LANES), LANES), width - LANES)
        else:
            width = refs[info_at[0]].shape[1]
            near, far = (refs[i][:classes, :] for i in info_at)
            halves = [
                jnp.where(feat_index == 0, near, far),
                jnp.where(feat_index == 0, far, near),
            ]
            sums_from = near
        rows = 2 * (width - LANES)
        masked = masked_gradients(halves, rows, node_count)
        sums = None if sums_from is None else child_sums(sums_from, rows, node_count)
        for i, first in enumerate(firsts):
            out_ref = out_refs[i]
            if cut is not None:
                codes = codes_ref[first : first + own, cut]
            elif codes_ref.shape[1] < rows:
                second = first + (codes_ref.shape[0] - classes) // 2
                codes = jnp.concatenate(
                    [codes_ref[low : low + own, : rows // 2] for low in (first, second)], axis=1
                )
            else:
                codes = codes_ref[first : first + own, :rows]
            product = lax.dot_general(
                masked,
                one_hot(codes),
                (((1,), (1,)), ((), ())),
                preferred_element_type=jnp.float32,
            )
            if s == 0:
                if held_refs:
                    out_ref[...] = sum(ref[...] for ref in held_refs[i::outs])
                else:
                    out_ref[...] = jnp.zeros(out_ref.shape, out_ref.dtype)
            out_ref[:pairs, :] += product
            if not carry or sums is None:
                continue
            low_row = pairs + (line >> 1) * node_count
            band = pl.ds(pl.multiple_of(low_row, node_count), node_count)
            for i in range(out_ref.shape[1] // LANES):
                here = jnp.where((row_index & 3) == i, 1.0, 0.0)
                out_ref[band, i * LANES : (i + 1) * LANES] += here * sums


def add_rows(classes, node_count, own, carry, plan, arrays, *held):
    shape = (2 * classes * node_count + 2 * node_count, own * BINS)
    whole = pl.BlockSpec(memory_space=pltpu.VMEM)
    outs = len(plan[0][3])
    return pl.pallas_call(
        functools.partial(add_kernel, classes, node_count, own, plan, carry),
        in_specs=[whole] * (len(arrays) + len(held) * outs),
        out_specs=[whole] * outs,
        out_shape=[jax.ShapeDtypeStruct(shape, jnp.float32)] * outs,
        compiler_params=pltpu.CompilerParams(vmem_limit_bytes=VMEM_BYTES),
        cost_estimate=SMALL_COST,
    )(*arrays, *[hist for hists in held for hist in hists])


def gain_kernel(classes, node_count, *refs):
    gain_ref, hist_ref = refs[-2:]
    hist_ref[...] = sum(ref[: hist_ref.shape[0], :] for ref in refs[:-2])
    write_gains(hist_ref, gain_ref, classes, node_count)


def swap(x, axis, bit):
    size = lax.axis_size(axis)
    return lax.ppermute(x, axis, [(i, i ^ bit) for i in range(size)])


def sum_over(x, axis):
    bit = 1
    while bit < lax.axis_size(axis):
        x = x + swap(x, axis, bit)
        bit *= 2
    return x


def prepare(blocks, splits, logits_t, labels, node_ids, bin_codes):
    classes, rows_dev = logits_t.shape
    feats_dev = bin_codes.shape[1]
    own = 8
    whole = pl.BlockSpec(memory_space=pltpu.VMEM)
    width = half_width(rows_dev)
    shapes = [
        jax.ShapeDtypeStruct((classes, 2 * width), jnp.float32),
        jax.ShapeDtypeStruct((classes, width), jnp.float32),
        jax.ShapeDtypeStruct((1, rows_dev), jnp.float32),
    ]
    for infos, pieces, spare in blocks:
        codes = len(pieces) * own
        if infos == 0:
            shapes.append(jax.ShapeDtypeStruct((codes, rows_dev + spare), jnp.int32))
        else:
            shape = (classes + codes * 2 // infos, infos * width)
            shapes.append(jax.ShapeDtypeStruct(shape, jnp.float32))
    operands = (
        bin_codes,
        logits_t,
        labels.reshape(-1, LANES),
        node_ids.reshape(-1, LANES),
        *splits,
    )
    spaces = [pltpu.VMEM] * 4 + [pltpu.SMEM] * 3
    return pl.pallas_call(
        functools.partial(prep_kernel, own, blocks),
        in_specs=[pl.BlockSpec(memory_space=pltpu.HBM)] * len(operands),
        out_specs=[whole] * len(shapes),
        out_shape=shapes,
        scratch_shapes=[pltpu.VMEM((feats_dev, rows_dev), jnp.int32)]
        + [space(x.shape, x.dtype) for space, x in zip(spaces, operands)]
        + [pltpu.SemaphoreType.DMA((len(operands),))],
        compiler_params=pltpu.CompilerParams(vmem_limit_bytes=PREP_VMEM_BYTES),
        cost_estimate=SMALL_COST,
    )(*operands)


def finish(logits_t, node_ids, side_count, sums, node_count):
    classes = logits_t.shape[0]
    width = 2 * classes
    side_sums = jnp.concatenate([sums[:, :width], sums[:, width:]], axis=0)
    side_sums = side_sums.reshape(node_count, 2, width)
    leaves = -side_sums[..., :classes] / (side_sums[..., classes:] + reg_lambda)
    row_side = (side_count > 0.5).astype(jnp.int32)
    slot_iota = jnp.arange(2 * node_count, dtype=jnp.int32)
    slot_hot = (node_ids[None, :] * 2 + row_side) == slot_iota[:, None]
    update = jnp.dot(
        leaves.reshape(2 * node_count, classes).T,
        slot_hot.astype(jnp.float32),
        precision=lax.Precision.HIGHEST,
    )
    return (logits_t + step_size * update).T, leaves


def local(logits, labels, node_ids, bin_codes, split_feature, split_bin, split_missing):
    rows_dev, classes = logits.shape
    feats_dev = bin_codes.shape[1]
    node_count = split_feature.shape[0]
    n_rows = lax.axis_size("rows")
    per_node = n_rows // node_count
    pairs_dev = feats_dev // per_node
    width = 2 * classes
    own = 8
    splits = (split_feature, split_bin, split_missing)
    logits_t = logits.T
    if feats_dev != own * n_rows or n_rows != 16 or lax.axis_size("feat") != 2:
        return by_groups(logits_t, labels, node_ids, bin_codes, splits, per_node, pairs_dev)
    add = functools.partial(add_rows, classes, node_count, own, True)

    def start(taker):
        return (taker & 1) * pairs_dev + (taker >> 1) * own

    def quarters(m, which):
        return tuple(lambda row, low=m ^ 3 ^ q: start(row ^ low) for q in which)

    blocks = (
        (0, quarters(0, (0, 1, 2, 3)), 0),
        (1, quarters(4, (0, 1)), 0),
        (0, quarters(8, (0, 1)), 3 * LANES),
        (0, quarters(12, (0, 1)), 3 * LANES),
        (0, quarters(4, (2, 3)), 0),
        (0, quarters(8, (2, 3)), 0),
        (0, quarters(12, (2, 3)), 0),
    )
    info, half, flags, codes_0, rows_4, codes_8, codes_12, late_4, late_8, late_12 = prepare(
        blocks, splits, logits_t, labels, node_ids, bin_codes
    )

    near_8 = swap(half, "rows", 8)
    rows_4 = swap(rows_4, "rows", 4)
    codes_8 = swap(codes_8, "rows", 8)
    codes_12 = swap(codes_12, "rows", 12)
    hist_a, hist_b, hist_c, hist_d = add(
        ((0, 0, (1,), (0, own, 2 * own, 3 * own)),), [codes_0, info]
    )
    near_8, rows_4, hist_a = lax.optimization_barrier((near_8, rows_4, hist_a))
    near_12 = swap(near_8, "rows", 4)
    far_8 = swap(near_8, "feat", 1)
    far_4 = swap(rows_4[:classes], "feat", 1)
    late_4 = swap(late_4, "rows", 4)
    late_8 = swap(late_8, "rows", 8)
    late_12 = swap(late_12, "rows", 12)
    hist_a, hist_b = add(
        ((4, 0, (0, 1), (classes, classes + own)),), [rows_4, far_4], [hist_a, hist_b]
    )
    near_12, codes_8, codes_12, hist_a = lax.optimization_barrier((near_12, codes_8, codes_12, hist_a))
    far_12 = swap(near_12, "feat", 1)
    hist_a, hist_b = add(((8, 0, (1, 2), (0, own)),), [codes_8, near_8, far_8], [hist_a, hist_b])
    hist_a, hist_b = add(((12, 0, (1, None), (0, own)),), [codes_12, near_12], [hist_a, hist_b])
    (to_core,) = add(((12, 0, (None, 1), (0,)),), [codes_12, far_12], [hist_a])
    from_core = swap(to_core, "rows", 1)
    (to_plane,) = add(((12, 0, (None, 1), (own,)),), [codes_12, far_12], [hist_b], [from_core])
    from_plane = swap(to_plane, "rows", 2)
    _, late_4 = lax.optimization_barrier((to_plane, late_4))
    hists = add(((4, 0, (1, 2), (0, own)),), [late_4, rows_4, far_4], [hist_c, hist_d])
    hists = add(((8, 0, (1, 2), (0, own)),), [late_8, near_8, far_8], hists)
    to_core, kept = add(((12, 0, (1, 2), (0, own)),), [late_12, near_12, far_12], hists)
    middle = to_core.shape[0] // 2
    from_core = [swap(part, "rows", 1) for part in (to_core[:middle], to_core[middle:])]
    from_core = jnp.concatenate(from_core, axis=0)

    pairs = node_count * width
    gains = pl.pallas_call(
        functools.partial(gain_kernel, classes, node_count),
        in_specs=[pl.BlockSpec(memory_space=pltpu.VMEM)] * 3,
        out_specs=pl.BlockSpec(memory_space=pltpu.VMEM),
        out_shape=jax.ShapeDtypeStruct((node_count, own, 2 * BINS), jnp.float32),
        scratch_shapes=[pltpu.VMEM((pairs, own * BINS), jnp.float32)],
        compiler_params=pltpu.CompilerParams(vmem_limit_bytes=VMEM_BYTES),
        cost_estimate=SMALL_COST,
    )(from_core, from_plane, kept)
    def gather(parts):
        return jnp.sum(parts.reshape(2, node_count, -1, LANES), axis=(0, 2))

    gains, from_plane = lax.optimization_barrier((gains, from_plane))
    sums = gather(from_core[pairs:] + from_plane[pairs:] + kept[pairs:])
    children = jnp.concatenate([sums, flags.reshape(-1, LANES)], axis=0)
    children = sum_over(children, "feat")
    side_count = children[node_count:].reshape(1, rows_dev)
    sums = children[:node_count]
    new_logits, leaves = finish(logits_t, node_ids, side_count, sums, node_count)

    halves = [[h + n * per_node for n in range(node_count)] for h in range(per_node)]
    gain_rows = lax.all_to_all(gains, "rows", 0, 0, tiled=True, axis_index_groups=halves)
    return (new_logits, gain_rows.reshape(1, pairs_dev, 2 * BINS), leaves)


def by_groups(logits_t, labels, node_ids, bin_codes, splits, per_node, pairs_dev):
    classes, rows_dev = logits_t.shape
    feats_dev = bin_codes.shape[1]
    node_count = splits[0].shape[0]
    n_rows = lax.axis_size("rows")
    width = 2 * classes
    own = 8
    group = feats_dev // own
    group_count = n_rows // group
    blocks = tuple((2, (lambda row, r=r: r * own,), 0) for r in range(group))
    info, _, flags, *rows_out = prepare(blocks, splits, logits_t, labels, node_ids, bin_codes)
    members = [[g * group + r for r in range(group)] for g in range(group_count)]
    rows_in = lax.all_to_all(
        jnp.stack(rows_out), "rows", 0, 0, tiled=True, axis_index_groups=members
    )
    hists = []
    for r in range(group):
        held = [hists] if hists else []
        hists = add_rows(
            classes, node_count, own, False, ((0, 0, (0,), (classes,)),), [rows_in[r]], *held
        )
    sums = lax.psum(child_sums(info[:, : half_width(rows_dev)], rows_dev, node_count), ("rows", "feat"))
    side_count = lax.psum(flags, "feat")
    new_logits, leaves = finish(logits_t, node_ids, side_count, sums, node_count)

    cuts = own // pairs_dev
    hist = hists[0][: node_count * width]
    hist = hist.reshape(node_count, width, cuts, pairs_dev, BINS).transpose(0, 2, 3, 4, 1)
    peers = [[g * group + r for g in range(group_count)] for r in range(group)]
    owned = lax.psum_scatter(
        hist.reshape(group_count, pairs_dev, BINS, width),
        "rows",
        scatter_dimension=0,
        axis_index_groups=peers,
    )
    bin_iota = jnp.arange(BINS, dtype=jnp.int32)
    lower_mask = (
        (bin_iota[:, None] < bin_iota[None, :]) & (bin_iota[:, None] < BINS - 1)
    ).astype(jnp.float32)
    left_base = jnp.einsum("pbc,bt->ptc", owned, lower_mask, precision=lax.Precision.HIGHEST)
    node_total = jnp.sum(owned, axis=1, keepdims=True)
    left_miss = left_base + owned[:, BINS - 1 :, :]
    parent_score = split_score(node_total, classes)
    gain_left = (
        split_score(left_miss, classes)
        + split_score(node_total - left_miss, classes)
        - parent_score
    )
    gain_right = (
        split_score(left_base, classes)
        + split_score(node_total - left_base, classes)
        - parent_score
    )
    gain = jnp.concatenate([gain_left, gain_right], axis=1) / (2.0 * classes)
    moves = [
        (n * per_node + cut * group + r, n * per_node + r * cuts + cut)
        for n in range(node_count)
        for cut in range(cuts)
        for r in range(group)
    ]
    gain_rows = lax.ppermute(gain, "rows", moves)
    return (new_logits, gain_rows[None], leaves)


def solution(mesh):
    return jax.shard_map(
        local,
        mesh=mesh,
        in_specs=(P("rows", None), P("rows"), P("rows"), P("rows", "feat"), P(), P(), P()),
        out_specs=(P("rows", None), P("rows", "feat", None), P()),
        check_vma=False,
    )
```

```python
import functools

import jax
import jax.numpy as jnp
from jax import lax
from jax.experimental import pallas as pl
from jax.experimental.pallas import tpu as pltpu
from jax.sharding import PartitionSpec as P

BINS = 64
LANES = 128
VMEM_BYTES = 12 * 1024 * 1024
PREP_VMEM_BYTES = 60 * 1024 * 1024
SMALL_COST = pl.CostEstimate(flops=1000000, bytes_accessed=1000000, transcendentals=0)


reg_lambda = 1.0
step_size = 0.3


def split_score(sums, classes):
    grad_part = sums[..., :classes]
    hess_part = sums[..., classes:]
    return jnp.sum(grad_part * grad_part / (hess_part + reg_lambda), axis=-1)


def three_parts(x):
    first = x.astype(jnp.bfloat16)
    rest = x - first.astype(jnp.float32)
    second = rest.astype(jnp.bfloat16)
    third = (rest - second.astype(jnp.float32)).astype(jnp.bfloat16)
    return first, second, third


def threshold_masks():
    row = lax.broadcasted_iota(jnp.int32, (2 * BINS, 4 * BINS), 0)
    col = lax.broadcasted_iota(jnp.int32, (2 * BINS, 4 * BINS), 1)
    bin_of = row % BINS
    threshold = col % BINS
    first_dir = (col // BINS) % 2 == 0
    below = (bin_of < threshold) & (bin_of < BINS - 1)
    missing = (bin_of == BINS - 1) & first_dir
    same = row // BINS == col // (2 * BINS)
    return jnp.where((below | missing) & same, 1.0, 0.0).astype(jnp.bfloat16)


def half_width(rows):
    return rows // 2 + LANES


def read_info(halves, rows):
    half = rows // 2
    chunks = half // LANES
    prob = jnp.concatenate([info[:, :half] for info in halves], axis=1)
    label, node = (
        jnp.concatenate(
            [info[i : i + 1, half:] for info in halves for i in range(low, low + chunks)], axis=1
        )
        for low in (0, chunks)
    )
    return prob, label, node


def child_sums(info, rows, node_count):
    return info[-node_count:, rows // 2 :]


def prep_kernel(
    own,
    blocks,
    *refs,
):
    operands, rest = refs[:7], refs[7:]
    info_ref, half_ref, flag_ref = rest[:3]
    outs = rest[3 : 3 + len(blocks)]
    turned, *buffers, sems = rest[3 + len(blocks) :]
    copies = [
        pltpu.make_async_copy(operand, buffer, sems.at[i])
        for i, (operand, buffer) in enumerate(zip(operands, buffers))
    ]
    for copy in copies:
        copy.start()
    codes_ref, logits_ref, labels_ref, nodes_ref, feature_ref, bin_ref, missing_ref = buffers
    row_index, feat_index = lax.axis_index("rows"), lax.axis_index("feat")
    classes, rows = logits_ref.shape
    half, width = rows // 2, half_width(rows)
    chunks = half // LANES
    for copy in copies[1:]:
        copy.wait()
    expo_vals = jnp.exp(logits_ref[...])
    prob = expo_vals / jnp.sum(expo_vals, axis=0, keepdims=True)
    for h in range(2):
        info_ref[:, h * width : h * width + half] = prob[:, h * half : (h + 1) * half]
    copies[0].wait()
    turned[...] = codes_ref[...].T
    for (infos, pieces, _), out_ref in zip(blocks, outs):
        if infos == 0 and out_ref.shape[1] > rows:
            out_ref[:, rows:] = jnp.zeros((out_ref.shape[0], out_ref.shape[1] - rows), out_ref.dtype)
        for i, start_of in enumerate(pieces):
            start = pl.multiple_of(start_of(row_index), own)
            if infos == 0:
                out_ref[i * own : (i + 1) * own, :rows] = turned[pl.ds(start, own), :]
                continue
            cut = rows * infos // 2
            for h in range(2 // infos):
                low = classes + (h * len(pieces) + i) * own
                part = turned[pl.ds(start, own), h * cut : (h + 1) * cut]
                out_ref[low : low + own, :cut] = part.astype(out_ref.dtype)
                out_ref[low : low + own, cut:] = jnp.zeros((own, infos * width - cut), out_ref.dtype)
    labels = labels_ref[...].astype(jnp.float32)
    nodes = nodes_ref[...].astype(jnp.float32)
    label = jnp.concatenate([labels[i : i + 1] for i in range(2 * chunks)], axis=1)
    node = jnp.concatenate([nodes[i : i + 1] for i in range(2 * chunks)], axis=1)

    feats = turned.shape[0]
    node_count = feature_ref.shape[0]
    side = jnp.zeros((1, rows), jnp.float32)
    for n in range(node_count):
        col = feature_ref[n] - feat_index * feats
        held = (col >= 0) & (col < feats)
        code = turned[pl.ds(jnp.clip(col, 0, feats - 1), 1), :]
        threshold = jnp.where(held, bin_ref[n], -1)
        missing = jnp.where(held & (missing_ref[n] == 1), BINS - 1, -1)
        left = (code < threshold) | (code == missing)
        value = jnp.where(left, 1.0, jnp.where(held, 2.0, 0.0))
        side = jnp.where(node == float(n), value, side)
    flag_ref[...] = jnp.where(side == 2.0, 1.0, 0.0)
    hot = jnp.concatenate(
        [
            jnp.where((node == float(slot // 2)) & (side == float(slot % 2 + 1)), 1.0, 0.0)
            for slot in range(2 * node_count)
        ],
        axis=0,
    ).astype(jnp.bfloat16)
    sums = lax.dot_general(
        hot,
        gradients(prob, label).astype(jnp.bfloat16),
        (((1,), (1,)), ((), ())),
        preferred_element_type=jnp.float32,
    )
    sums = jnp.concatenate([sums[:node_count], sums[node_count:]], axis=1)
    pad = [jnp.zeros((classes - 2 * chunks - node_count, LANES), jnp.float32)]
    pad = pad if pad[0].shape[0] > 0 else []
    for h in range(2):
        some = slice(h * chunks, (h + 1) * chunks)
        info_ref[:, h * width + half : (h + 1) * width] = jnp.concatenate(
            [labels[some], nodes[some]] + pad + [sums], axis=0
        )
    half_ref[...] = jnp.where(feat_index == 0, info_ref[:, :width], info_ref[:, width:])
    for (infos, _, _), out_ref in zip(blocks, outs):
        if infos > 0:
            out_ref[:classes, :] = half_ref[...] if infos == 1 else info_ref[...]


def gradients(prob, label):
    class_iota = lax.broadcasted_iota(jnp.int32, prob.shape, 0).astype(jnp.float32)
    target = jnp.where(class_iota == label, 1.0, 0.0)
    return jnp.concatenate([prob - target, prob * (1.0 - prob)], axis=0)


def masked_gradients(halves, rows, node_count):
    prob, label, node = read_info(halves, rows)
    grad_hess = gradients(prob, label)
    return jnp.concatenate(
        [jnp.where(node == float(n), grad_hess, 0.0).astype(jnp.bfloat16) for n in range(node_count)],
        axis=0,
    )


def one_hot(codes):
    feats, rows = codes.shape
    bin_iota = lax.broadcasted_iota(jnp.int32, (BINS, rows), 0).astype(codes.dtype)
    return jnp.concatenate(
        [
            jnp.where(codes[f : f + 1, :] == bin_iota, 1.0, 0.0).astype(jnp.bfloat16)
            for f in range(feats)
        ],
        axis=0,
    )


def write_gains(hist_ref, gain_ref, classes, node_count):
    masks = threshold_masks()
    ones = jnp.where(
        lax.broadcasted_iota(jnp.int32, (2 * BINS, 4 * BINS), 0) < BINS, 1.0, 0.0
    ).astype(jnp.bfloat16)

    def times(parts, right):
        return sum(jnp.dot(part, right, preferred_element_type=jnp.float32) for part in parts)

    total = times(three_parts(hist_ref[:, : 2 * BINS]), ones)
    for pair in range(gain_ref.shape[1] // 2):
        span = slice(pair * 2 * BINS, (pair + 1) * 2 * BINS)
        left = times(three_parts(hist_ref[:, span]), masks)
        right = total - left
        for n in range(node_count):
            grads = slice(n * 2 * classes, n * 2 * classes + classes)
            hesss = slice(n * 2 * classes + classes, (n + 1) * 2 * classes)
            score = (
                left[grads] * left[grads] / (left[hesss] + reg_lambda)
                + right[grads] * right[grads] / (right[hesss] + reg_lambda)
            )
            parent = total[grads] * total[grads] / (total[hesss] + reg_lambda)
            gain = (
                jnp.sum(score, axis=0, keepdims=True) - jnp.sum(parent, axis=0, keepdims=True)
            ) / (2.0 * classes)
            gain_ref[n, 2 * pair : 2 * pair + 1, :] = gain[:, : 2 * BINS]
            gain_ref[n, 2 * pair + 1 : 2 * pair + 2, :] = gain[:, 2 * BINS :]


def add_kernel(classes, node_count, own, plan, carry, *refs):
    outs = len(plan[0][3])
    arrays = 1 + max(max((c,) + tuple(j for j in i if j is not None)) for _, c, i, _ in plan)
    out_refs = refs[-outs:]
    held_refs = refs[arrays:-outs]
    pairs = 2 * classes * node_count
    row_index, feat_index = lax.axis_index("rows"), lax.axis_index("feat")
    for s, (m, codes_at, info_at, firsts) in enumerate(plan):
        codes_ref = refs[codes_at]
        line = (row_index >> 2) ^ (m >> 2)
        cut = None
        if len(info_at) == 1:
            width = refs[info_at[0]].shape[1] // 2
            halves = [refs[info_at[0]][:classes, h * width : (h + 1) * width] for h in range(2)]
            sums_from = halves[0]
        elif None in info_at:
            near_only = info_at[1] is None
            info_ref = refs[info_at[0] if near_only else info_at[1]]
            width = info_ref.shape[1]
            halves = [info_ref[:classes, :]]
            sums_from = halves[0] if near_only else None
            which = feat_index if near_only else 1 - feat_index
            cut = pl.ds(pl.multiple_of(which * (width - LANES), LANES), width - LANES)
        else:
            width = refs[info_at[0]].shape[1]
            near, far = (refs[i][:classes, :] for i in info_at)
            halves = [
                jnp.where(feat_index == 0, near, far),
                jnp.where(feat_index == 0, far, near),
            ]
            sums_from = near
        rows = 2 * (width - LANES)
        masked = masked_gradients(halves, rows, node_count)
        sums = None if sums_from is None else child_sums(sums_from, rows, node_count)
        for i, first in enumerate(firsts):
            out_ref = out_refs[i]
            if cut is not None and codes_ref.shape[1] < rows:
                low = first + which * ((codes_ref.shape[0] - classes) // 2)
                codes = codes_ref[pl.ds(pl.multiple_of(low, own), own), : rows // 2]
            elif cut is not None:
                codes = codes_ref[first : first + own, cut]
            elif codes_ref.shape[1] < rows:
                second = first + (codes_ref.shape[0] - classes) // 2
                codes = jnp.concatenate(
                    [codes_ref[low : low + own, : rows // 2] for low in (first, second)], axis=1
                )
            else:
                codes = codes_ref[first : first + own, :rows]
            product = lax.dot_general(
                masked,
                one_hot(codes),
                (((1,), (1,)), ((), ())),
                preferred_element_type=jnp.float32,
            )
            if s == 0:
                if held_refs:
                    out_ref[...] = sum(ref[...] for ref in held_refs[i::outs])
                else:
                    out_ref[...] = jnp.zeros(out_ref.shape, out_ref.dtype)
            out_ref[:pairs, :] += product
            if not carry or sums is None:
                continue
            low_row = pairs + (line >> 1) * node_count
            band = pl.ds(pl.multiple_of(low_row, node_count), node_count)
            for i in range(out_ref.shape[1] // LANES):
                here = jnp.where((row_index & 3) == i, 1.0, 0.0)
                out_ref[band, i * LANES : (i + 1) * LANES] += here * sums


def add_rows(classes, node_count, own, carry, plan, arrays, *held):
    shape = (2 * classes * node_count + 2 * node_count, own * BINS)
    whole = pl.BlockSpec(memory_space=pltpu.VMEM)
    outs = len(plan[0][3])
    return pl.pallas_call(
        functools.partial(add_kernel, classes, node_count, own, plan, carry),
        in_specs=[whole] * (len(arrays) + len(held) * outs),
        out_specs=[whole] * outs,
        out_shape=[jax.ShapeDtypeStruct(shape, jnp.float32)] * outs,
        compiler_params=pltpu.CompilerParams(vmem_limit_bytes=VMEM_BYTES),
        cost_estimate=SMALL_COST,
    )(*arrays, *[hist for hists in held for hist in hists])


def gain_kernel(classes, node_count, *refs):
    gain_ref, hist_ref = refs[-2:]
    hist_ref[...] = sum(ref[: hist_ref.shape[0], :] for ref in refs[:-2])
    write_gains(hist_ref, gain_ref, classes, node_count)


def swap(x, axis, bit):
    size = lax.axis_size(axis)
    return lax.ppermute(x, axis, [(i, i ^ bit) for i in range(size)])


def sum_over(x, axis):
    bit = 1
    while bit < lax.axis_size(axis):
        x = x + swap(x, axis, bit)
        bit *= 2
    return x


def prepare(blocks, splits, logits_t, labels, node_ids, bin_codes):
    classes, rows_dev = logits_t.shape
    feats_dev = bin_codes.shape[1]
    own = 8
    whole = pl.BlockSpec(memory_space=pltpu.VMEM)
    width = half_width(rows_dev)
    shapes = [
        jax.ShapeDtypeStruct((classes, 2 * width), jnp.float32),
        jax.ShapeDtypeStruct((classes, width), jnp.float32),
        jax.ShapeDtypeStruct((1, rows_dev), jnp.float32),
    ]
    for infos, pieces, spare in blocks:
        codes = len(pieces) * own
        if infos == 0:
            shapes.append(jax.ShapeDtypeStruct((codes, rows_dev + spare), jnp.int32))
        else:
            shape = (classes + codes * 2 // infos, infos * width)
            shapes.append(jax.ShapeDtypeStruct(shape, jnp.float32))
    operands = (
        bin_codes,
        logits_t,
        labels.reshape(-1, LANES),
        node_ids.reshape(-1, LANES),
        *splits,
    )
    spaces = [pltpu.VMEM] * 4 + [pltpu.SMEM] * 3
    return pl.pallas_call(
        functools.partial(prep_kernel, own, blocks),
        in_specs=[pl.BlockSpec(memory_space=pltpu.HBM)] * len(operands),
        out_specs=[whole] * len(shapes),
        out_shape=shapes,
        scratch_shapes=[pltpu.VMEM((feats_dev, rows_dev), jnp.int32)]
        + [space(x.shape, x.dtype) for space, x in zip(spaces, operands)]
        + [pltpu.SemaphoreType.DMA((len(operands),))],
        compiler_params=pltpu.CompilerParams(vmem_limit_bytes=PREP_VMEM_BYTES),
        cost_estimate=SMALL_COST,
    )(*operands)


def finish(logits_t, node_ids, side_count, sums, node_count):
    classes = logits_t.shape[0]
    width = 2 * classes
    side_sums = jnp.concatenate([sums[:, :width], sums[:, width:]], axis=0)
    side_sums = side_sums.reshape(node_count, 2, width)
    leaves = -side_sums[..., :classes] / (side_sums[..., classes:] + reg_lambda)
    row_side = (side_count > 0.5).astype(jnp.int32)
    slot_iota = jnp.arange(2 * node_count, dtype=jnp.int32)
    slot_hot = (node_ids[None, :] * 2 + row_side) == slot_iota[:, None]
    update = jnp.dot(
        leaves.reshape(2 * node_count, classes).T,
        slot_hot.astype(jnp.float32),
        precision=lax.Precision.HIGHEST,
    )
    return (logits_t + step_size * update).T, leaves


def local(logits, labels, node_ids, bin_codes, split_feature, split_bin, split_missing):
    rows_dev, classes = logits.shape
    feats_dev = bin_codes.shape[1]
    node_count = split_feature.shape[0]
    n_rows = lax.axis_size("rows")
    per_node = n_rows // node_count
    pairs_dev = feats_dev // per_node
    width = 2 * classes
    own = 8
    splits = (split_feature, split_bin, split_missing)
    logits_t = logits.T
    if feats_dev != own * n_rows or n_rows != 16 or lax.axis_size("feat") != 2:
        return by_groups(logits_t, labels, node_ids, bin_codes, splits, per_node, pairs_dev)
    add = functools.partial(add_rows, classes, node_count, own, True)

    def start(taker):
        return (taker & 1) * pairs_dev + (taker >> 1) * own

    def quarters(m, which):
        return tuple(lambda row, low=m ^ 3 ^ q: start(row ^ low) for q in which)

    blocks = (
        (0, quarters(0, (0, 1, 2, 3)), 0),
        (1, quarters(4, (0, 1)), 0),
        (0, quarters(8, (0, 1)), 3 * LANES),
        (0, quarters(12, (0, 1)), 3 * LANES),
        (0, quarters(4, (2, 3)), 0),
        (0, quarters(8, (2, 3)), 0),
        (0, quarters(12, (2, 3)), 0),
    )
    info, half, flags, codes_0, rows_4, codes_8, codes_12, late_4, late_8, late_12 = prepare(
        blocks, splits, logits_t, labels, node_ids, bin_codes
    )

    near_8 = swap(half, "rows", 8)
    rows_4 = swap(rows_4, "rows", 4)
    codes_8 = swap(codes_8, "rows", 8)
    codes_12 = swap(codes_12, "rows", 12)
    hist_a, hist_b, hist_c, hist_d = add(
        ((0, 0, (1,), (0, own, 2 * own, 3 * own)),), [codes_0, info]
    )
    near_8, rows_4, hist_a = lax.optimization_barrier((near_8, rows_4, hist_a))
    near_12 = swap(near_8, "rows", 4)
    far_8 = swap(near_8, "feat", 1)
    far_4 = swap(rows_4[:classes], "feat", 1)
    late_4 = swap(late_4, "rows", 4)
    late_8 = swap(late_8, "rows", 8)
    late_12 = swap(late_12, "rows", 12)
    firsts = (classes, classes + own)
    hists = add(((4, 0, (0, None), firsts),), [rows_4], [hist_a, hist_b])
    hists = add(((4, 0, (None, 1), firsts),), [rows_4, far_4], hists)
    hist_a, hist_b = add(((8, 0, (1, None), (0, own)),), [codes_8, near_8], hists)
    near_12, codes_12, hist_a = lax.optimization_barrier((near_12, codes_12, hist_a))
    far_12 = swap(near_12, "feat", 1)
    hist_a, hist_b = add(((8, 0, (None, 1), (0, own)),), [codes_8, far_8], [hist_a, hist_b])
    hist_a, hist_b = add(((12, 0, (1, None), (0, own)),), [codes_12, near_12], [hist_a, hist_b])
    (to_core,) = add(((12, 0, (None, 1), (0,)),), [codes_12, far_12], [hist_a])
    from_core = swap(to_core, "rows", 1)
    (to_plane,) = add(((12, 0, (None, 1), (own,)),), [codes_12, far_12], [hist_b], [from_core])
    from_plane = swap(to_plane, "rows", 2)
    _, late_4 = lax.optimization_barrier((to_plane, late_4))
    hists = add(((4, 0, (1, 2), (0, own)),), [late_4, rows_4, far_4], [hist_c, hist_d])
    hists = add(((8, 0, (1, 2), (0, own)),), [late_8, near_8, far_8], hists)
    to_core, kept = add(((12, 0, (1, 2), (0, own)),), [late_12, near_12, far_12], hists)
    middle = to_core.shape[0] // 2
    from_core = [swap(part, "rows", 1) for part in (to_core[:middle], to_core[middle:])]
    from_core = jnp.concatenate(from_core, axis=0)

    pairs = node_count * width
    gains = pl.pallas_call(
        functools.partial(gain_kernel, classes, node_count),
        in_specs=[pl.BlockSpec(memory_space=pltpu.VMEM)] * 3,
        out_specs=pl.BlockSpec(memory_space=pltpu.VMEM),
        out_shape=jax.ShapeDtypeStruct((node_count, own, 2 * BINS), jnp.float32),
        scratch_shapes=[pltpu.VMEM((pairs, own * BINS), jnp.float32)],
        compiler_params=pltpu.CompilerParams(vmem_limit_bytes=VMEM_BYTES),
        cost_estimate=SMALL_COST,
    )(from_core, from_plane, kept)
    def gather(parts):
        return jnp.sum(parts.reshape(2, node_count, -1, LANES), axis=(0, 2))

    gains, from_plane = lax.optimization_barrier((gains, from_plane))
    sums = gather(from_core[pairs:] + from_plane[pairs:] + kept[pairs:])
    children = jnp.concatenate([sums, flags.reshape(-1, LANES)], axis=0)
    children = sum_over(children, "feat")
    side_count = children[node_count:].reshape(1, rows_dev)
    sums = children[:node_count]
    new_logits, leaves = finish(logits_t, node_ids, side_count, sums, node_count)

    halves = [[h + n * per_node for n in range(node_count)] for h in range(per_node)]
    gain_rows = lax.all_to_all(gains, "rows", 0, 0, tiled=True, axis_index_groups=halves)
    return (new_logits, gain_rows.reshape(1, pairs_dev, 2 * BINS), leaves)


def by_groups(logits_t, labels, node_ids, bin_codes, splits, per_node, pairs_dev):
    classes, rows_dev = logits_t.shape
    feats_dev = bin_codes.shape[1]
    node_count = splits[0].shape[0]
    n_rows = lax.axis_size("rows")
    width = 2 * classes
    own = 8
    group = feats_dev // own
    group_count = n_rows // group
    blocks = tuple((2, (lambda row, r=r: r * own,), 0) for r in range(group))
    info, _, flags, *rows_out = prepare(blocks, splits, logits_t, labels, node_ids, bin_codes)
    members = [[g * group + r for r in range(group)] for g in range(group_count)]
    rows_in = lax.all_to_all(
        jnp.stack(rows_out), "rows", 0, 0, tiled=True, axis_index_groups=members
    )
    hists = []
    for r in range(group):
        held = [hists] if hists else []
        hists = add_rows(
            classes, node_count, own, False, ((0, 0, (0,), (classes,)),), [rows_in[r]], *held
        )
    sums = lax.psum(child_sums(info[:, : half_width(rows_dev)], rows_dev, node_count), ("rows", "feat"))
    side_count = lax.psum(flags, "feat")
    new_logits, leaves = finish(logits_t, node_ids, side_count, sums, node_count)

    cuts = own // pairs_dev
    hist = hists[0][: node_count * width]
    hist = hist.reshape(node_count, width, cuts, pairs_dev, BINS).transpose(0, 2, 3, 4, 1)
    peers = [[g * group + r for g in range(group_count)] for r in range(group)]
    owned = lax.psum_scatter(
        hist.reshape(group_count, pairs_dev, BINS, width),
        "rows",
        scatter_dimension=0,
        axis_index_groups=peers,
    )
    bin_iota = jnp.arange(BINS, dtype=jnp.int32)
    lower_mask = (
        (bin_iota[:, None] < bin_iota[None, :]) & (bin_iota[:, None] < BINS - 1)
    ).astype(jnp.float32)
    left_base = jnp.einsum("pbc,bt->ptc", owned, lower_mask, precision=lax.Precision.HIGHEST)
    node_total = jnp.sum(owned, axis=1, keepdims=True)
    left_miss = left_base + owned[:, BINS - 1 :, :]
    parent_score = split_score(node_total, classes)
    gain_left = (
        split_score(left_miss, classes)
        + split_score(node_total - left_miss, classes)
        - parent_score
    )
    gain_right = (
        split_score(left_base, classes)
        + split_score(node_total - left_base, classes)
        - parent_score
    )
    gain = jnp.concatenate([gain_left, gain_right], axis=1) / (2.0 * classes)
    moves = [
        (n * per_node + cut * group + r, n * per_node + r * cuts + cut)
        for n in range(node_count)
        for cut in range(cuts)
        for r in range(group)
    ]
    gain_rows = lax.ppermute(gain, "rows", moves)
    return (new_logits, gain_rows[None], leaves)


def solution(mesh):
    return jax.shard_map(
        local,
        mesh=mesh,
        in_specs=(P("rows", None), P("rows"), P("rows"), P("rows", "feat"), P(), P(), P()),
        out_specs=(P("rows", None), P("rows", "feat", None), P()),
        check_vma=False,
    )
```

```python
import functools

import jax
import jax.numpy as jnp
from jax import lax
from jax.experimental import pallas as pl
from jax.experimental.pallas import tpu as pltpu
from jax.sharding import PartitionSpec as P

BINS = 64
LANES = 128
VMEM_BYTES = 12 * 1024 * 1024
PREP_VMEM_BYTES = 60 * 1024 * 1024
SMALL_COST = pl.CostEstimate(flops=1000000, bytes_accessed=1000000, transcendentals=0)


reg_lambda = 1.0
step_size = 0.3


def split_score(sums, classes):
    grad_part = sums[..., :classes]
    hess_part = sums[..., classes:]
    return jnp.sum(grad_part * grad_part / (hess_part + reg_lambda), axis=-1)


def three_parts(x):
    first = x.astype(jnp.bfloat16)
    rest = x - first.astype(jnp.float32)
    second = rest.astype(jnp.bfloat16)
    third = (rest - second.astype(jnp.float32)).astype(jnp.bfloat16)
    return first, second, third


def threshold_masks():
    row = lax.broadcasted_iota(jnp.int32, (2 * BINS, 4 * BINS), 0)
    col = lax.broadcasted_iota(jnp.int32, (2 * BINS, 4 * BINS), 1)
    bin_of = row % BINS
    threshold = col % BINS
    first_dir = (col // BINS) % 2 == 0
    below = (bin_of < threshold) & (bin_of < BINS - 1)
    missing = (bin_of == BINS - 1) & first_dir
    same = row // BINS == col // (2 * BINS)
    return jnp.where((below | missing) & same, 1.0, 0.0).astype(jnp.bfloat16)


def half_width(rows):
    return rows // 2 + LANES


def read_info(halves, rows):
    half = rows // 2
    chunks = half // LANES
    prob = jnp.concatenate([info[:, :half] for info in halves], axis=1)
    label, node = (
        jnp.concatenate(
            [info[i : i + 1, half:] for info in halves for i in range(low, low + chunks)], axis=1
        )
        for low in (0, chunks)
    )
    return prob, label, node


def child_sums(info, rows, node_count):
    return info[-node_count:, rows // 2 :]


def prep_kernel(
    own,
    blocks,
    *refs,
):
    operands, rest = refs[:7], refs[7:]
    info_ref, half_ref, flag_ref = rest[:3]
    outs = rest[3 : 3 + len(blocks)]
    turned, *buffers, sems, out_sems = rest[3 + len(blocks) :]
    copies = [
        pltpu.make_async_copy(operand, buffer, sems.at[i])
        for i, (operand, buffer) in enumerate(zip(operands, buffers))
    ]
    for copy in copies:
        copy.start()
    codes_ref, logits_ref, labels_ref, nodes_ref, feature_ref, bin_ref, missing_ref = buffers
    row_index, feat_index = lax.axis_index("rows"), lax.axis_index("feat")
    classes, rows = logits_ref.shape
    half, width = rows // 2, half_width(rows)
    chunks = half // LANES
    for copy in copies[1:]:
        copy.wait()
    expo_vals = jnp.exp(logits_ref[...])
    prob = expo_vals / jnp.sum(expo_vals, axis=0, keepdims=True)
    for h in range(2):
        info_ref[:, h * width : h * width + half] = prob[:, h * half : (h + 1) * half]
    copies[0].wait()
    turned[...] = codes_ref[...].T
    leaving = []
    for (infos, pieces, _), out_ref in zip(blocks, outs):
        for i, start_of in enumerate(pieces):
            start = pl.multiple_of(start_of(row_index), own)
            if infos == 0:
                copy = pltpu.make_async_copy(
                    turned.at[pl.ds(start, own), :],
                    out_ref.at[i * own : (i + 1) * own, :rows],
                    out_sems.at[len(leaving)],
                )
                copy.start()
                leaving.append(copy)
                continue
            cut = rows * infos // 2
            for h in range(2 // infos):
                low = classes + (h * len(pieces) + i) * own
                part = turned[pl.ds(start, own), h * cut : (h + 1) * cut]
                out_ref[low : low + own, :cut] = part.astype(out_ref.dtype)
                out_ref[low : low + own, cut:] = jnp.zeros((own, infos * width - cut), out_ref.dtype)
    labels = labels_ref[...].astype(jnp.float32)
    nodes = nodes_ref[...].astype(jnp.float32)
    label = jnp.concatenate([labels[i : i + 1] for i in range(2 * chunks)], axis=1)
    node = jnp.concatenate([nodes[i : i + 1] for i in range(2 * chunks)], axis=1)

    feats = turned.shape[0]
    node_count = feature_ref.shape[0]
    side = jnp.zeros((1, rows), jnp.float32)
    for n in range(node_count):
        col = feature_ref[n] - feat_index * feats
        held = (col >= 0) & (col < feats)
        code = turned[pl.ds(jnp.clip(col, 0, feats - 1), 1), :]
        threshold = jnp.where(held, bin_ref[n], -1)
        missing = jnp.where(held & (missing_ref[n] == 1), BINS - 1, -1)
        left = (code < threshold) | (code == missing)
        value = jnp.where(left, 1.0, jnp.where(held, 2.0, 0.0))
        side = jnp.where(node == float(n), value, side)
    flag_ref[...] = jnp.where(side == 2.0, 1.0, 0.0)
    hot = jnp.concatenate(
        [
            jnp.where((node == float(slot // 2)) & (side == float(slot % 2 + 1)), 1.0, 0.0)
            for slot in range(2 * node_count)
        ],
        axis=0,
    ).astype(jnp.bfloat16)
    sums = lax.dot_general(
        hot,
        gradients(prob, label).astype(jnp.bfloat16),
        (((1,), (1,)), ((), ())),
        preferred_element_type=jnp.float32,
    )
    sums = jnp.concatenate([sums[:node_count], sums[node_count:]], axis=1)
    pad = [jnp.zeros((classes - 2 * chunks - node_count, LANES), jnp.float32)]
    pad = pad if pad[0].shape[0] > 0 else []
    for h in range(2):
        some = slice(h * chunks, (h + 1) * chunks)
        info_ref[:, h * width + half : (h + 1) * width] = jnp.concatenate(
            [labels[some], nodes[some]] + pad + [sums], axis=0
        )
    half_ref[...] = jnp.where(feat_index == 0, info_ref[:, :width], info_ref[:, width:])
    for (infos, _, _), out_ref in zip(blocks, outs):
        if infos > 0:
            out_ref[:classes, :] = half_ref[...] if infos == 1 else info_ref[...]
    for copy in leaving:
        copy.wait()


def gradients(prob, label):
    class_iota = lax.broadcasted_iota(jnp.int32, prob.shape, 0).astype(jnp.float32)
    target = jnp.where(class_iota == label, 1.0, 0.0)
    return jnp.concatenate([prob - target, prob * (1.0 - prob)], axis=0)


def masked_gradients(halves, rows, node_count):
    prob, label, node = read_info(halves, rows)
    grad_hess = gradients(prob, label)
    return jnp.concatenate(
        [jnp.where(node == float(n), grad_hess, 0.0).astype(jnp.bfloat16) for n in range(node_count)],
        axis=0,
    )


def one_hot(codes):
    feats, rows = codes.shape
    bin_iota = lax.broadcasted_iota(jnp.int32, (BINS, rows), 0).astype(codes.dtype)
    return jnp.concatenate(
        [
            jnp.where(codes[f : f + 1, :] == bin_iota, 1.0, 0.0).astype(jnp.bfloat16)
            for f in range(feats)
        ],
        axis=0,
    )


def write_gains(hist_ref, gain_ref, classes, node_count):
    masks = threshold_masks()
    ones = jnp.where(
        lax.broadcasted_iota(jnp.int32, (2 * BINS, 4 * BINS), 0) < BINS, 1.0, 0.0
    ).astype(jnp.bfloat16)

    def times(parts, right):
        return sum(jnp.dot(part, right, preferred_element_type=jnp.float32) for part in parts)

    total = times(three_parts(hist_ref[:, : 2 * BINS]), ones)
    for pair in range(gain_ref.shape[1] // 2):
        span = slice(pair * 2 * BINS, (pair + 1) * 2 * BINS)
        left = times(three_parts(hist_ref[:, span]), masks)
        right = total - left
        for n in range(node_count):
            grads = slice(n * 2 * classes, n * 2 * classes + classes)
            hesss = slice(n * 2 * classes + classes, (n + 1) * 2 * classes)
            score = (
                left[grads] * left[grads] / (left[hesss] + reg_lambda)
                + right[grads] * right[grads] / (right[hesss] + reg_lambda)
            )
            parent = total[grads] * total[grads] / (total[hesss] + reg_lambda)
            gain = (
                jnp.sum(score, axis=0, keepdims=True) - jnp.sum(parent, axis=0, keepdims=True)
            ) / (2.0 * classes)
            gain_ref[n, 2 * pair : 2 * pair + 1, :] = gain[:, : 2 * BINS]
            gain_ref[n, 2 * pair + 1 : 2 * pair + 2, :] = gain[:, 2 * BINS :]


def add_kernel(classes, node_count, own, plan, carry, *refs):
    outs = len(plan[0][3])
    arrays = 1 + max(max((c,) + tuple(j for j in i if j is not None)) for _, c, i, _ in plan)
    out_refs = refs[-outs:]
    held_refs = refs[arrays:-outs]
    pairs = 2 * classes * node_count
    row_index, feat_index = lax.axis_index("rows"), lax.axis_index("feat")
    for s, (m, codes_at, info_at, firsts) in enumerate(plan):
        codes_ref = refs[codes_at]
        line = (row_index >> 2) ^ (m >> 2)
        cut = None
        if len(info_at) == 1:
            width = refs[info_at[0]].shape[1] // 2
            halves = [refs[info_at[0]][:classes, h * width : (h + 1) * width] for h in range(2)]
            sums_from = halves[0]
        elif None in info_at:
            near_only = info_at[1] is None
            info_ref = refs[info_at[0] if near_only else info_at[1]]
            width = info_ref.shape[1]
            halves = [info_ref[:classes, :]]
            sums_from = halves[0] if near_only else None
            which = feat_index if near_only else 1 - feat_index
            cut = pl.ds(pl.multiple_of(which * (width - LANES), LANES), width - LANES)
        else:
            width = refs[info_at[0]].shape[1]
            near, far = (refs[i][:classes, :] for i in info_at)
            halves = [
                jnp.where(feat_index == 0, near, far),
                jnp.where(feat_index == 0, far, near),
            ]
            sums_from = near
        rows = 2 * (width - LANES)
        masked = masked_gradients(halves, rows, node_count)
        sums = None if sums_from is None else child_sums(sums_from, rows, node_count)
        for i, first in enumerate(firsts):
            out_ref = out_refs[i]
            if cut is not None and codes_ref.shape[1] < rows:
                low = first + which * ((codes_ref.shape[0] - classes) // 2)
                codes = codes_ref[pl.ds(pl.multiple_of(low, own), own), : rows // 2]
            elif cut is not None:
                codes = codes_ref[first : first + own, cut]
            elif codes_ref.shape[1] < rows:
                second = first + (codes_ref.shape[0] - classes) // 2
                codes = jnp.concatenate(
                    [codes_ref[low : low + own, : rows // 2] for low in (first, second)], axis=1
                )
            else:
                codes = codes_ref[first : first + own, :rows]
            product = lax.dot_general(
                masked,
                one_hot(codes),
                (((1,), (1,)), ((), ())),
                preferred_element_type=jnp.float32,
            )
            if s == 0:
                if held_refs:
                    out_ref[...] = sum(ref[...] for ref in held_refs[i::outs])
                else:
                    out_ref[...] = jnp.zeros(out_ref.shape, out_ref.dtype)
            out_ref[:pairs, :] += product
            if not carry or sums is None:
                continue
            low_row = pairs + (line >> 1) * node_count
            band = pl.ds(pl.multiple_of(low_row, node_count), node_count)
            for i in range(out_ref.shape[1] // LANES):
                here = jnp.where((row_index & 3) == i, 1.0, 0.0)
                out_ref[band, i * LANES : (i + 1) * LANES] += here * sums


def add_rows(classes, node_count, own, carry, plan, arrays, *held):
    shape = (2 * classes * node_count + 2 * node_count, own * BINS)
    whole = pl.BlockSpec(memory_space=pltpu.VMEM)
    outs = len(plan[0][3])
    return pl.pallas_call(
        functools.partial(add_kernel, classes, node_count, own, plan, carry),
        in_specs=[whole] * (len(arrays) + len(held) * outs),
        out_specs=[whole] * outs,
        out_shape=[jax.ShapeDtypeStruct(shape, jnp.float32)] * outs,
        compiler_params=pltpu.CompilerParams(vmem_limit_bytes=VMEM_BYTES),
        cost_estimate=SMALL_COST,
    )(*arrays, *[hist for hists in held for hist in hists])


def gain_kernel(classes, node_count, *refs):
    gain_ref, hist_ref = refs[-2:]
    hist_ref[...] = sum(ref[: hist_ref.shape[0], :] for ref in refs[:-2])
    write_gains(hist_ref, gain_ref, classes, node_count)


def swap(x, axis, bit):
    size = lax.axis_size(axis)
    return lax.ppermute(x, axis, [(i, i ^ bit) for i in range(size)])


def sum_over(x, axis):
    bit = 1
    while bit < lax.axis_size(axis):
        x = x + swap(x, axis, bit)
        bit *= 2
    return x


def prepare(blocks, splits, logits_t, labels, node_ids, bin_codes):
    classes, rows_dev = logits_t.shape
    feats_dev = bin_codes.shape[1]
    own = 8
    whole = pl.BlockSpec(memory_space=pltpu.VMEM)
    width = half_width(rows_dev)
    shapes = [
        jax.ShapeDtypeStruct((classes, 2 * width), jnp.float32),
        jax.ShapeDtypeStruct((classes, width), jnp.float32),
        jax.ShapeDtypeStruct((1, rows_dev), jnp.float32),
    ]
    for infos, pieces, spare in blocks:
        codes = len(pieces) * own
        if infos == 0:
            shapes.append(jax.ShapeDtypeStruct((codes, rows_dev + spare), jnp.int32))
        else:
            shape = (classes + codes * 2 // infos, infos * width)
            shapes.append(jax.ShapeDtypeStruct(shape, jnp.float32))
    operands = (
        bin_codes,
        logits_t,
        labels.reshape(-1, LANES),
        node_ids.reshape(-1, LANES),
        *splits,
    )
    spaces = [pltpu.VMEM] * 4 + [pltpu.SMEM] * 3
    loose = sum(len(pieces) for infos, pieces, _ in blocks if infos == 0)
    return pl.pallas_call(
        functools.partial(prep_kernel, own, blocks),
        in_specs=[pl.BlockSpec(memory_space=pltpu.HBM)] * len(operands),
        out_specs=[whole] * 3
        + [pl.BlockSpec(memory_space=pltpu.HBM) if infos == 0 else whole for infos, _, _ in blocks],
        out_shape=shapes,
        scratch_shapes=[pltpu.VMEM((feats_dev, rows_dev), jnp.int32)]
        + [space(x.shape, x.dtype) for space, x in zip(spaces, operands)]
        + [pltpu.SemaphoreType.DMA((len(operands),)), pltpu.SemaphoreType.DMA((max(1, loose),))],
        compiler_params=pltpu.CompilerParams(vmem_limit_bytes=PREP_VMEM_BYTES),
        cost_estimate=SMALL_COST,
    )(*operands)


def finish(logits_t, node_ids, side_count, sums, node_count):
    classes = logits_t.shape[0]
    width = 2 * classes
    side_sums = jnp.concatenate([sums[:, :width], sums[:, width:]], axis=0)
    side_sums = side_sums.reshape(node_count, 2, width)
    leaves = -side_sums[..., :classes] / (side_sums[..., classes:] + reg_lambda)
    row_side = (side_count > 0.5).astype(jnp.int32)
    slot_iota = jnp.arange(2 * node_count, dtype=jnp.int32)
    slot_hot = (node_ids[None, :] * 2 + row_side) == slot_iota[:, None]
    update = jnp.dot(
        leaves.reshape(2 * node_count, classes).T,
        slot_hot.astype(jnp.float32),
        precision=lax.Precision.HIGHEST,
    )
    return (logits_t + step_size * update).T, leaves


def local(logits, labels, node_ids, bin_codes, split_feature, split_bin, split_missing):
    rows_dev, classes = logits.shape
    feats_dev = bin_codes.shape[1]
    node_count = split_feature.shape[0]
    n_rows = lax.axis_size("rows")
    per_node = n_rows // node_count
    pairs_dev = feats_dev // per_node
    width = 2 * classes
    own = 8
    splits = (split_feature, split_bin, split_missing)
    logits_t = logits.T
    if feats_dev != own * n_rows or n_rows != 16 or lax.axis_size("feat") != 2:
        return by_groups(logits_t, labels, node_ids, bin_codes, splits, per_node, pairs_dev)
    add = functools.partial(add_rows, classes, node_count, own, True)

    def start(taker):
        return (taker & 1) * pairs_dev + (taker >> 1) * own

    def quarters(m, which):
        return tuple(lambda row, low=m ^ 3 ^ q: start(row ^ low) for q in which)

    blocks = (
        (0, quarters(0, (0, 1, 2, 3)), 0),
        (1, quarters(4, (0, 1)), 0),
        (0, quarters(8, (0, 1)), 3 * LANES),
        (0, quarters(12, (0, 1)), 3 * LANES),
        (0, quarters(4, (2, 3)), 0),
        (0, quarters(8, (2, 3)), 0),
        (0, quarters(12, (2, 3)), 0),
    )
    info, half, flags, codes_0, rows_4, codes_8, codes_12, late_4, late_8, late_12 = prepare(
        blocks, splits, logits_t, labels, node_ids, bin_codes
    )

    near_8 = swap(half, "rows", 8)
    rows_4 = swap(rows_4, "rows", 4)
    codes_8 = swap(codes_8, "rows", 8)
    codes_12 = swap(codes_12, "rows", 12)
    hist_a, hist_b, hist_c, hist_d = add(
        ((0, 0, (1,), (0, own, 2 * own, 3 * own)),), [codes_0, info]
    )
    near_8, rows_4, hist_a = lax.optimization_barrier((near_8, rows_4, hist_a))
    near_12 = swap(near_8, "rows", 4)
    far_8 = swap(near_8, "feat", 1)
    far_4 = swap(rows_4[:classes], "feat", 1)
    late_4 = swap(late_4, "rows", 4)
    late_8 = swap(late_8, "rows", 8)
    late_12 = swap(late_12, "rows", 12)
    firsts = (classes, classes + own)
    hists = add(((4, 0, (0, None), firsts),), [rows_4], [hist_a, hist_b])
    hists = add(((4, 0, (None, 1), firsts),), [rows_4, far_4], hists)
    hist_a, hist_b = add(((8, 0, (1, None), (0, own)),), [codes_8, near_8], hists)
    near_12, codes_12, hist_a = lax.optimization_barrier((near_12, codes_12, hist_a))
    far_12 = swap(near_12, "feat", 1)
    hist_a, hist_b = add(((8, 0, (None, 1), (0, own)),), [codes_8, far_8], [hist_a, hist_b])
    hist_a, hist_b = add(((12, 0, (1, None), (0, own)),), [codes_12, near_12], [hist_a, hist_b])
    (to_core,) = add(((12, 0, (None, 1), (0,)),), [codes_12, far_12], [hist_a])
    from_core = swap(to_core, "rows", 1)
    (to_plane,) = add(((12, 0, (None, 1), (own,)),), [codes_12, far_12], [hist_b], [from_core])
    from_plane = swap(to_plane, "rows", 2)
    _, late_4 = lax.optimization_barrier((to_plane, late_4))
    hists = add(((4, 0, (1, 2), (0, own)),), [late_4, rows_4, far_4], [hist_c, hist_d])
    hists = add(((8, 0, (1, 2), (0, own)),), [late_8, near_8, far_8], hists)
    to_core, kept = add(((12, 0, (1, 2), (0, own)),), [late_12, near_12, far_12], hists)
    middle = to_core.shape[0] // 2
    from_core = [swap(part, "rows", 1) for part in (to_core[:middle], to_core[middle:])]
    from_core = jnp.concatenate(from_core, axis=0)

    pairs = node_count * width
    gains = pl.pallas_call(
        functools.partial(gain_kernel, classes, node_count),
        in_specs=[pl.BlockSpec(memory_space=pltpu.VMEM)] * 3,
        out_specs=pl.BlockSpec(memory_space=pltpu.VMEM),
        out_shape=jax.ShapeDtypeStruct((node_count, own, 2 * BINS), jnp.float32),
        scratch_shapes=[pltpu.VMEM((pairs, own * BINS), jnp.float32)],
        compiler_params=pltpu.CompilerParams(vmem_limit_bytes=VMEM_BYTES),
        cost_estimate=SMALL_COST,
    )(from_core, from_plane, kept)
    def gather(parts):
        return jnp.sum(parts.reshape(2, node_count, -1, LANES), axis=(0, 2))

    gains, from_plane = lax.optimization_barrier((gains, from_plane))
    sums = gather(from_core[pairs:] + from_plane[pairs:] + kept[pairs:])
    children = jnp.concatenate([sums, flags.reshape(-1, LANES)], axis=0)
    children = sum_over(children, "feat")
    side_count = children[node_count:].reshape(1, rows_dev)
    sums = children[:node_count]
    new_logits, leaves = finish(logits_t, node_ids, side_count, sums, node_count)

    halves = [[h + n * per_node for n in range(node_count)] for h in range(per_node)]
    gain_rows = lax.all_to_all(gains, "rows", 0, 0, tiled=True, axis_index_groups=halves)
    return (new_logits, gain_rows.reshape(1, pairs_dev, 2 * BINS), leaves)


def by_groups(logits_t, labels, node_ids, bin_codes, splits, per_node, pairs_dev):
    classes, rows_dev = logits_t.shape
    feats_dev = bin_codes.shape[1]
    node_count = splits[0].shape[0]
    n_rows = lax.axis_size("rows")
    width = 2 * classes
    own = 8
    group = feats_dev // own
    group_count = n_rows // group
    blocks = tuple((2, (lambda row, r=r: r * own,), 0) for r in range(group))
    info, _, flags, *rows_out = prepare(blocks, splits, logits_t, labels, node_ids, bin_codes)
    members = [[g * group + r for r in range(group)] for g in range(group_count)]
    rows_in = lax.all_to_all(
        jnp.stack(rows_out), "rows", 0, 0, tiled=True, axis_index_groups=members
    )
    hists = []
    for r in range(group):
        held = [hists] if hists else []
        hists = add_rows(
            classes, node_count, own, False, ((0, 0, (0,), (classes,)),), [rows_in[r]], *held
        )
    sums = lax.psum(child_sums(info[:, : half_width(rows_dev)], rows_dev, node_count), ("rows", "feat"))
    side_count = lax.psum(flags, "feat")
    new_logits, leaves = finish(logits_t, node_ids, side_count, sums, node_count)

    cuts = own // pairs_dev
    hist = hists[0][: node_count * width]
    hist = hist.reshape(node_count, width, cuts, pairs_dev, BINS).transpose(0, 2, 3, 4, 1)
    peers = [[g * group + r for g in range(group_count)] for r in range(group)]
    owned = lax.psum_scatter(
        hist.reshape(group_count, pairs_dev, BINS, width),
        "rows",
        scatter_dimension=0,
        axis_index_groups=peers,
    )
    bin_iota = jnp.arange(BINS, dtype=jnp.int32)
    lower_mask = (
        (bin_iota[:, None] < bin_iota[None, :]) & (bin_iota[:, None] < BINS - 1)
    ).astype(jnp.float32)
    left_base = jnp.einsum("pbc,bt->ptc", owned, lower_mask, precision=lax.Precision.HIGHEST)
    node_total = jnp.sum(owned, axis=1, keepdims=True)
    left_miss = left_base + owned[:, BINS - 1 :, :]
    parent_score = split_score(node_total, classes)
    gain_left = (
        split_score(left_miss, classes)
        + split_score(node_total - left_miss, classes)
        - parent_score
    )
    gain_right = (
        split_score(left_base, classes)
        + split_score(node_total - left_base, classes)
        - parent_score
    )
    gain = jnp.concatenate([gain_left, gain_right], axis=1) / (2.0 * classes)
    moves = [
        (n * per_node + cut * group + r, n * per_node + r * cuts + cut)
        for n in range(node_count)
        for cut in range(cuts)
        for r in range(group)
    ]
    gain_rows = lax.ppermute(gain, "rows", moves)
    return (new_logits, gain_rows[None], leaves)


def solution(mesh):
    return jax.shard_map(
        local,
        mesh=mesh,
        in_specs=(P("rows", None), P("rows"), P("rows"), P("rows", "feat"), P(), P(), P()),
        out_specs=(P("rows", None), P("rows", "feat", None), P()),
        check_vma=False,
    )
```

```python
import functools

import jax
import jax.numpy as jnp
from jax import lax
from jax.experimental import pallas as pl
from jax.experimental.pallas import tpu as pltpu
from jax.sharding import PartitionSpec as P

BINS = 64
LANES = 128
VMEM_BYTES = 12 * 1024 * 1024
PREP_VMEM_BYTES = 60 * 1024 * 1024
SMALL_COST = pl.CostEstimate(flops=1000000, bytes_accessed=1000000, transcendentals=0)


reg_lambda = 1.0
step_size = 0.3


def split_score(sums, classes):
    grad_part = sums[..., :classes]
    hess_part = sums[..., classes:]
    return jnp.sum(grad_part * grad_part / (hess_part + reg_lambda), axis=-1)


def three_parts(x):
    first = x.astype(jnp.bfloat16)
    rest = x - first.astype(jnp.float32)
    second = rest.astype(jnp.bfloat16)
    third = (rest - second.astype(jnp.float32)).astype(jnp.bfloat16)
    return first, second, third


def threshold_masks():
    row = lax.broadcasted_iota(jnp.int32, (2 * BINS, 4 * BINS), 0)
    col = lax.broadcasted_iota(jnp.int32, (2 * BINS, 4 * BINS), 1)
    bin_of = row % BINS
    threshold = col % BINS
    first_dir = (col // BINS) % 2 == 0
    below = (bin_of < threshold) & (bin_of < BINS - 1)
    missing = (bin_of == BINS - 1) & first_dir
    same = row // BINS == col // (2 * BINS)
    return jnp.where((below | missing) & same, 1.0, 0.0).astype(jnp.bfloat16)


def half_width(rows):
    return rows // 2 + LANES


def read_info(halves, rows):
    half = rows // 2
    chunks = half // LANES
    prob = jnp.concatenate([info[:, :half] for info in halves], axis=1)
    label, node = (
        jnp.concatenate(
            [info[i : i + 1, half:] for info in halves for i in range(low, low + chunks)], axis=1
        )
        for low in (0, chunks)
    )
    return prob, label, node


def child_sums(info, rows, node_count):
    return info[-node_count:, rows // 2 :]


def prep_kernel(
    own,
    blocks,
    *refs,
):
    operands, rest = refs[:7], refs[7:]
    info_ref, half_ref, flag_ref = rest[:3]
    outs = rest[3 : 3 + len(blocks)]
    turned, *buffers, sems = rest[3 + len(blocks) :]
    copies = [
        pltpu.make_async_copy(operand, buffer, sems.at[i])
        for i, (operand, buffer) in enumerate(zip(operands, buffers))
    ]
    for copy in copies:
        copy.start()
    codes_ref, logits_ref, labels_ref, nodes_ref, feature_ref, bin_ref, missing_ref = buffers
    row_index, feat_index = lax.axis_index("rows"), lax.axis_index("feat")
    classes, rows = logits_ref.shape
    half, width = rows // 2, half_width(rows)
    chunks = half // LANES
    for copy in copies[1:]:
        copy.wait()
    expo_vals = jnp.exp(logits_ref[...])
    prob = expo_vals / jnp.sum(expo_vals, axis=0, keepdims=True)
    for h in range(2):
        info_ref[:, h * width : h * width + half] = prob[:, h * half : (h + 1) * half]
    copies[0].wait()
    turned[...] = codes_ref[...].T
    for (infos, pieces, _), out_ref in zip(blocks, outs):
        if infos == 0 and out_ref.shape[1] > rows:
            out_ref[:, rows:] = jnp.zeros((out_ref.shape[0], out_ref.shape[1] - rows), out_ref.dtype)
        for i, start_of in enumerate(pieces):
            start = pl.multiple_of(start_of(row_index), own)
            if infos == 0:
                out_ref[i * own : (i + 1) * own, :rows] = turned[pl.ds(start, own), :]
                continue
            cut = rows * infos // 2
            for h in range(2 // infos):
                low = classes + (h * len(pieces) + i) * own
                part = turned[pl.ds(start, own), h * cut : (h + 1) * cut]
                out_ref[low : low + own, :cut] = part.astype(out_ref.dtype)
                out_ref[low : low + own, cut:] = jnp.zeros((own, infos * width - cut), out_ref.dtype)
    labels = labels_ref[...].astype(jnp.float32)
    nodes = nodes_ref[...].astype(jnp.float32)
    label = jnp.concatenate([labels[i : i + 1] for i in range(2 * chunks)], axis=1)
    node = jnp.concatenate([nodes[i : i + 1] for i in range(2 * chunks)], axis=1)

    feats = turned.shape[0]
    node_count = feature_ref.shape[0]
    side = jnp.zeros((1, rows), jnp.float32)
    for n in range(node_count):
        col = feature_ref[n] - feat_index * feats
        held = (col >= 0) & (col < feats)
        code = turned[pl.ds(jnp.clip(col, 0, feats - 1), 1), :]
        threshold = jnp.where(held, bin_ref[n], -1)
        missing = jnp.where(held & (missing_ref[n] == 1), BINS - 1, -1)
        left = (code < threshold) | (code == missing)
        value = jnp.where(left, 1.0, jnp.where(held, 2.0, 0.0))
        side = jnp.where(node == float(n), value, side)
    flag_ref[...] = jnp.where(side == 2.0, 1.0, 0.0)
    hot = jnp.concatenate(
        [
            jnp.where((node == float(slot // 2)) & (side == float(slot % 2 + 1)), 1.0, 0.0)
            for slot in range(2 * node_count)
        ],
        axis=0,
    ).astype(jnp.bfloat16)
    sums = lax.dot_general(
        hot,
        gradients(prob, label).astype(jnp.bfloat16),
        (((1,), (1,)), ((), ())),
        preferred_element_type=jnp.float32,
    )
    sums = jnp.concatenate([sums[:node_count], sums[node_count:]], axis=1)
    pad = [jnp.zeros((classes - 2 * chunks - node_count, LANES), jnp.float32)]
    pad = pad if pad[0].shape[0] > 0 else []
    for h in range(2):
        some = slice(h * chunks, (h + 1) * chunks)
        info_ref[:, h * width + half : (h + 1) * width] = jnp.concatenate(
            [labels[some], nodes[some]] + pad + [sums], axis=0
        )
    half_ref[...] = jnp.where(feat_index == 0, info_ref[:, :width], info_ref[:, width:])
    for (infos, _, _), out_ref in zip(blocks, outs):
        if infos > 0:
            out_ref[:classes, :] = half_ref[...] if infos == 1 else info_ref[...]


def gradients(prob, label):
    class_iota = lax.broadcasted_iota(jnp.int32, prob.shape, 0).astype(jnp.float32)
    target = jnp.where(class_iota == label, 1.0, 0.0)
    return jnp.concatenate([prob - target, prob * (1.0 - prob)], axis=0)


def masked_gradients(halves, rows, node_count):
    prob, label, node = read_info(halves, rows)
    grad_hess = gradients(prob, label)
    return jnp.concatenate(
        [jnp.where(node == float(n), grad_hess, 0.0).astype(jnp.bfloat16) for n in range(node_count)],
        axis=0,
    )


def one_hot(codes):
    feats, rows = codes.shape
    bin_iota = lax.broadcasted_iota(jnp.int32, (BINS, rows), 0).astype(codes.dtype)
    return jnp.concatenate(
        [
            jnp.where(codes[f : f + 1, :] == bin_iota, 1.0, 0.0).astype(jnp.bfloat16)
            for f in range(feats)
        ],
        axis=0,
    )


def write_gains(hist_ref, gain_ref, classes, node_count):
    masks = threshold_masks()
    ones = jnp.where(
        lax.broadcasted_iota(jnp.int32, (2 * BINS, 4 * BINS), 0) < BINS, 1.0, 0.0
    ).astype(jnp.bfloat16)

    def times(parts, right):
        return sum(jnp.dot(part, right, preferred_element_type=jnp.float32) for part in parts)

    total = times(three_parts(hist_ref[:, : 2 * BINS]), ones)
    for pair in range(gain_ref.shape[1] // 2):
        span = slice(pair * 2 * BINS, (pair + 1) * 2 * BINS)
        left = times(three_parts(hist_ref[:, span]), masks)
        right = total - left
        for n in range(node_count):
            grads = slice(n * 2 * classes, n * 2 * classes + classes)
            hesss = slice(n * 2 * classes + classes, (n + 1) * 2 * classes)
            score = (
                left[grads] * left[grads] / (left[hesss] + reg_lambda)
                + right[grads] * right[grads] / (right[hesss] + reg_lambda)
            )
            parent = total[grads] * total[grads] / (total[hesss] + reg_lambda)
            gain = (
                jnp.sum(score, axis=0, keepdims=True) - jnp.sum(parent, axis=0, keepdims=True)
            ) / (2.0 * classes)
            gain_ref[n, 2 * pair : 2 * pair + 1, :] = gain[:, : 2 * BINS]
            gain_ref[n, 2 * pair + 1 : 2 * pair + 2, :] = gain[:, 2 * BINS :]


def add_kernel(classes, node_count, own, plan, carry, cuts, *refs):
    outs = len(plan[0][3])
    arrays = 1 + max(max((c,) + tuple(j for j in i if j is not None)) for _, c, i, _ in plan)
    if cuts is None:
        piece_refs, out_refs = None, refs[-outs:]
        held_refs = refs[arrays:-outs]
    else:
        out_refs = refs[-outs:]
        piece_refs = refs[-outs - sum(cuts) : -outs]
        held_refs = refs[arrays : -outs - sum(cuts)]
    pairs = 2 * classes * node_count
    row_index, feat_index = lax.axis_index("rows"), lax.axis_index("feat")
    for s, (m, codes_at, info_at, firsts) in enumerate(plan):
        codes_ref = refs[codes_at]
        line = (row_index >> 2) ^ (m >> 2)
        cut = None
        if len(info_at) == 1:
            width = refs[info_at[0]].shape[1] // 2
            halves = [refs[info_at[0]][:classes, h * width : (h + 1) * width] for h in range(2)]
            sums_from = halves[0]
        elif None in info_at:
            near_only = info_at[1] is None
            info_ref = refs[info_at[0] if near_only else info_at[1]]
            width = info_ref.shape[1]
            halves = [info_ref[:classes, :]]
            sums_from = halves[0] if near_only else None
            which = feat_index if near_only else 1 - feat_index
            cut = pl.ds(pl.multiple_of(which * (width - LANES), LANES), width - LANES)
        else:
            width = refs[info_at[0]].shape[1]
            near, far = (refs[i][:classes, :] for i in info_at)
            halves = [
                jnp.where(feat_index == 0, near, far),
                jnp.where(feat_index == 0, far, near),
            ]
            sums_from = near
        rows = 2 * (width - LANES)
        masked = masked_gradients(halves, rows, node_count)
        sums = None if sums_from is None else child_sums(sums_from, rows, node_count)
        for i, first in enumerate(firsts):
            out_ref = out_refs[i]
            if cut is not None and codes_ref.shape[1] < rows:
                low = first + which * ((codes_ref.shape[0] - classes) // 2)
                codes = codes_ref[pl.ds(pl.multiple_of(low, own), own), : rows // 2]
            elif cut is not None:
                codes = codes_ref[first : first + own, cut]
            elif codes_ref.shape[1] < rows:
                second = first + (codes_ref.shape[0] - classes) // 2
                codes = jnp.concatenate(
                    [codes_ref[low : low + own, : rows // 2] for low in (first, second)], axis=1
                )
            else:
                codes = codes_ref[first : first + own, :rows]
            product = lax.dot_general(
                masked,
                one_hot(codes),
                (((1,), (1,)), ((), ())),
                preferred_element_type=jnp.float32,
            )
            if s == 0:
                if held_refs:
                    out_ref[...] = sum(ref[...] for ref in held_refs[i::outs])
                else:
                    out_ref[...] = jnp.zeros(out_ref.shape, out_ref.dtype)
            out_ref[:pairs, :] += product
            if not carry or sums is None:
                continue
            low_row = pairs + (line >> 1) * node_count
            band = pl.ds(pl.multiple_of(low_row, node_count), node_count)
            for i in range(out_ref.shape[1] // LANES):
                here = jnp.where((row_index & 3) == i, 1.0, 0.0)
                out_ref[band, i * LANES : (i + 1) * LANES] += here * sums
    if cuts is not None:
        for out_ref, cut in zip(out_refs, cuts):
            rows = out_ref.shape[0] // cut
            for i in range(cut):
                piece_refs[i][...] = out_ref[i * rows : (i + 1) * rows, :]
            piece_refs = piece_refs[cut:]


def add_rows(classes, node_count, own, carry, plan, arrays, *held, cuts=None):
    shape = (2 * classes * node_count + 2 * node_count, own * BINS)
    whole = pl.BlockSpec(memory_space=pltpu.VMEM)
    outs = len(plan[0][3])
    heights = [shape[0]] * outs
    if cuts is not None:
        heights = [shape[0] // cut for cut in cuts for _ in range(cut)]
    return pl.pallas_call(
        functools.partial(add_kernel, classes, node_count, own, plan, carry, cuts),
        in_specs=[whole] * (len(arrays) + len(held) * outs),
        out_specs=[whole] * len(heights),
        out_shape=[jax.ShapeDtypeStruct((height, shape[1]), jnp.float32) for height in heights],
        scratch_shapes=[] if cuts is None else [pltpu.VMEM(shape, jnp.float32)] * outs,
        compiler_params=pltpu.CompilerParams(vmem_limit_bytes=VMEM_BYTES),
        cost_estimate=SMALL_COST,
    )(*arrays, *[hist for hists in held for hist in hists])


def gain_kernel(classes, node_count, cuts, *refs):
    gain_ref, hist_ref = refs[-2:]
    pairs = hist_ref.shape[0]
    for i, cut in enumerate(cuts):
        pieces, refs = refs[:cut], refs[cut:]
        rows = pieces[0].shape[0]
        for j, piece in enumerate(pieces):
            low, high = j * rows, min((j + 1) * rows, pairs)
            part = piece[: high - low, :]
            hist_ref[low:high, :] = part if i == 0 else hist_ref[low:high, :] + part
    write_gains(hist_ref, gain_ref, classes, node_count)


def swap(x, axis, bit):
    size = lax.axis_size(axis)
    return lax.ppermute(x, axis, [(i, i ^ bit) for i in range(size)])


def sum_over(x, axis):
    bit = 1
    while bit < lax.axis_size(axis):
        x = x + swap(x, axis, bit)
        bit *= 2
    return x


def prepare(blocks, splits, logits_t, labels, node_ids, bin_codes):
    classes, rows_dev = logits_t.shape
    feats_dev = bin_codes.shape[1]
    own = 8
    whole = pl.BlockSpec(memory_space=pltpu.VMEM)
    width = half_width(rows_dev)
    shapes = [
        jax.ShapeDtypeStruct((classes, 2 * width), jnp.float32),
        jax.ShapeDtypeStruct((classes, width), jnp.float32),
        jax.ShapeDtypeStruct((1, rows_dev), jnp.float32),
    ]
    for infos, pieces, spare in blocks:
        codes = len(pieces) * own
        if infos == 0:
            shapes.append(jax.ShapeDtypeStruct((codes, rows_dev + spare), jnp.int32))
        else:
            shape = (classes + codes * 2 // infos, infos * width)
            shapes.append(jax.ShapeDtypeStruct(shape, jnp.float32))
    operands = (
        bin_codes,
        logits_t,
        labels.reshape(-1, LANES),
        node_ids.reshape(-1, LANES),
        *splits,
    )
    spaces = [pltpu.VMEM] * 4 + [pltpu.SMEM] * 3
    return pl.pallas_call(
        functools.partial(prep_kernel, own, blocks),
        in_specs=[pl.BlockSpec(memory_space=pltpu.HBM)] * len(operands),
        out_specs=[whole] * len(shapes),
        out_shape=shapes,
        scratch_shapes=[pltpu.VMEM((feats_dev, rows_dev), jnp.int32)]
        + [space(x.shape, x.dtype) for space, x in zip(spaces, operands)]
        + [pltpu.SemaphoreType.DMA((len(operands),))],
        compiler_params=pltpu.CompilerParams(vmem_limit_bytes=PREP_VMEM_BYTES),
        cost_estimate=SMALL_COST,
    )(*operands)


def finish(logits_t, node_ids, side_count, sums, node_count):
    classes = logits_t.shape[0]
    width = 2 * classes
    side_sums = jnp.concatenate([sums[:, :width], sums[:, width:]], axis=0)
    side_sums = side_sums.reshape(node_count, 2, width)
    leaves = -side_sums[..., :classes] / (side_sums[..., classes:] + reg_lambda)
    row_side = (side_count > 0.5).astype(jnp.int32)
    slot_iota = jnp.arange(2 * node_count, dtype=jnp.int32)
    slot_hot = (node_ids[None, :] * 2 + row_side) == slot_iota[:, None]
    update = jnp.dot(
        leaves.reshape(2 * node_count, classes).T,
        slot_hot.astype(jnp.float32),
        precision=lax.Precision.HIGHEST,
    )
    return (logits_t + step_size * update).T, leaves


def local(logits, labels, node_ids, bin_codes, split_feature, split_bin, split_missing):
    rows_dev, classes = logits.shape
    feats_dev = bin_codes.shape[1]
    node_count = split_feature.shape[0]
    n_rows = lax.axis_size("rows")
    per_node = n_rows // node_count
    pairs_dev = feats_dev // per_node
    width = 2 * classes
    own = 8
    splits = (split_feature, split_bin, split_missing)
    logits_t = logits.T
    if feats_dev != own * n_rows or n_rows != 16 or lax.axis_size("feat") != 2:
        return by_groups(logits_t, labels, node_ids, bin_codes, splits, per_node, pairs_dev)
    add = functools.partial(add_rows, classes, node_count, own, True)

    def start(taker):
        return (taker & 1) * pairs_dev + (taker >> 1) * own

    def quarters(m, which):
        return tuple(lambda row, low=m ^ 3 ^ q: start(row ^ low) for q in which)

    blocks = (
        (0, quarters(0, (0, 1, 2, 3)), 0),
        (1, quarters(4, (0, 1)), 0),
        (0, quarters(8, (0, 1)), 3 * LANES),
        (0, quarters(12, (0, 1)), 3 * LANES),
        (0, quarters(4, (2, 3)), 0),
        (0, quarters(8, (2, 3)), 0),
        (0, quarters(12, (2, 3)), 0),
    )
    info, half, flags, codes_0, rows_4, codes_8, codes_12, late_4, late_8, late_12 = prepare(
        blocks, splits, logits_t, labels, node_ids, bin_codes
    )

    near_8 = swap(half, "rows", 8)
    rows_4 = swap(rows_4, "rows", 4)
    codes_8 = swap(codes_8, "rows", 8)
    codes_12 = swap(codes_12, "rows", 12)
    hist_a, hist_b, hist_c, hist_d = add(
        ((0, 0, (1,), (0, own, 2 * own, 3 * own)),), [codes_0, info]
    )
    near_8, rows_4, hist_a = lax.optimization_barrier((near_8, rows_4, hist_a))
    near_12 = swap(near_8, "rows", 4)
    far_8 = swap(near_8, "feat", 1)
    far_4 = swap(rows_4[:classes], "feat", 1)
    late_4 = swap(late_4, "rows", 4)
    late_8 = swap(late_8, "rows", 8)
    late_12 = swap(late_12, "rows", 12)
    firsts = (classes, classes + own)
    hists = add(((4, 0, (0, None), firsts),), [rows_4], [hist_a, hist_b])
    hists = add(((4, 0, (None, 1), firsts),), [rows_4, far_4], hists)
    hist_a, hist_b = add(((8, 0, (1, None), (0, own)),), [codes_8, near_8], hists)
    near_12, codes_12, hist_a = lax.optimization_barrier((near_12, codes_12, hist_a))
    far_12 = swap(near_12, "feat", 1)
    hist_a, hist_b = add(((8, 0, (None, 1), (0, own)),), [codes_8, far_8], [hist_a, hist_b])
    hist_a, hist_b = add(((12, 0, (1, None), (0, own)),), [codes_12, near_12], [hist_a, hist_b])
    (to_core,) = add(((12, 0, (None, 1), (0,)),), [codes_12, far_12], [hist_a])
    from_core = swap(to_core, "rows", 1)
    to_plane = add(
        ((12, 0, (None, 1), (own,)),), [codes_12, far_12], [hist_b], [from_core], cuts=(2,)
    )
    from_plane = [swap(piece, "rows", 2) for piece in to_plane]
    _, late_4 = lax.optimization_barrier((to_plane, late_4))
    hists = add(((4, 0, (1, 2), (0, own)),), [late_4, rows_4, far_4], [hist_c, hist_d])
    hists = add(((8, 0, (1, 2), (0, own)),), [late_8, near_8, far_8], hists)
    *to_core, kept = add(
        ((12, 0, (1, 2), (0, own)),), [late_12, near_12, far_12], hists, cuts=(3, 1)
    )
    from_core = [swap(piece, "rows", 1) for piece in to_core]

    pairs = node_count * width
    gains = pl.pallas_call(
        functools.partial(gain_kernel, classes, node_count, (1, len(from_core), len(from_plane))),
        in_specs=[pl.BlockSpec(memory_space=pltpu.VMEM)] * (1 + len(from_core) + len(from_plane)),
        out_specs=pl.BlockSpec(memory_space=pltpu.VMEM),
        out_shape=jax.ShapeDtypeStruct((node_count, own, 2 * BINS), jnp.float32),
        scratch_shapes=[pltpu.VMEM((pairs, own * BINS), jnp.float32)],
        compiler_params=pltpu.CompilerParams(vmem_limit_bytes=VMEM_BYTES),
        cost_estimate=SMALL_COST,
    )(kept, *from_core, *from_plane)
    def gather(parts):
        return jnp.sum(parts.reshape(2, node_count, -1, LANES), axis=(0, 2))

    gains, from_plane = lax.optimization_barrier((gains, from_plane))
    low = -2 * node_count
    sums = gather(from_core[-1][low:] + from_plane[-1][low:] + kept[low:])
    children = jnp.concatenate([sums, flags.reshape(-1, LANES)], axis=0)
    children = sum_over(children, "feat")
    side_count = children[node_count:].reshape(1, rows_dev)
    sums = children[:node_count]
    new_logits, leaves = finish(logits_t, node_ids, side_count, sums, node_count)

    halves = [[h + n * per_node for n in range(node_count)] for h in range(per_node)]
    gain_rows = lax.all_to_all(gains, "rows", 0, 0, tiled=True, axis_index_groups=halves)
    return (new_logits, gain_rows.reshape(1, pairs_dev, 2 * BINS), leaves)


def by_groups(logits_t, labels, node_ids, bin_codes, splits, per_node, pairs_dev):
    classes, rows_dev = logits_t.shape
    feats_dev = bin_codes.shape[1]
    node_count = splits[0].shape[0]
    n_rows = lax.axis_size("rows")
    width = 2 * classes
    own = 8
    group = feats_dev // own
    group_count = n_rows // group
    blocks = tuple((2, (lambda row, r=r: r * own,), 0) for r in range(group))
    info, _, flags, *rows_out = prepare(blocks, splits, logits_t, labels, node_ids, bin_codes)
    members = [[g * group + r for r in range(group)] for g in range(group_count)]
    rows_in = lax.all_to_all(
        jnp.stack(rows_out), "rows", 0, 0, tiled=True, axis_index_groups=members
    )
    hists = []
    for r in range(group):
        held = [hists] if hists else []
        hists = add_rows(
            classes, node_count, own, False, ((0, 0, (0,), (classes,)),), [rows_in[r]], *held
        )
    sums = lax.psum(child_sums(info[:, : half_width(rows_dev)], rows_dev, node_count), ("rows", "feat"))
    side_count = lax.psum(flags, "feat")
    new_logits, leaves = finish(logits_t, node_ids, side_count, sums, node_count)

    cuts = own // pairs_dev
    hist = hists[0][: node_count * width]
    hist = hist.reshape(node_count, width, cuts, pairs_dev, BINS).transpose(0, 2, 3, 4, 1)
    peers = [[g * group + r for g in range(group_count)] for r in range(group)]
    owned = lax.psum_scatter(
        hist.reshape(group_count, pairs_dev, BINS, width),
        "rows",
        scatter_dimension=0,
        axis_index_groups=peers,
    )
    bin_iota = jnp.arange(BINS, dtype=jnp.int32)
    lower_mask = (
        (bin_iota[:, None] < bin_iota[None, :]) & (bin_iota[:, None] < BINS - 1)
    ).astype(jnp.float32)
    left_base = jnp.einsum("pbc,bt->ptc", owned, lower_mask, precision=lax.Precision.HIGHEST)
    node_total = jnp.sum(owned, axis=1, keepdims=True)
    left_miss = left_base + owned[:, BINS - 1 :, :]
    parent_score = split_score(node_total, classes)
    gain_left = (
        split_score(left_miss, classes)
        + split_score(node_total - left_miss, classes)
        - parent_score
    )
    gain_right = (
        split_score(left_base, classes)
        + split_score(node_total - left_base, classes)
        - parent_score
    )
    gain = jnp.concatenate([gain_left, gain_right], axis=1) / (2.0 * classes)
    moves = [
        (n * per_node + cut * group + r, n * per_node + r * cuts + cut)
        for n in range(node_count)
        for cut in range(cuts)
        for r in range(group)
    ]
    gain_rows = lax.ppermute(gain, "rows", moves)
    return (new_logits, gain_rows[None], leaves)


def solution(mesh):
    return jax.shard_map(
        local,
        mesh=mesh,
        in_specs=(P("rows", None), P("rows"), P("rows"), P("rows", "feat"), P(), P(), P()),
        out_specs=(P("rows", None), P("rows", "feat", None), P()),
        check_vma=False,
    )
```

```python
import functools

import jax
import jax.numpy as jnp
from jax import lax
from jax.experimental import pallas as pl
from jax.experimental.pallas import tpu as pltpu
from jax.sharding import PartitionSpec as P

BINS = 64
LANES = 128
VMEM_BYTES = 12 * 1024 * 1024
PREP_VMEM_BYTES = 60 * 1024 * 1024
SMALL_COST = pl.CostEstimate(flops=1000000, bytes_accessed=1000000, transcendentals=0)


reg_lambda = 1.0
step_size = 0.3


def split_score(sums, classes):
    grad_part = sums[..., :classes]
    hess_part = sums[..., classes:]
    return jnp.sum(grad_part * grad_part / (hess_part + reg_lambda), axis=-1)


def three_parts(x):
    first = x.astype(jnp.bfloat16)
    rest = x - first.astype(jnp.float32)
    second = rest.astype(jnp.bfloat16)
    third = (rest - second.astype(jnp.float32)).astype(jnp.bfloat16)
    return first, second, third


def threshold_masks():
    row = lax.broadcasted_iota(jnp.int32, (2 * BINS, 4 * BINS), 0)
    col = lax.broadcasted_iota(jnp.int32, (2 * BINS, 4 * BINS), 1)
    bin_of = row % BINS
    threshold = col % BINS
    first_dir = (col // BINS) % 2 == 0
    below = (bin_of < threshold) & (bin_of < BINS - 1)
    missing = (bin_of == BINS - 1) & first_dir
    same = row // BINS == col // (2 * BINS)
    return jnp.where((below | missing) & same, 1.0, 0.0).astype(jnp.bfloat16)


def half_width(rows):
    return rows // 2 + LANES


def read_info(halves, rows):
    half = rows // 2
    chunks = half // LANES
    prob = jnp.concatenate([info[:, :half] for info in halves], axis=1)
    label, node = (
        jnp.concatenate(
            [info[i : i + 1, half:] for info in halves for i in range(low, low + chunks)], axis=1
        )
        for low in (0, chunks)
    )
    return prob, label, node


def child_sums(info, rows, node_count):
    return info[-node_count:, rows // 2 :]


def prep_kernel(
    own,
    blocks,
    *refs,
):
    operands, rest = refs[:7], refs[7:]
    info_ref, half_ref, flag_ref = rest[:3]
    outs = rest[3 : 3 + len(blocks)]
    turned, *buffers, sems = rest[3 + len(blocks) :]
    copies = [
        pltpu.make_async_copy(operand, buffer, sems.at[i])
        for i, (operand, buffer) in enumerate(zip(operands, buffers))
    ]
    for copy in copies:
        copy.start()
    codes_ref, logits_ref, labels_ref, nodes_ref, feature_ref, bin_ref, missing_ref = buffers
    row_index, feat_index = lax.axis_index("rows"), lax.axis_index("feat")
    classes, rows = logits_ref.shape
    half, width = rows // 2, half_width(rows)
    chunks = half // LANES
    for copy in copies[1:]:
        copy.wait()
    expo_vals = jnp.exp(logits_ref[...])
    prob = expo_vals / jnp.sum(expo_vals, axis=0, keepdims=True)
    for h in range(2):
        info_ref[:, h * width : h * width + half] = prob[:, h * half : (h + 1) * half]
    copies[0].wait()
    turned[...] = codes_ref[...].T
    for (infos, pieces, _), out_ref in zip(blocks, outs):
        if infos == 0 and out_ref.shape[1] > rows:
            out_ref[:, rows:] = jnp.zeros((out_ref.shape[0], out_ref.shape[1] - rows), out_ref.dtype)
        for i, start_of in enumerate(pieces):
            start = pl.multiple_of(start_of(row_index), own)
            if infos == 0:
                out_ref[i * own : (i + 1) * own, :rows] = turned[pl.ds(start, own), :]
                continue
            cut = rows * infos // 2
            for h in range(2 // infos):
                low = classes + (h * len(pieces) + i) * own
                part = turned[pl.ds(start, own), h * cut : (h + 1) * cut]
                out_ref[low : low + own, :cut] = part.astype(out_ref.dtype)
                out_ref[low : low + own, cut:] = jnp.zeros((own, infos * width - cut), out_ref.dtype)
    labels = labels_ref[...].astype(jnp.float32)
    nodes = nodes_ref[...].astype(jnp.float32)
    label = jnp.concatenate([labels[i : i + 1] for i in range(2 * chunks)], axis=1)
    node = jnp.concatenate([nodes[i : i + 1] for i in range(2 * chunks)], axis=1)

    feats = turned.shape[0]
    node_count = feature_ref.shape[0]
    side = jnp.zeros((1, rows), jnp.float32)
    for n in range(node_count):
        col = feature_ref[n] - feat_index * feats
        held = (col >= 0) & (col < feats)
        code = turned[pl.ds(jnp.clip(col, 0, feats - 1), 1), :]
        threshold = jnp.where(held, bin_ref[n], -1)
        missing = jnp.where(held & (missing_ref[n] == 1), BINS - 1, -1)
        left = (code < threshold) | (code == missing)
        value = jnp.where(left, 1.0, jnp.where(held, 2.0, 0.0))
        side = jnp.where(node == float(n), value, side)
    flag_ref[...] = jnp.where(side == 2.0, 1.0, 0.0)
    hot = jnp.concatenate(
        [
            jnp.where((node == float(slot // 2)) & (side == float(slot % 2 + 1)), 1.0, 0.0)
            for slot in range(2 * node_count)
        ],
        axis=0,
    ).astype(jnp.bfloat16)
    sums = lax.dot_general(
        hot,
        gradients(prob, label).astype(jnp.bfloat16),
        (((1,), (1,)), ((), ())),
        preferred_element_type=jnp.float32,
    )
    sums = jnp.concatenate([sums[:node_count], sums[node_count:]], axis=1)
    pad = [jnp.zeros((classes - 2 * chunks - node_count, LANES), jnp.float32)]
    pad = pad if pad[0].shape[0] > 0 else []
    for h in range(2):
        some = slice(h * chunks, (h + 1) * chunks)
        info_ref[:, h * width + half : (h + 1) * width] = jnp.concatenate(
            [labels[some], nodes[some]] + pad + [sums], axis=0
        )
    half_ref[...] = jnp.where(feat_index == 0, info_ref[:, :width], info_ref[:, width:])
    for (infos, _, _), out_ref in zip(blocks, outs):
        if infos > 0:
            out_ref[:classes, :] = half_ref[...] if infos == 1 else info_ref[...]


def gradients(prob, label):
    class_iota = lax.broadcasted_iota(jnp.int32, prob.shape, 0).astype(jnp.float32)
    target = jnp.where(class_iota == label, 1.0, 0.0)
    return jnp.concatenate([prob - target, prob * (1.0 - prob)], axis=0)


def masked_gradients(halves, rows, node_count):
    prob, label, node = read_info(halves, rows)
    grad_hess = gradients(prob, label)
    return jnp.concatenate(
        [jnp.where(node == float(n), grad_hess, 0.0).astype(jnp.bfloat16) for n in range(node_count)],
        axis=0,
    )


def one_hot(codes):
    feats, rows = codes.shape
    bin_iota = lax.broadcasted_iota(jnp.int32, (BINS, rows), 0).astype(codes.dtype)
    return jnp.concatenate(
        [
            jnp.where(codes[f : f + 1, :] == bin_iota, 1.0, 0.0).astype(jnp.bfloat16)
            for f in range(feats)
        ],
        axis=0,
    )


def write_gains(hist_ref, gain_ref, classes, node_count):
    masks = threshold_masks()
    ones = jnp.where(
        lax.broadcasted_iota(jnp.int32, (2 * BINS, 4 * BINS), 0) < BINS, 1.0, 0.0
    ).astype(jnp.bfloat16)

    def times(parts, right):
        return sum(jnp.dot(part, right, preferred_element_type=jnp.float32) for part in parts)

    total = times(three_parts(hist_ref[:, : 2 * BINS]), ones)
    for pair in range(gain_ref.shape[1] // 2):
        span = slice(pair * 2 * BINS, (pair + 1) * 2 * BINS)
        left = times(three_parts(hist_ref[:, span]), masks)
        right = total - left
        for n in range(node_count):
            grads = slice(n * 2 * classes, n * 2 * classes + classes)
            hesss = slice(n * 2 * classes + classes, (n + 1) * 2 * classes)
            score = (
                left[grads] * left[grads] / (left[hesss] + reg_lambda)
                + right[grads] * right[grads] / (right[hesss] + reg_lambda)
            )
            parent = total[grads] * total[grads] / (total[hesss] + reg_lambda)
            gain = (
                jnp.sum(score, axis=0, keepdims=True) - jnp.sum(parent, axis=0, keepdims=True)
            ) / (2.0 * classes)
            gain_ref[n, 2 * pair : 2 * pair + 1, :] = gain[:, : 2 * BINS]
            gain_ref[n, 2 * pair + 1 : 2 * pair + 2, :] = gain[:, 2 * BINS :]


def add_kernel(classes, node_count, own, plan, carry, cuts, *refs):
    outs = len(plan[0][3])
    arrays = 1 + max(max((c,) + tuple(j for j in i if j is not None)) for _, c, i, _ in plan)
    if cuts is None:
        piece_refs, out_refs = None, refs[-outs:]
        held_refs = refs[arrays:-outs]
    else:
        out_refs = refs[-outs:]
        count = sum(len(cut) for cut in cuts)
        piece_refs = refs[-outs - count : -outs]
        held_refs = refs[arrays : -outs - count]
    pairs = 2 * classes * node_count
    row_index, feat_index = lax.axis_index("rows"), lax.axis_index("feat")
    for s, (m, codes_at, info_at, firsts) in enumerate(plan):
        codes_ref = refs[codes_at]
        line = (row_index >> 2) ^ (m >> 2)
        cut = None
        if len(info_at) == 1:
            width = refs[info_at[0]].shape[1] // 2
            halves = [refs[info_at[0]][:classes, h * width : (h + 1) * width] for h in range(2)]
            sums_from = halves[0]
        elif None in info_at:
            near_only = info_at[1] is None
            info_ref = refs[info_at[0] if near_only else info_at[1]]
            width = info_ref.shape[1]
            halves = [info_ref[:classes, :]]
            sums_from = halves[0] if near_only else None
            which = feat_index if near_only else 1 - feat_index
            cut = pl.ds(pl.multiple_of(which * (width - LANES), LANES), width - LANES)
        else:
            width = refs[info_at[0]].shape[1]
            near, far = (refs[i][:classes, :] for i in info_at)
            halves = [
                jnp.where(feat_index == 0, near, far),
                jnp.where(feat_index == 0, far, near),
            ]
            sums_from = near
        rows = 2 * (width - LANES)
        masked = masked_gradients(halves, rows, node_count)
        sums = None if sums_from is None else child_sums(sums_from, rows, node_count)
        for i, first in enumerate(firsts):
            out_ref = out_refs[i]
            if cut is not None and codes_ref.shape[1] < rows:
                low = first + which * ((codes_ref.shape[0] - classes) // 2)
                codes = codes_ref[pl.ds(pl.multiple_of(low, own), own), : rows // 2]
            elif cut is not None:
                codes = codes_ref[first : first + own, cut]
            elif codes_ref.shape[1] < rows:
                second = first + (codes_ref.shape[0] - classes) // 2
                codes = jnp.concatenate(
                    [codes_ref[low : low + own, : rows // 2] for low in (first, second)], axis=1
                )
            else:
                codes = codes_ref[first : first + own, :rows]
            product = lax.dot_general(
                masked,
                one_hot(codes),
                (((1,), (1,)), ((), ())),
                preferred_element_type=jnp.float32,
            )
            if s == 0:
                if held_refs:
                    out_ref[...] = sum(ref[...] for ref in held_refs[i::outs])
                else:
                    out_ref[...] = jnp.zeros(out_ref.shape, out_ref.dtype)
            out_ref[:pairs, :] += product
            if not carry or sums is None:
                continue
            low_row = pairs + (line >> 1) * node_count
            band = pl.ds(pl.multiple_of(low_row, node_count), node_count)
            for i in range(out_ref.shape[1] // LANES):
                here = jnp.where((row_index & 3) == i, 1.0, 0.0)
                out_ref[band, i * LANES : (i + 1) * LANES] += here * sums
    if cuts is not None:
        for out_ref, cut in zip(out_refs, cuts):
            low = 0
            for i, height in enumerate(cut):
                piece_refs[i][...] = out_ref[low : low + height, :]
                low += height
            piece_refs = piece_refs[len(cut) :]


def add_rows(classes, node_count, own, carry, plan, arrays, *held, cuts=None):
    shape = (2 * classes * node_count + 2 * node_count, own * BINS)
    whole = pl.BlockSpec(memory_space=pltpu.VMEM)
    outs = len(plan[0][3])
    heights = [shape[0]] * outs
    if cuts is not None:
        heights = [height for cut in cuts for height in cut]
    return pl.pallas_call(
        functools.partial(add_kernel, classes, node_count, own, plan, carry, cuts),
        in_specs=[whole] * (len(arrays) + len(held) * outs),
        out_specs=[whole] * len(heights),
        out_shape=[jax.ShapeDtypeStruct((height, shape[1]), jnp.float32) for height in heights],
        scratch_shapes=[] if cuts is None else [pltpu.VMEM(shape, jnp.float32)] * outs,
        compiler_params=pltpu.CompilerParams(vmem_limit_bytes=VMEM_BYTES),
        cost_estimate=SMALL_COST,
    )(*arrays, *[hist for hists in held for hist in hists])


def gain_kernel(classes, node_count, cuts, *refs):
    gain_ref, hist_ref = refs[-2:]
    pairs = hist_ref.shape[0]
    for i, cut in enumerate(cuts):
        pieces, refs = refs[:cut], refs[cut:]
        high = 0
        for piece in pieces:
            low, high = high, min(high + piece.shape[0], pairs)
            part = piece[: high - low, :]
            hist_ref[low:high, :] = part if i == 0 else hist_ref[low:high, :] + part
    write_gains(hist_ref, gain_ref, classes, node_count)


def swap(x, axis, bit):
    size = lax.axis_size(axis)
    return lax.ppermute(x, axis, [(i, i ^ bit) for i in range(size)])


def sum_over(x, axis):
    bit = 1
    while bit < lax.axis_size(axis):
        x = x + swap(x, axis, bit)
        bit *= 2
    return x


def prepare(blocks, splits, logits_t, labels, node_ids, bin_codes):
    classes, rows_dev = logits_t.shape
    feats_dev = bin_codes.shape[1]
    own = 8
    whole = pl.BlockSpec(memory_space=pltpu.VMEM)
    width = half_width(rows_dev)
    shapes = [
        jax.ShapeDtypeStruct((classes, 2 * width), jnp.float32),
        jax.ShapeDtypeStruct((classes, width), jnp.float32),
        jax.ShapeDtypeStruct((1, rows_dev), jnp.float32),
    ]
    for infos, pieces, spare in blocks:
        codes = len(pieces) * own
        if infos == 0:
            shapes.append(jax.ShapeDtypeStruct((codes, rows_dev + spare), jnp.int32))
        else:
            shape = (classes + codes * 2 // infos, infos * width)
            shapes.append(jax.ShapeDtypeStruct(shape, jnp.float32))
    operands = (
        bin_codes,
        logits_t,
        labels.reshape(-1, LANES),
        node_ids.reshape(-1, LANES),
        *splits,
    )
    spaces = [pltpu.VMEM] * 4 + [pltpu.SMEM] * 3
    return pl.pallas_call(
        functools.partial(prep_kernel, own, blocks),
        in_specs=[pl.BlockSpec(memory_space=pltpu.HBM)] * len(operands),
        out_specs=[whole] * len(shapes),
        out_shape=shapes,
        scratch_shapes=[pltpu.VMEM((feats_dev, rows_dev), jnp.int32)]
        + [space(x.shape, x.dtype) for space, x in zip(spaces, operands)]
        + [pltpu.SemaphoreType.DMA((len(operands),))],
        compiler_params=pltpu.CompilerParams(vmem_limit_bytes=PREP_VMEM_BYTES),
        cost_estimate=SMALL_COST,
    )(*operands)


def finish(logits_t, node_ids, side_count, sums, node_count):
    classes = logits_t.shape[0]
    width = 2 * classes
    side_sums = jnp.concatenate([sums[:, :width], sums[:, width:]], axis=0)
    side_sums = side_sums.reshape(node_count, 2, width)
    leaves = -side_sums[..., :classes] / (side_sums[..., classes:] + reg_lambda)
    row_side = (side_count > 0.5).astype(jnp.int32)
    slot_iota = jnp.arange(2 * node_count, dtype=jnp.int32)
    slot_hot = (node_ids[None, :] * 2 + row_side) == slot_iota[:, None]
    update = jnp.dot(
        leaves.reshape(2 * node_count, classes).T,
        slot_hot.astype(jnp.float32),
        precision=lax.Precision.HIGHEST,
    )
    return (logits_t + step_size * update).T, leaves


def local(logits, labels, node_ids, bin_codes, split_feature, split_bin, split_missing):
    rows_dev, classes = logits.shape
    feats_dev = bin_codes.shape[1]
    node_count = split_feature.shape[0]
    n_rows = lax.axis_size("rows")
    per_node = n_rows // node_count
    pairs_dev = feats_dev // per_node
    width = 2 * classes
    own = 8
    splits = (split_feature, split_bin, split_missing)
    logits_t = logits.T
    if feats_dev != own * n_rows or n_rows != 16 or lax.axis_size("feat") != 2:
        return by_groups(logits_t, labels, node_ids, bin_codes, splits, per_node, pairs_dev)
    add = functools.partial(add_rows, classes, node_count, own, True)

    def start(taker):
        return (taker & 1) * pairs_dev + (taker >> 1) * own

    def quarters(m, which):
        return tuple(lambda row, low=m ^ 3 ^ q: start(row ^ low) for q in which)

    blocks = (
        (0, quarters(0, (0, 1, 2, 3)), 0),
        (1, quarters(4, (0, 1)), 0),
        (0, quarters(8, (0, 1)), 3 * LANES),
        (0, quarters(12, (0, 1)), 3 * LANES),
        (0, quarters(4, (2, 3)), 0),
        (0, quarters(8, (2, 3)), 1 * LANES),
        (0, quarters(12, (2, 3)), 1 * LANES),
    )
    info, half, flags, codes_0, rows_4, codes_8, codes_12, late_4, late_8, late_12 = prepare(
        blocks, splits, logits_t, labels, node_ids, bin_codes
    )

    near_8 = swap(half, "rows", 8)
    rows_4 = swap(rows_4, "rows", 4)
    codes_8 = swap(codes_8, "rows", 8)
    codes_12 = swap(codes_12, "rows", 12)
    hist_a, hist_b, hist_c, hist_d = add(
        ((0, 0, (1,), (0, own, 2 * own, 3 * own)),), [codes_0, info]
    )
    near_8, rows_4, hist_a = lax.optimization_barrier((near_8, rows_4, hist_a))
    near_12 = swap(near_8, "rows", 4)
    far_8 = swap(near_8, "feat", 1)
    far_4 = swap(rows_4[:classes], "feat", 1)
    late_4 = swap(late_4, "rows", 4)
    late_8 = swap(late_8, "rows", 8)
    late_12 = swap(late_12, "rows", 12)
    firsts = (classes, classes + own)
    hists = add(((4, 0, (0, None), firsts),), [rows_4], [hist_a, hist_b])
    hists = add(((4, 0, (None, 1), firsts),), [rows_4, far_4], hists)
    hist_a, hist_b = add(((8, 0, (1, None), (0, own)),), [codes_8, near_8], hists)
    near_12, codes_12, hist_a = lax.optimization_barrier((near_12, codes_12, hist_a))
    far_12 = swap(near_12, "feat", 1)
    hist_a, hist_b = add(((8, 0, (None, 1), (0, own)),), [codes_8, far_8], [hist_a, hist_b])
    hist_a, hist_b = add(((12, 0, (1, None), (0, own)),), [codes_12, near_12], [hist_a, hist_b])
    (to_core,) = add(((12, 0, (None, 1), (0,)),), [codes_12, far_12], [hist_a])
    from_core = swap(to_core, "rows", 1)
    (to_plane,) = add(((12, 0, (None, 1), (own,)),), [codes_12, far_12], [hist_b], [from_core])
    from_plane = [swap(to_plane, "rows", 2)]
    _, late_4 = lax.optimization_barrier((to_plane, late_4))
    hists = add(((4, 0, (1, 2), (0, own)),), [late_4, rows_4, far_4], [hist_c, hist_d])
    hists = add(((8, 0, (1, 2), (0, own)),), [late_8, near_8, far_8], hists)
    *to_core, kept = add(
        ((12, 0, (1, 2), (0, own)),), [late_12, near_12, far_12], hists, cuts=((176,176,176), (528,))
    )
    from_core = [swap(piece, "rows", 1) for piece in to_core]

    pairs = node_count * width
    gains = pl.pallas_call(
        functools.partial(gain_kernel, classes, node_count, (1, len(from_core), len(from_plane))),
        in_specs=[pl.BlockSpec(memory_space=pltpu.VMEM)] * (1 + len(from_core) + len(from_plane)),
        out_specs=pl.BlockSpec(memory_space=pltpu.VMEM),
        out_shape=jax.ShapeDtypeStruct((node_count, own, 2 * BINS), jnp.float32),
        scratch_shapes=[pltpu.VMEM((pairs, own * BINS), jnp.float32)],
        compiler_params=pltpu.CompilerParams(vmem_limit_bytes=VMEM_BYTES),
        cost_estimate=SMALL_COST,
    )(kept, *from_core, *from_plane)
    def gather(parts):
        return jnp.sum(parts.reshape(2, node_count, -1, LANES), axis=(0, 2))

    gains, from_plane = lax.optimization_barrier((gains, from_plane))
    low = -2 * node_count
    sums = gather(from_core[-1][low:] + from_plane[-1][low:] + kept[low:])
    children = jnp.concatenate([sums, flags.reshape(-1, LANES)], axis=0)
    children = sum_over(children, "feat")
    side_count = children[node_count:].reshape(1, rows_dev)
    sums = children[:node_count]
    new_logits, leaves = finish(logits_t, node_ids, side_count, sums, node_count)

    halves = [[h + n * per_node for n in range(node_count)] for h in range(per_node)]
    gain_rows = lax.all_to_all(gains, "rows", 0, 0, tiled=True, axis_index_groups=halves)
    return (new_logits, gain_rows.reshape(1, pairs_dev, 2 * BINS), leaves)


def by_groups(logits_t, labels, node_ids, bin_codes, splits, per_node, pairs_dev):
    classes, rows_dev = logits_t.shape
    feats_dev = bin_codes.shape[1]
    node_count = splits[0].shape[0]
    n_rows = lax.axis_size("rows")
    width = 2 * classes
    own = 8
    group = feats_dev // own
    group_count = n_rows // group
    blocks = tuple((2, (lambda row, r=r: r * own,), 0) for r in range(group))
    info, _, flags, *rows_out = prepare(blocks, splits, logits_t, labels, node_ids, bin_codes)
    members = [[g * group + r for r in range(group)] for g in range(group_count)]
    rows_in = lax.all_to_all(
        jnp.stack(rows_out), "rows", 0, 0, tiled=True, axis_index_groups=members
    )
    hists = []
    for r in range(group):
        held = [hists] if hists else []
        hists = add_rows(
            classes, node_count, own, False, ((0, 0, (0,), (classes,)),), [rows_in[r]], *held
        )
    sums = lax.psum(child_sums(info[:, : half_width(rows_dev)], rows_dev, node_count), ("rows", "feat"))
    side_count = lax.psum(flags, "feat")
    new_logits, leaves = finish(logits_t, node_ids, side_count, sums, node_count)

    cuts = own // pairs_dev
    hist = hists[0][: node_count * width]
    hist = hist.reshape(node_count, width, cuts, pairs_dev, BINS).transpose(0, 2, 3, 4, 1)
    peers = [[g * group + r for g in range(group_count)] for r in range(group)]
    owned = lax.psum_scatter(
        hist.reshape(group_count, pairs_dev, BINS, width),
        "rows",
        scatter_dimension=0,
        axis_index_groups=peers,
    )
    bin_iota = jnp.arange(BINS, dtype=jnp.int32)
    lower_mask = (
        (bin_iota[:, None] < bin_iota[None, :]) & (bin_iota[:, None] < BINS - 1)
    ).astype(jnp.float32)
    left_base = jnp.einsum("pbc,bt->ptc", owned, lower_mask, precision=lax.Precision.HIGHEST)
    node_total = jnp.sum(owned, axis=1, keepdims=True)
    left_miss = left_base + owned[:, BINS - 1 :, :]
    parent_score = split_score(node_total, classes)
    gain_left = (
        split_score(left_miss, classes)
        + split_score(node_total - left_miss, classes)
        - parent_score
    )
    gain_right = (
        split_score(left_base, classes)
        + split_score(node_total - left_base, classes)
        - parent_score
    )
    gain = jnp.concatenate([gain_left, gain_right], axis=1) / (2.0 * classes)
    moves = [
        (n * per_node + cut * group + r, n * per_node + r * cuts + cut)
        for n in range(node_count)
        for cut in range(cuts)
        for r in range(group)
    ]
    gain_rows = lax.ppermute(gain, "rows", moves)
    return (new_logits, gain_rows[None], leaves)


def solution(mesh):
    return jax.shard_map(
        local,
        mesh=mesh,
        in_specs=(P("rows", None), P("rows"), P("rows"), P("rows", "feat"), P(), P(), P()),
        out_specs=(P("rows", None), P("rows", "feat", None), P()),
        check_vma=False,
    )
```

```python
import functools

import jax
import jax.numpy as jnp
from jax import lax
from jax.experimental import pallas as pl
from jax.experimental.pallas import tpu as pltpu
from jax.sharding import PartitionSpec as P

BINS = 64
LANES = 128
VMEM_BYTES = 12 * 1024 * 1024
PREP_VMEM_BYTES = 60 * 1024 * 1024
SMALL_COST = pl.CostEstimate(flops=1000000, bytes_accessed=1000000, transcendentals=0)


reg_lambda = 1.0
step_size = 0.3


def split_score(sums, classes):
    grad_part = sums[..., :classes]
    hess_part = sums[..., classes:]
    return jnp.sum(grad_part * grad_part / (hess_part + reg_lambda), axis=-1)


def three_parts(x):
    first = x.astype(jnp.bfloat16)
    rest = x - first.astype(jnp.float32)
    second = rest.astype(jnp.bfloat16)
    third = (rest - second.astype(jnp.float32)).astype(jnp.bfloat16)
    return first, second, third


def threshold_masks():
    row = lax.broadcasted_iota(jnp.int32, (2 * BINS, 4 * BINS), 0)
    col = lax.broadcasted_iota(jnp.int32, (2 * BINS, 4 * BINS), 1)
    bin_of = row % BINS
    threshold = col % BINS
    first_dir = (col // BINS) % 2 == 0
    below = (bin_of < threshold) & (bin_of < BINS - 1)
    missing = (bin_of == BINS - 1) & first_dir
    same = row // BINS == col // (2 * BINS)
    return jnp.where((below | missing) & same, 1.0, 0.0).astype(jnp.bfloat16)


def half_width(rows):
    return rows // 2 + LANES


def read_info(halves, rows):
    half = rows // 2
    chunks = half // LANES
    prob = jnp.concatenate([info[:, :half] for info in halves], axis=1)
    label, node = (
        jnp.concatenate(
            [info[i : i + 1, half:] for info in halves for i in range(low, low + chunks)], axis=1
        )
        for low in (0, chunks)
    )
    return prob, label, node


def child_sums(info, rows, node_count):
    return info[-node_count:, rows // 2 :]


def prep_kernel(
    own,
    blocks,
    *refs,
):
    operands, rest = refs[:7], refs[7:]
    info_ref, half_ref, flag_ref = rest[:3]
    outs = rest[3 : 3 + len(blocks)]
    turned, *buffers, sems = rest[3 + len(blocks) :]
    copies = [
        pltpu.make_async_copy(operand, buffer, sems.at[i])
        for i, (operand, buffer) in enumerate(zip(operands, buffers))
    ]
    for copy in copies:
        copy.start()
    codes_ref, logits_ref, labels_ref, nodes_ref, feature_ref, bin_ref, missing_ref = buffers
    row_index, feat_index = lax.axis_index("rows"), lax.axis_index("feat")
    classes, rows = logits_ref.shape
    half, width = rows // 2, half_width(rows)
    chunks = half // LANES
    for copy in copies[1:]:
        copy.wait()
    expo_vals = jnp.exp(logits_ref[...])
    prob = expo_vals / jnp.sum(expo_vals, axis=0, keepdims=True)
    for h in range(2):
        info_ref[:, h * width : h * width + half] = prob[:, h * half : (h + 1) * half]
    copies[0].wait()
    turned[...] = codes_ref[...].T
    for (infos, pieces, _), out_ref in zip(blocks, outs):
        if infos == 0 and out_ref.shape[1] > rows:
            out_ref[:, rows:] = jnp.zeros((out_ref.shape[0], out_ref.shape[1] - rows), out_ref.dtype)
        for i, start_of in enumerate(pieces):
            start = pl.multiple_of(start_of(row_index), own)
            if infos == 0:
                out_ref[i * own : (i + 1) * own, :rows] = turned[pl.ds(start, own), :]
                continue
            cut = rows * infos // 2
            for h in range(2 // infos):
                low = classes + (h * len(pieces) + i) * own
                part = turned[pl.ds(start, own), h * cut : (h + 1) * cut]
                out_ref[low : low + own, :cut] = part.astype(out_ref.dtype)
                out_ref[low : low + own, cut:] = jnp.zeros((own, infos * width - cut), out_ref.dtype)
    labels = labels_ref[...].astype(jnp.float32)
    nodes = nodes_ref[...].astype(jnp.float32)
    label = jnp.concatenate([labels[i : i + 1] for i in range(2 * chunks)], axis=1)
    node = jnp.concatenate([nodes[i : i + 1] for i in range(2 * chunks)], axis=1)

    feats = turned.shape[0]
    node_count = feature_ref.shape[0]
    side = jnp.zeros((1, rows), jnp.float32)
    for n in range(node_count):
        col = feature_ref[n] - feat_index * feats
        held = (col >= 0) & (col < feats)
        code = turned[pl.ds(jnp.clip(col, 0, feats - 1), 1), :]
        threshold = jnp.where(held, bin_ref[n], -1)
        missing = jnp.where(held & (missing_ref[n] == 1), BINS - 1, -1)
        left = (code < threshold) | (code == missing)
        value = jnp.where(left, 1.0, jnp.where(held, 2.0, 0.0))
        side = jnp.where(node == float(n), value, side)
    flag_ref[...] = jnp.where(side == 2.0, 1.0, 0.0)
    hot = jnp.concatenate(
        [
            jnp.where((node == float(slot // 2)) & (side == float(slot % 2 + 1)), 1.0, 0.0)
            for slot in range(2 * node_count)
        ],
        axis=0,
    ).astype(jnp.bfloat16)
    sums = lax.dot_general(
        hot,
        gradients(prob, label).astype(jnp.bfloat16),
        (((1,), (1,)), ((), ())),
        preferred_element_type=jnp.float32,
    )
    sums = jnp.concatenate([sums[:node_count], sums[node_count:]], axis=1)
    pad = [jnp.zeros((classes - 2 * chunks - node_count, LANES), jnp.float32)]
    pad = pad if pad[0].shape[0] > 0 else []
    for h in range(2):
        some = slice(h * chunks, (h + 1) * chunks)
        info_ref[:, h * width + half : (h + 1) * width] = jnp.concatenate(
            [labels[some], nodes[some]] + pad + [sums], axis=0
        )
    half_ref[...] = jnp.where(feat_index == 0, info_ref[:, :width], info_ref[:, width:])
    for (infos, _, _), out_ref in zip(blocks, outs):
        if infos > 0:
            out_ref[:classes, :] = half_ref[...] if infos == 1 else info_ref[...]


def gradients(prob, label):
    class_iota = lax.broadcasted_iota(jnp.int32, prob.shape, 0).astype(jnp.float32)
    target = jnp.where(class_iota == label, 1.0, 0.0)
    return jnp.concatenate([prob - target, prob * (1.0 - prob)], axis=0)


def masked_gradients(halves, rows, node_count):
    prob, label, node = read_info(halves, rows)
    grad_hess = gradients(prob, label)
    return jnp.concatenate(
        [jnp.where(node == float(n), grad_hess, 0.0).astype(jnp.bfloat16) for n in range(node_count)],
        axis=0,
    )


def one_hot(codes):
    feats, rows = codes.shape
    bin_iota = lax.broadcasted_iota(jnp.int32, (BINS, rows), 0).astype(codes.dtype)
    return jnp.concatenate(
        [
            jnp.where(codes[f : f + 1, :] == bin_iota, 1.0, 0.0).astype(jnp.bfloat16)
            for f in range(feats)
        ],
        axis=0,
    )


def write_gains(hist_ref, gain_ref, classes, node_count):
    masks = threshold_masks()
    ones = jnp.where(
        lax.broadcasted_iota(jnp.int32, (2 * BINS, 4 * BINS), 0) < BINS, 1.0, 0.0
    ).astype(jnp.bfloat16)

    def times(parts, right):
        return sum(jnp.dot(part, right, preferred_element_type=jnp.float32) for part in parts)

    total = times(three_parts(hist_ref[:, : 2 * BINS]), ones)
    for pair in range(gain_ref.shape[1] // 2):
        span = slice(pair * 2 * BINS, (pair + 1) * 2 * BINS)
        left = times(three_parts(hist_ref[:, span]), masks)
        right = total - left
        for n in range(node_count):
            grads = slice(n * 2 * classes, n * 2 * classes + classes)
            hesss = slice(n * 2 * classes + classes, (n + 1) * 2 * classes)
            score = (
                left[grads] * left[grads] / (left[hesss] + reg_lambda)
                + right[grads] * right[grads] / (right[hesss] + reg_lambda)
            )
            parent = total[grads] * total[grads] / (total[hesss] + reg_lambda)
            gain = (
                jnp.sum(score, axis=0, keepdims=True) - jnp.sum(parent, axis=0, keepdims=True)
            ) / (2.0 * classes)
            gain_ref[n, 2 * pair : 2 * pair + 1, :] = gain[:, : 2 * BINS]
            gain_ref[n, 2 * pair + 1 : 2 * pair + 2, :] = gain[:, 2 * BINS :]


def add_kernel(classes, node_count, own, plan, carry, *refs):
    outs = len(plan[0][3])
    arrays = 1 + max(max((c,) + tuple(j for j in i if j is not None)) for _, c, i, _ in plan)
    out_refs = refs[-outs:]
    held_refs = refs[arrays:-outs]
    pairs = 2 * classes * node_count
    row_index, feat_index = lax.axis_index("rows"), lax.axis_index("feat")
    for s, (m, codes_at, info_at, firsts) in enumerate(plan):
        codes_ref = refs[codes_at]
        line = (row_index >> 2) ^ (m >> 2)
        cut = None
        if len(info_at) == 1:
            width = refs[info_at[0]].shape[1] // 2
            halves = [refs[info_at[0]][:classes, h * width : (h + 1) * width] for h in range(2)]
            sums_from = halves[0]
        elif None in info_at:
            near_only = info_at[1] is None
            info_ref = refs[info_at[0] if near_only else info_at[1]]
            width = info_ref.shape[1]
            halves = [info_ref[:classes, :]]
            sums_from = halves[0] if near_only else None
            which = feat_index if near_only else 1 - feat_index
            cut = pl.ds(pl.multiple_of(which * (width - LANES), LANES), width - LANES)
        else:
            width = refs[info_at[0]].shape[1]
            near, far = (refs[i][:classes, :] for i in info_at)
            halves = [
                jnp.where(feat_index == 0, near, far),
                jnp.where(feat_index == 0, far, near),
            ]
            sums_from = near
        rows = 2 * (width - LANES)
        masked = masked_gradients(halves, rows, node_count)
        sums = None if sums_from is None else child_sums(sums_from, rows, node_count)
        for i, first in enumerate(firsts):
            out_ref = out_refs[i]
            if cut is not None and codes_ref.shape[1] < rows:
                low = first + which * ((codes_ref.shape[0] - classes) // 2)
                codes = codes_ref[pl.ds(pl.multiple_of(low, own), own), : rows // 2]
            elif cut is not None:
                codes = codes_ref[first : first + own, cut]
            elif codes_ref.shape[1] < rows:
                second = first + (codes_ref.shape[0] - classes) // 2
                codes = jnp.concatenate(
                    [codes_ref[low : low + own, : rows // 2] for low in (first, second)], axis=1
                )
            else:
                codes = codes_ref[first : first + own, :rows]
            product = lax.dot_general(
                masked,
                one_hot(codes),
                (((1,), (1,)), ((), ())),
                preferred_element_type=jnp.float32,
            )
            if s == 0:
                if held_refs:
                    out_ref[...] = sum(ref[...] for ref in held_refs[i::outs])
                else:
                    out_ref[...] = jnp.zeros(out_ref.shape, out_ref.dtype)
            out_ref[:pairs, :] += product
            if not carry or sums is None:
                continue
            low_row = pairs + (line >> 1) * node_count
            band = pl.ds(pl.multiple_of(low_row, node_count), node_count)
            for i in range(out_ref.shape[1] // LANES):
                here = jnp.where((row_index & 3) == i, 1.0, 0.0)
                out_ref[band, i * LANES : (i + 1) * LANES] += here * sums


def add_rows(classes, node_count, own, carry, plan, arrays, *held):
    shape = (2 * classes * node_count + 2 * node_count, own * BINS)
    whole = pl.BlockSpec(memory_space=pltpu.VMEM)
    outs = len(plan[0][3])
    return pl.pallas_call(
        functools.partial(add_kernel, classes, node_count, own, plan, carry),
        in_specs=[whole] * (len(arrays) + len(held) * outs),
        out_specs=[whole] * outs,
        out_shape=[jax.ShapeDtypeStruct(shape, jnp.float32)] * outs,
        compiler_params=pltpu.CompilerParams(vmem_limit_bytes=VMEM_BYTES),
        cost_estimate=SMALL_COST,
    )(*arrays, *[hist for hists in held for hist in hists])


def gain_kernel(classes, node_count, *refs):
    gain_ref, hist_ref = refs[-2:]
    hist_ref[...] = sum(ref[: hist_ref.shape[0], :] for ref in refs[:-2])
    write_gains(hist_ref, gain_ref, classes, node_count)


def swap(x, axis, bit):
    size = lax.axis_size(axis)
    return lax.ppermute(x, axis, [(i, i ^ bit) for i in range(size)])


def sum_over(x, axis):
    bit = 1
    while bit < lax.axis_size(axis):
        x = x + swap(x, axis, bit)
        bit *= 2
    return x


def prepare(blocks, splits, logits_t, labels, node_ids, bin_codes):
    classes, rows_dev = logits_t.shape
    feats_dev = bin_codes.shape[1]
    own = 8
    whole = pl.BlockSpec(memory_space=pltpu.VMEM)
    width = half_width(rows_dev)
    shapes = [
        jax.ShapeDtypeStruct((classes, 2 * width), jnp.float32),
        jax.ShapeDtypeStruct((classes, width), jnp.float32),
        jax.ShapeDtypeStruct((1, rows_dev), jnp.float32),
    ]
    for infos, pieces, spare in blocks:
        codes = len(pieces) * own
        if infos == 0:
            shapes.append(jax.ShapeDtypeStruct((codes, rows_dev + spare), jnp.int32))
        else:
            shape = (classes + codes * 2 // infos, infos * width)
            shapes.append(jax.ShapeDtypeStruct(shape, jnp.float32))
    operands = (
        bin_codes,
        logits_t,
        labels.reshape(-1, LANES),
        node_ids.reshape(-1, LANES),
        *splits,
    )
    spaces = [pltpu.VMEM] * 4 + [pltpu.SMEM] * 3
    return pl.pallas_call(
        functools.partial(prep_kernel, own, blocks),
        in_specs=[pl.BlockSpec(memory_space=pltpu.HBM)] * len(operands),
        out_specs=[whole] * len(shapes),
        out_shape=shapes,
        scratch_shapes=[pltpu.VMEM((feats_dev, rows_dev), jnp.int32)]
        + [space(x.shape, x.dtype) for space, x in zip(spaces, operands)]
        + [pltpu.SemaphoreType.DMA((len(operands),))],
        compiler_params=pltpu.CompilerParams(vmem_limit_bytes=PREP_VMEM_BYTES),
        cost_estimate=SMALL_COST,
    )(*operands)


def finish(logits_t, node_ids, side_count, sums, node_count):
    classes = logits_t.shape[0]
    width = 2 * classes
    side_sums = jnp.concatenate([sums[:, :width], sums[:, width:]], axis=0)
    side_sums = side_sums.reshape(node_count, 2, width)
    leaves = -side_sums[..., :classes] / (side_sums[..., classes:] + reg_lambda)
    row_side = (side_count > 0.5).astype(jnp.int32)
    slot_iota = jnp.arange(2 * node_count, dtype=jnp.int32)
    slot_hot = (node_ids[None, :] * 2 + row_side) == slot_iota[:, None]
    update = jnp.dot(
        leaves.reshape(2 * node_count, classes).T,
        slot_hot.astype(jnp.float32),
        precision=lax.Precision.HIGHEST,
    )
    return (logits_t + step_size * update).T, leaves


def local(logits, labels, node_ids, bin_codes, split_feature, split_bin, split_missing):
    rows_dev, classes = logits.shape
    feats_dev = bin_codes.shape[1]
    node_count = split_feature.shape[0]
    n_rows = lax.axis_size("rows")
    per_node = n_rows // node_count
    pairs_dev = feats_dev // per_node
    width = 2 * classes
    own = 8
    splits = (split_feature, split_bin, split_missing)
    logits_t = logits.T
    if feats_dev != own * n_rows or n_rows != 16 or lax.axis_size("feat") != 2:
        return by_groups(logits_t, labels, node_ids, bin_codes, splits, per_node, pairs_dev)
    add = functools.partial(add_rows, classes, node_count, own, True)

    def start(taker):
        return (taker & 1) * pairs_dev + (taker >> 1) * own

    def quarters(m, which):
        return tuple(lambda row, low=m ^ 3 ^ q: start(row ^ low) for q in which)

    blocks = (
        (0, quarters(0, (0, 1, 2, 3)), 0),
        (1, quarters(4, (0, 1, 2, 3)), 0),
        (0, quarters(8, (0, 1)), 3 * LANES),
        (0, quarters(12, (0, 1)), 3 * LANES),
        (0, quarters(8, (2, 3)), 0),
        (0, quarters(12, (2, 3)), 0),
    )
    info, half, flags, codes_0, rows_4, codes_8, codes_12, late_8, late_12 = prepare(
        blocks, splits, logits_t, labels, node_ids, bin_codes
    )

    near_8 = swap(half, "rows", 8)
    rows_4 = swap(rows_4, "rows", 4)
    codes_8 = swap(codes_8, "rows", 8)
    codes_12 = swap(codes_12, "rows", 12)
    hist_a, hist_b, hist_c, hist_d = add(
        ((0, 0, (1,), (0, own, 2 * own, 3 * own)),), [codes_0, info]
    )
    near_8, rows_4, hist_a = lax.optimization_barrier((near_8, rows_4, hist_a))
    near_12 = swap(near_8, "rows", 4)
    far_8 = swap(near_8, "feat", 1)
    far_4 = swap(rows_4[:classes], "feat", 1)
    late_8 = swap(late_8, "rows", 8)
    late_12 = swap(late_12, "rows", 12)
    firsts = (classes, classes + own)
    hists = add(((4, 0, (0, None), firsts),), [rows_4], [hist_a, hist_b])
    hists = add(((4, 0, (None, 1), firsts),), [rows_4, far_4], hists)
    hist_a, hist_b = add(((8, 0, (1, None), (0, own)),), [codes_8, near_8], hists)
    near_12, codes_12, hist_a = lax.optimization_barrier((near_12, codes_12, hist_a))
    far_12 = swap(near_12, "feat", 1)
    hist_a, hist_b = add(((8, 0, (None, 1), (0, own)),), [codes_8, far_8], [hist_a, hist_b])
    hist_a, hist_b = add(((12, 0, (1, None), (0, own)),), [codes_12, near_12], [hist_a, hist_b])
    (to_core,) = add(((12, 0, (None, 1), (0,)),), [codes_12, far_12], [hist_a])
    from_core = swap(to_core, "rows", 1)
    (to_plane,) = add(((12, 0, (None, 1), (own,)),), [codes_12, far_12], [hist_b], [from_core])
    from_plane = swap(to_plane, "rows", 2)
    _, hist_c = lax.optimization_barrier((to_plane, hist_c))
    lasts = (classes + 2 * own, classes + 3 * own)
    hists = add(((4, 0, (0, 1), lasts),), [rows_4, far_4], [hist_c, hist_d])
    hists = add(((8, 0, (1, 2), (0, own)),), [late_8, near_8, far_8], hists)
    to_core, kept = add(((12, 0, (1, 2), (0, own)),), [late_12, near_12, far_12], hists)
    middle = to_core.shape[0] // 2
    from_core = [swap(part, "rows", 1) for part in (to_core[:middle], to_core[middle:])]
    from_core = jnp.concatenate(from_core, axis=0)

    pairs = node_count * width
    gains = pl.pallas_call(
        functools.partial(gain_kernel, classes, node_count),
        in_specs=[pl.BlockSpec(memory_space=pltpu.VMEM)] * 3,
        out_specs=pl.BlockSpec(memory_space=pltpu.VMEM),
        out_shape=jax.ShapeDtypeStruct((node_count, own, 2 * BINS), jnp.float32),
        scratch_shapes=[pltpu.VMEM((pairs, own * BINS), jnp.float32)],
        compiler_params=pltpu.CompilerParams(vmem_limit_bytes=VMEM_BYTES),
        cost_estimate=SMALL_COST,
    )(from_core, from_plane, kept)
    def gather(parts):
        return jnp.sum(parts.reshape(2, node_count, -1, LANES), axis=(0, 2))

    gains, from_plane = lax.optimization_barrier((gains, from_plane))
    sums = gather(from_core[pairs:] + from_plane[pairs:] + kept[pairs:])
    children = jnp.concatenate([sums, flags.reshape(-1, LANES)], axis=0)
    children = sum_over(children, "feat")
    side_count = children[node_count:].reshape(1, rows_dev)
    sums = children[:node_count]
    new_logits, leaves = finish(logits_t, node_ids, side_count, sums, node_count)

    halves = [[h + n * per_node for n in range(node_count)] for h in range(per_node)]
    gain_rows = lax.all_to_all(gains, "rows", 0, 0, tiled=True, axis_index_groups=halves)
    return (new_logits, gain_rows.reshape(1, pairs_dev, 2 * BINS), leaves)


def by_groups(logits_t, labels, node_ids, bin_codes, splits, per_node, pairs_dev):
    classes, rows_dev = logits_t.shape
    feats_dev = bin_codes.shape[1]
    node_count = splits[0].shape[0]
    n_rows = lax.axis_size("rows")
    width = 2 * classes
    own = 8
    group = feats_dev // own
    group_count = n_rows // group
    blocks = tuple((2, (lambda row, r=r: r * own,), 0) for r in range(group))
    info, _, flags, *rows_out = prepare(blocks, splits, logits_t, labels, node_ids, bin_codes)
    members = [[g * group + r for r in range(group)] for g in range(group_count)]
    rows_in = lax.all_to_all(
        jnp.stack(rows_out), "rows", 0, 0, tiled=True, axis_index_groups=members
    )
    hists = []
    for r in range(group):
        held = [hists] if hists else []
        hists = add_rows(
            classes, node_count, own, False, ((0, 0, (0,), (classes,)),), [rows_in[r]], *held
        )
    sums = lax.psum(child_sums(info[:, : half_width(rows_dev)], rows_dev, node_count), ("rows", "feat"))
    side_count = lax.psum(flags, "feat")
    new_logits, leaves = finish(logits_t, node_ids, side_count, sums, node_count)

    cuts = own // pairs_dev
    hist = hists[0][: node_count * width]
    hist = hist.reshape(node_count, width, cuts, pairs_dev, BINS).transpose(0, 2, 3, 4, 1)
    peers = [[g * group + r for g in range(group_count)] for r in range(group)]
    owned = lax.psum_scatter(
        hist.reshape(group_count, pairs_dev, BINS, width),
        "rows",
        scatter_dimension=0,
        axis_index_groups=peers,
    )
    bin_iota = jnp.arange(BINS, dtype=jnp.int32)
    lower_mask = (
        (bin_iota[:, None] < bin_iota[None, :]) & (bin_iota[:, None] < BINS - 1)
    ).astype(jnp.float32)
    left_base = jnp.einsum("pbc,bt->ptc", owned, lower_mask, precision=lax.Precision.HIGHEST)
    node_total = jnp.sum(owned, axis=1, keepdims=True)
    left_miss = left_base + owned[:, BINS - 1 :, :]
    parent_score = split_score(node_total, classes)
    gain_left = (
        split_score(left_miss, classes)
        + split_score(node_total - left_miss, classes)
        - parent_score
    )
    gain_right = (
        split_score(left_base, classes)
        + split_score(node_total - left_base, classes)
        - parent_score
    )
    gain = jnp.concatenate([gain_left, gain_right], axis=1) / (2.0 * classes)
    moves = [
        (n * per_node + cut * group + r, n * per_node + r * cuts + cut)
        for n in range(node_count)
        for cut in range(cuts)
        for r in range(group)
    ]
    gain_rows = lax.ppermute(gain, "rows", moves)
    return (new_logits, gain_rows[None], leaves)


def solution(mesh):
    return jax.shard_map(
        local,
        mesh=mesh,
        in_specs=(P("rows", None), P("rows"), P("rows"), P("rows", "feat"), P(), P(), P()),
        out_specs=(P("rows", None), P("rows", "feat", None), P()),
        check_vma=False,
    )
```
